32 devices in a mesh: fsdp: 8 (over z, x), layer: 4 (over y, core).
Axes of the slice: x: 2, y: 2, z: 4, core: 2. Of those that a mesh axis runs over, the one named last changes fastest.
Arguments:
- gradients: bfloat16 [4, 64, 256, 256], P('layer', 'fsdp'), may hold values from -8 to 8
- second_moment: float32 [4, 64, 256, 256], P('layer', 'fsdp'), may hold values from 0.0001 to 0.01
- owners: int32 [4, 64, 1], P('layer'), may hold values from 0 to 7, as said below
- left_stats: float32 [4, 64, 256, 256], P('layer', 'fsdp'), may hold values from -0.3 to 4.3, as said below
- right_stats: float32 [4, 64, 256, 256], P('layer', 'fsdp'), may hold values from -0.3 to 4.3, as said below
- left_root: bfloat16 [4, 64, 256, 256], P('layer', 'fsdp'), may hold values from -0.3 to 1.8
- right_root: bfloat16 [4, 64, 256, 256], P('layer', 'fsdp'), may hold values from -0.3 to 1.8
Outputs:
- update: bfloat16 [4, 64, 256, 256], P('layer', 'fsdp')
- new_left_stats: float32 [4, 64, 256, 256], P('layer', 'fsdp')
- new_right_stats: float32 [4, 64, 256, 256], P('layer', 'fsdp')
The draws below stay inside these ranges and needn't reach their ends.
Inputs may be any that keep to these rules, and one draw needn't show every extreme that they name: In the list of one matrix, the 8 blocks of one index of fsdp (blocks i * 8 to (i + 1) * 8 - 1) name distinct owners, and no owner is named more than 8 times; every owner keeps the statistics and roots of its k-th owned block (in list order) in its slot k, and slots past its count are unused. `left_stats`: Symmetric. `right_stats`: Symmetric.
All inputs are finite; a program needn't handle non-finite values.
Results may differ from the reference program's by a relative error of at most 0.0057.
Values may be sent and summed in bfloat16 or wider, within the bound.
No kernel may reach another device: no remote copies, remote signals or barrier semaphores. Data moves between devices by JAX's collectives and lax.ppermute only.
A program may use at most 192 MiB of HBM per device.

```python
import math
import jax
import jax.numpy as jnp
from jax import lax

BS = 256
BLK_DEV = 8
CAP = 8
NB = 64
SLOTS = 64
MATS = 4
N_FSDP = 8


def symmetric_part(key, spread):
    raw_part = jax.random.uniform(key, (MATS, SLOTS, BS, BS), jnp.float32, -1.0, 1.0) * (spread / math.sqrt(BS))
    return (raw_part + jnp.swapaxes(raw_part, 2, 3)) * 0.5


def draw_gradients(key, part):
    key = jax.random.fold_in(key, 11)
    key_noise, key_rows, key_cols = jax.random.split(key, 3)
    block_pos = jnp.arange(NB, dtype=jnp.float32) / float(NB - 1)
    matrix_pos = jnp.arange(MATS, dtype=jnp.float32) / float(max(MATS - 1, 1))
    ramp_sq = (1.0 + 2.0 * block_pos)[None, :] * (1.0 + 2.0 * matrix_pos)[:, None]
    noise_draw = jnp.clip(jax.random.normal(key_noise, (MATS, NB, BS, BS), jnp.float32), -4.0, 4.0)
    row_scale = jnp.exp(jax.random.uniform(key_rows, (MATS, NB, BS, 1), jnp.float32) * math.log(10.0))
    col_scale = jnp.exp(jax.random.uniform(key_cols, (MATS, NB, 1, BS), jnp.float32) * math.log(10.0))
    values = 0.005 * jnp.sqrt(ramp_sq)[:, :, None, None] * row_scale * col_scale * noise_draw
    return values.astype(jnp.bfloat16)


def owner_list_one(key):
    key_perm, key_tilt = jax.random.split(key)
    order = jax.random.permutation(key_perm, N_FSDP).astype(jnp.int32)
    spare = CAP - BLK_DEV
    tilt = jax.random.randint(key_tilt, (N_FSDP // 2,), 0, spare + 1).astype(jnp.int32)
    tilt = tilt.at[0].set(spare)
    pair_counts = jnp.stack([BLK_DEV + tilt, BLK_DEV - tilt], axis=1).reshape(N_FSDP)
    listed = jnp.repeat(order, pair_counts, total_repeat_length=NB)
    return listed.reshape(BLK_DEV, N_FSDP).T.reshape(NB).astype(jnp.int32)


def draw_owners(key, part):
    key = jax.random.fold_in(key, 31)
    rows = [owner_list_one(jax.random.fold_in(key, matrix_index)) for matrix_index in range(MATS)]
    return jnp.stack(rows)[:, :, None].astype(jnp.int32)


def stats_matrix(key):
    key_diag, key_off = jax.random.split(key)
    diagonal = jnp.exp(jax.random.uniform(key_diag, (MATS, SLOTS, BS), jnp.float32) * math.log(4.0))
    return symmetric_part(key_off, 1.2) + diagonal[:, :, :, None] * jnp.eye(BS, dtype=jnp.float32)


def root_matrix(key):
    key_diag, key_off = jax.random.split(key)
    diagonal = 0.5 * jnp.exp(jax.random.uniform(key_diag, (MATS, SLOTS, BS), jnp.float32) * math.log(3.0))
    return (symmetric_part(key_off, 1.2) + diagonal[:, :, :, None] * jnp.eye(BS, dtype=jnp.float32)).astype(jnp.bfloat16)


def draw_left_stats(key, part):
    key = jax.random.fold_in(key, 21)
    return stats_matrix(key)


def draw_right_stats(key, part):
    key = jax.random.fold_in(key, 22)
    return stats_matrix(key)


def draw_left_root(key, part):
    key = jax.random.fold_in(key, 23)
    return root_matrix(key)


def draw_right_root(key, part):
    key = jax.random.fold_in(key, 24)
    return root_matrix(key)


def shard_levels(rng, shape, shards, least, top_value):
    level, own = 1.0, jax.random.fold_in(rng, 6)
    for dim, blocks in shards:
        heights = jnp.exp(jax.random.uniform(jax.random.fold_in(own, dim), (blocks,), jnp.float32, least / len(shards), top_value / len(shards)))
        level = level * jnp.repeat(heights, shape[dim] // blocks).reshape([-1 if axis == dim else 1 for axis in range(len(shape))])
    return level


def setup_inputs(seed: int = 0) -> dict:
    keys = jax.random.split(jax.random.key(seed), 8)
    gradients = draw_gradients(jax.random.fold_in(keys[7], 71), 0)
    second_moment = jnp.clip(jnp.exp(math.log(0.01) - 4.6051702 * jax.random.uniform(keys[1], (MATS, NB, BS, BS), jnp.float32) ** shard_levels(keys[1], (MATS, NB, BS, BS), ((0, 4), (1, 8)), -0.2, 0.2)), 0.0001, 0.01)
    owners = draw_owners(jax.random.fold_in(keys[7], 71), 0)
    left_stats = draw_left_stats(jax.random.fold_in(keys[7], 71), 0)
    right_stats = draw_right_stats(jax.random.fold_in(keys[7], 71), 0)
    left_root = draw_left_root(jax.random.fold_in(keys[7], 71), 0)
    right_root = draw_right_root(jax.random.fold_in(keys[7], 71), 0)
    return dict(gradients=gradients, second_moment=second_moment, owners=owners, left_stats=left_stats, right_stats=right_stats, left_root=left_root, right_root=right_root)


ADAM_EPS = 1e-08
DECAY_RATE = 0.95
UPDATE_RMS = 1.0
NORM_FLOOR = 1e-06

def reference(gradients, second_moment, owners, left_stats, right_stats, left_root, right_root):
    adam_dir = gradients.astype(jnp.float32) / (jnp.sqrt(second_moment) + ADAM_EPS)
    block_sq = lax.optimization_barrier(jnp.sum(adam_dir * adam_dir, axis=(2, 3)))
    global_sq = jnp.sum(block_sq)
    clip_factor = jnp.minimum(1.0, UPDATE_RMS / jnp.sqrt(global_sq / float(MATS * NB * BS * BS)))
    updates = []
    lefts = []
    rights = []
    for matrix_index in range(MATS):
        owner_list = owners[matrix_index, :, 0].astype(jnp.int32)
        owner_hot = (owner_list[:, None] == jnp.arange(N_FSDP, dtype=jnp.int32)[None, :]).astype(jnp.int32)
        earlier = jnp.cumsum(owner_hot, axis=0) - owner_hot
        slot_number = lax.optimization_barrier(jnp.sum(earlier * owner_hot, axis=1)).astype(jnp.int32)
        slot_index = (owner_list * CAP + slot_number).astype(jnp.int32)
        grad_block = gradients[matrix_index].astype(jnp.float32)
        gram_left = jnp.einsum('bij,bkj->bik', grad_block, grad_block)
        gram_right = jnp.einsum('bji,bjk->bik', grad_block, grad_block)
        decayed_left = DECAY_RATE * left_stats[matrix_index]
        decayed_right = DECAY_RATE * right_stats[matrix_index]
        lefts.append(decayed_left.at[slot_index].add((1.0 - DECAY_RATE) * gram_left))
        rights.append(decayed_right.at[slot_index].add((1.0 - DECAY_RATE) * gram_right))
        left_sel = jnp.take(left_root[matrix_index], slot_index, axis=0).astype(jnp.float32)
        right_sel = jnp.take(right_root[matrix_index], slot_index, axis=0).astype(jnp.float32)
        half_done = jnp.einsum('bij,bjk->bik', left_sel, grad_block).astype(jnp.bfloat16)
        preconditioned = jnp.einsum('bij,bjk->bik', half_done.astype(jnp.float32), right_sel).astype(jnp.bfloat16)
        pre_float = preconditioned.astype(jnp.float32)
        graft_ratio = jnp.sqrt(block_sq[matrix_index] / float(BS * BS)) / jnp.sqrt(lax.optimization_barrier(jnp.sum(pre_float * pre_float, axis=(1, 2))) / float(BS * BS) + NORM_FLOOR)
        updates.append((pre_float * (graft_ratio * clip_factor)[:, None, None]).astype(jnp.bfloat16))
    return (jnp.stack(updates), jnp.stack(lefts), jnp.stack(rights))
```

```python
import functools

import jax
import jax.numpy as jnp
from jax import lax
from jax.experimental import pallas as pl
from jax.experimental.pallas import tpu as pltpu
from jax.sharding import PartitionSpec as P

ADAM_EPS = 1e-08
DECAY_RATE = 0.95
UPDATE_RMS = 1.0
NORM_FLOOR = 1e-06


def selection_tables(owner_list, owner_count, blocks, slots_here, my_index):
    total_blocks = owner_list.shape[0]
    owner_hot = (owner_list[:, None] == lax.iota(jnp.int32, owner_count)[None, :]).astype(
        jnp.float32
    )
    row_ids = lax.iota(jnp.int32, total_blocks)
    strict_lower = (row_ids[:, None] > row_ids[None, :]).astype(jnp.float32)
    before_all = jnp.dot(strict_lower, owner_hot, precision=lax.Precision.HIGHEST)
    slot_number = jnp.sum(before_all * owner_hot, axis=1)
    mine_mask = (owner_list == my_index).astype(jnp.float32)
    slot_hot = (slot_number[:, None] == lax.iota(jnp.float32, slots_here)[None, :]).astype(
        jnp.float32
    ) * mine_mask[:, None]
    home_hot = ((row_ids // blocks)[:, None] == lax.iota(jnp.int32, owner_count)[None, :]).astype(
        jnp.float32
    )
    return (owner_hot, home_hot, slot_hot)


def owner_work(gathered, left_stats, right_stats, left_root, right_root):
    gram_left = jnp.einsum("sij,skj->sik", gathered, gathered, preferred_element_type=jnp.float32)
    gram_right = jnp.einsum("sji,sjk->sik", gathered, gathered, preferred_element_type=jnp.float32)
    new_left = DECAY_RATE * left_stats[0] + (1.0 - DECAY_RATE) * gram_left
    new_right = DECAY_RATE * right_stats[0] + (1.0 - DECAY_RATE) * gram_right
    half_done = jnp.einsum(
        "sij,sjk->sik", left_root[0], gathered, preferred_element_type=jnp.float32
    ).astype(jnp.bfloat16)
    preconditioned = jnp.einsum(
        "sij,sjk->sik", half_done, right_root[0], preferred_element_type=jnp.float32
    ).astype(jnp.bfloat16)
    return (preconditioned, new_left[None], new_right[None])


def per_device_general(gradients, second_moment, owners, left_stats, right_stats, left_root, right_root):
    owner_count = lax.axis_size("fsdp")
    my_index = lax.axis_index("fsdp")
    blocks = gradients.shape[1]
    block_side = gradients.shape[3]
    slots_here = left_stats.shape[1]
    grad_local = gradients[0]
    owner_list = owners[0, :, 0]
    total_blocks = owner_list.shape[0]
    adam_dir = grad_local.astype(jnp.float32) / (jnp.sqrt(second_moment[0]) + ADAM_EPS)
    block_sq = jnp.sum(adam_dir * adam_dir, axis=(1, 2))
    global_sq = lax.psum(jnp.sum(block_sq), ("fsdp", "layer"))
    entry_count = float(total_blocks * lax.axis_size("layer") * block_side * block_side)
    clip_factor = jnp.minimum(1.0, UPDATE_RMS / jnp.sqrt(global_sq / entry_count))
    owner_hot, home_hot, slot_hot = selection_tables(
        owner_list, owner_count, blocks, slots_here, my_index
    )
    first_row = my_index * blocks
    my_owner_hot = lax.dynamic_slice_in_dim(owner_hot, first_row, blocks, 0).astype(jnp.bfloat16)
    outgoing = jnp.einsum(
        "jo,jxy->oxy", my_owner_hot, grad_local, preferred_element_type=jnp.float32
    ).astype(jnp.bfloat16)
    received = lax.all_to_all(outgoing, "fsdp", split_axis=0, concat_axis=0, tiled=True)
    pick_table = jnp.einsum("bs,bh->sh", slot_hot, home_hot).astype(jnp.bfloat16)
    gathered = jnp.einsum(
        "sh,hxy->sxy", pick_table, received, preferred_element_type=jnp.float32
    ).astype(jnp.bfloat16)
    preconditioned, new_left, new_right = owner_work(
        gathered, left_stats, right_stats, left_root, right_root
    )
    answers = jnp.einsum(
        "sh,sxy->hxy", pick_table, preconditioned, preferred_element_type=jnp.float32
    ).astype(jnp.bfloat16)
    returned = lax.all_to_all(answers, "fsdp", split_axis=0, concat_axis=0, tiled=True)
    home_blocks = jnp.einsum(
        "jo,oxy->jxy", my_owner_hot, returned, preferred_element_type=jnp.float32
    )
    pre_float = home_blocks.astype(jnp.bfloat16).astype(jnp.float32)
    graft_ratio = jnp.sqrt(block_sq / float(block_side * block_side)) / jnp.sqrt(
        jnp.sum(pre_float * pre_float, axis=(1, 2)) / float(block_side * block_side) + NORM_FLOOR
    )
    update = (pre_float * (graft_ratio * clip_factor)[:, None, None]).astype(jnp.bfloat16)
    return (update[None], new_left, new_right)


TAIL = 16


def kernel_params(mebibytes):
    return pltpu.CompilerParams(vmem_limit_bytes=mebibytes * 2**20)


def home_slot(named, target):
    block = jnp.int32(0)
    for j in range(1, len(named)):
        block = jnp.where(named[j] == target, jnp.int32(j), block)
    return block


def route_kernel(order, owners_hbm, me_ref, grad_hbm, *refs):
    outs, (owners_ref, held, owner_sem, grad_sem) = refs[:-4], refs[-4:]
    count = held.shape[0]
    me = me_ref[0]
    fetch_owners = pltpu.make_async_copy(owners_hbm, owners_ref, owner_sem)
    fetch_grads = pltpu.make_async_copy(grad_hbm.at[0], held, grad_sem)
    fetch_owners.start()
    fetch_grads.start()
    fetch_owners.wait()
    named = [owners_ref[me * count + j] for j in range(count)]
    blocks = [home_slot(named, me ^ m) for m in order]
    fetch_grads.wait()
    for block, out in zip(blocks, outs):
        out[...] = held[block]


def route(order, owner_list, me, gradients):
    count, side = gradients.shape[1], gradients.shape[3]
    hbm = pl.BlockSpec(memory_space=pltpu.HBM)
    piece = jax.ShapeDtypeStruct((side, side), gradients.dtype)
    return pl.pallas_call(
        functools.partial(route_kernel, order),
        in_specs=[hbm, pl.BlockSpec(memory_space=pltpu.SMEM), hbm],
        out_specs=[pl.BlockSpec(memory_space=pltpu.VMEM)] * count,
        scratch_shapes=[
            pltpu.SMEM(owner_list.shape, jnp.int32),
            pltpu.VMEM((count, side, side), gradients.dtype),
            pltpu.SemaphoreType.DMA,
            pltpu.SemaphoreType.DMA,
        ],
        out_shape=[piece] * count,
        compiler_params=kernel_params(6),
        cost_estimate=pl.CostEstimate(
            flops=0, bytes_accessed=4 * count * side * side, transcendentals=0
        ),
    )(
        pltpu.with_memory_space_constraint(owner_list, pltpu.HBM),
        me,
        pltpu.with_memory_space_constraint(gradients, pltpu.HBM),
    )


def adam_kernel(grad_hbm, moment_hbm, out_ref, total_ref, grads, moments, sems):
    count, side = grads.shape[0], grads.shape[2]
    lanes = out_ref.shape[1]
    copies = []
    for b in range(count):
        pair = (
            pltpu.make_async_copy(grad_hbm.at[0, b], grads.at[b], sems.at[0, b]),
            pltpu.make_async_copy(moment_hbm.at[0, b], moments.at[b], sems.at[1, b]),
        )
        for copy in pair:
            copy.start()
        copies.append(pair)
    total = jnp.zeros((1, lanes), jnp.float32)
    for b, pair in enumerate(copies):
        for copy in pair:
            copy.wait()
        adam_dir = grads[b].astype(jnp.float32) / (jnp.sqrt(moments[b]) + ADAM_EPS)
        squares = jnp.sum(adam_dir * adam_dir, axis=0, keepdims=True)
        row = squares[:, 0:lanes]
        for k in range(lanes, side, lanes):
            row = row + squares[:, k : k + lanes]
        out_ref[b : b + 1, :] = row
        total = total + row
    total_ref[...] = jnp.broadcast_to(total, total_ref.shape)


def adam_squares(gradients, second_moment):
    count, side = gradients.shape[1], gradients.shape[3]
    hbm = pl.BlockSpec(memory_space=pltpu.HBM)
    return pl.pallas_call(
        adam_kernel,
        in_specs=[hbm, hbm],
        out_specs=[pl.BlockSpec(memory_space=pltpu.VMEM)] * 2,
        out_shape=[
            jax.ShapeDtypeStruct((count, 128), jnp.float32),
            jax.ShapeDtypeStruct((8, 128), jnp.float32),
        ],
        scratch_shapes=[
            pltpu.VMEM((count, side, side), gradients.dtype),
            pltpu.VMEM((count, side, side), second_moment.dtype),
            pltpu.SemaphoreType.DMA((2, count)),
        ],
        compiler_params=kernel_params(8),
        cost_estimate=pl.CostEstimate(
            flops=8 * count * side * side,
            bytes_accessed=6 * count * side * side,
            transcendentals=2 * count * side * side,
        ),
    )(
        pltpu.with_memory_space_constraint(gradients, pltpu.HBM),
        pltpu.with_memory_space_constraint(second_moment, pltpu.HBM),
    )


def tail_kernel(total_ref, out_ref):
    total = jnp.sum(total_ref[0:1, :], keepdims=True)
    high = total.astype(jnp.bfloat16).astype(jnp.float32)
    rest = total - high
    middle = rest.astype(jnp.bfloat16).astype(jnp.float32)
    low = rest - middle
    row = lax.broadcasted_iota(jnp.int32, out_ref.shape, 0)
    value = jnp.where(row == 0, high, jnp.where(row == 1, middle, jnp.where(row == 2, low, 0.0)))
    out_ref[...] = value.astype(jnp.bfloat16)


def sum_tail(total, side):
    return pl.pallas_call(
        tail_kernel,
        in_specs=[pl.BlockSpec(memory_space=pltpu.VMEM)],
        out_specs=pl.BlockSpec(memory_space=pltpu.VMEM),
        out_shape=jax.ShapeDtypeStruct((TAIL, side), jnp.bfloat16),
        compiler_params=kernel_params(2),
        cost_estimate=pl.CostEstimate(flops=4096, bytes_accessed=32768, transcendentals=0),
    )(total)


def precondition_kernel(m, me_ref, grad_ref, left_ref, right_ref, tail_ref, out_ref):
    side = grad_ref.shape[0]
    slot = me_ref[0] ^ m
    half_done = jnp.dot(
        left_ref[0, slot], grad_ref[...], preferred_element_type=jnp.float32
    ).astype(jnp.bfloat16)
    out_ref[0:side, :] = jnp.dot(
        half_done, right_ref[0, slot], preferred_element_type=jnp.float32
    ).astype(jnp.bfloat16)
    out_ref[side:, :] = tail_ref[...]


def precondition(m, me, block, left_root, right_root, tail):
    side = block.shape[0]
    return pl.pallas_call(
        functools.partial(precondition_kernel, m),
        grid_spec=pltpu.PrefetchScalarGridSpec(
            num_scalar_prefetch=1,
            grid=(),
            in_specs=[pl.BlockSpec(memory_space=pltpu.VMEM)] * 4,
            out_specs=pl.BlockSpec(memory_space=pltpu.VMEM),
        ),
        out_shape=jax.ShapeDtypeStruct((side + TAIL, side), jnp.bfloat16),
        compiler_params=kernel_params(6),
        cost_estimate=pl.CostEstimate(
            flops=4 * side**3, bytes_accessed=8 * side * side, transcendentals=0
        ),
    )(me, block, left_root, right_root, tail)


def gram_kernel(order, me_ref, *refs):
    count = len(refs) - 4
    grads = refs[:count]
    left_ref, right_ref, new_left_ref, new_right_ref = refs[count:]
    step = pl.program_id(0)
    for k, m in enumerate(order):

        @pl.when(step == m)
        def _():
            block = grads[k][...]
            gram_left = lax.dot_general(
                block, block, (((1,), (1,)), ((), ())), preferred_element_type=jnp.float32
            )
            gram_right = lax.dot_general(
                block, block, (((0,), (0,)), ((), ())), preferred_element_type=jnp.float32
            )
            new_left_ref[0, 0] = DECAY_RATE * left_ref[0, 0] + (1.0 - DECAY_RATE) * gram_left
            new_right_ref[0, 0] = DECAY_RATE * right_ref[0, 0] + (1.0 - DECAY_RATE) * gram_right


def gram_update(order, me, blocks, left_stats, right_stats):
    count, side = len(blocks), blocks[0].shape[0]
    stat = pl.BlockSpec((1, 1, side, side), lambda i, me_ref: (0, me_ref[0] ^ i, 0, 0))
    whole = pl.BlockSpec(memory_space=pltpu.VMEM)
    return pl.pallas_call(
        functools.partial(gram_kernel, order),
        grid_spec=pltpu.PrefetchScalarGridSpec(
            num_scalar_prefetch=1,
            grid=(count,),
            in_specs=[whole] * count + [stat, stat],
            out_specs=[stat, stat],
        ),
        out_shape=[
            jax.ShapeDtypeStruct(left_stats.shape, left_stats.dtype),
            jax.ShapeDtypeStruct(right_stats.shape, right_stats.dtype),
        ],
        compiler_params=kernel_params(12),
        cost_estimate=pl.CostEstimate(
            flops=4 * count * side**3, bytes_accessed=18 * count * side * side, transcendentals=0
        ),
    )(me, *blocks, left_stats, right_stats)


def finish_kernel(order, entries, owners_ref, me_ref, *refs):
    count = len(order)
    pieces = refs[:count]
    squares_ref, out_ref, held, sems = refs[count:]
    side = out_ref.shape[3]
    me = me_ref[0]
    named = [owners_ref[me * count + j] for j in range(count)]
    global_sq = jnp.zeros((1, 1), jnp.float32)
    for piece in pieces:
        terms = piece[side:, 0:1].astype(jnp.float32)
        global_sq = global_sq + jnp.sum(terms, axis=0, keepdims=True)
    clip_factor = jnp.minimum(1.0, UPDATE_RMS / jnp.sqrt(global_sq / entries))
    area = float(side * side)
    copies = []
    for k, m in enumerate(order):
        block = home_slot(named, me ^ m)
        pre_float = pieces[k][0:side, :].astype(jnp.float32)
        pre_sq = jnp.sum(pre_float * pre_float, keepdims=True)
        block_sq = jnp.sum(squares_ref[pl.ds(block, 1), :], axis=1, keepdims=True)
        graft_ratio = jnp.sqrt(block_sq / area) / jnp.sqrt(pre_sq / area + NORM_FLOOR)
        held[k] = (pre_float * (graft_ratio * clip_factor)).astype(jnp.bfloat16)
        copy = pltpu.make_async_copy(held.at[k], out_ref.at[0, block], sems.at[k])
        copy.start()
        copies.append(copy)
    for copy in copies:
        copy.wait()


def finish(order, owner_list, me, pieces, squares, entries):
    count, side = len(pieces), pieces[0].shape[1]
    return pl.pallas_call(
        functools.partial(finish_kernel, order, entries),
        grid_spec=pltpu.PrefetchScalarGridSpec(
            num_scalar_prefetch=2,
            grid=(),
            in_specs=[pl.BlockSpec(memory_space=pltpu.VMEM)] * (count + 1),
            out_specs=pl.BlockSpec(memory_space=pl.ANY),
            scratch_shapes=[
                pltpu.VMEM((count, side, side), jnp.bfloat16),
                pltpu.SemaphoreType.DMA((count,)),
            ],
        ),
        out_shape=jax.ShapeDtypeStruct((1, count, side, side), jnp.bfloat16),
        compiler_params=kernel_params(8),
        cost_estimate=pl.CostEstimate(
            flops=6 * count * side * side, bytes_accessed=4 * count * side * side, transcendentals=0
        ),
    )(owner_list, me, *pieces, squares)


def per_device_exchange(
    gradients, second_moment, owners, left_stats, right_stats, left_root, right_root
):
    count = lax.axis_size("fsdp")
    layers = lax.axis_size("layer")
    side = gradients.shape[3]
    me = lax.axis_index("fsdp").astype(jnp.int32).reshape(1)
    owner_list = owners[0, :, 0]
    order = list(range(count))

    def swap(value, m):
        if m == 0:
            return value
        return lax.ppermute(value, "fsdp", [(i, i ^ m) for i in range(count)])

    outgoing = route(order, owner_list, me, gradients)
    received = {m: swap(outgoing[m], m) for m in order}
    squares, total = adam_squares(gradients, second_moment)
    k = 1
    while k < layers:
        total = total + lax.ppermute(total, "layer", [(i, i ^ k) for i in range(layers)])
        k *= 2
    tail = sum_tail(total, side)
    returned = {
        m: swap(precondition(m, me, received[m], left_root, right_root, tail), m) for m in order
    }
    new_left, new_right = gram_update(
        order, me, [received[m] for m in order], left_stats, right_stats
    )
    entries = float(owner_list.shape[0] * layers * side * side)
    update = finish(order, owner_list, me, [returned[m] for m in order], squares, entries)
    return (update, new_left, new_right)


def per_device(gradients, second_moment, owners, left_stats, right_stats, left_root, right_root):
    owner_count, blocks, slots = lax.axis_size("fsdp"), gradients.shape[1], left_stats.shape[1]
    layers = lax.axis_size("layer")
    paired = owner_count == blocks == slots
    paired = paired and owner_count & (owner_count - 1) == 0 and layers & (layers - 1) == 0
    body = per_device_exchange if paired else per_device_general
    return body(
        gradients, second_moment, owners, left_stats, right_stats, left_root, right_root
    )


def solution(mesh):
    return jax.shard_map(
        per_device,
        mesh=mesh,
        in_specs=(
            P("layer", "fsdp", None, None),
            P("layer", "fsdp", None, None),
            P("layer", None, None),
            P("layer", "fsdp", None, None),
            P("layer", "fsdp", None, None),
            P("layer", "fsdp", None, None),
            P("layer", "fsdp", None, None),
        ),
        out_specs=(
            P("layer", "fsdp", None, None),
            P("layer", "fsdp", None, None),
            P("layer", "fsdp", None, None),
        ),
        check_vma=False,
    )
```

```python
import functools

import jax
import jax.numpy as jnp
from jax import lax
from jax.experimental import pallas as pl
from jax.experimental.pallas import tpu as pltpu
from jax.sharding import PartitionSpec as P

ADAM_EPS = 1e-08
DECAY_RATE = 0.95
UPDATE_RMS = 1.0
NORM_FLOOR = 1e-06


def selection_tables(owner_list, owner_count, blocks, slots_here, my_index):
    total_blocks = owner_list.shape[0]
    owner_hot = (owner_list[:, None] == lax.iota(jnp.int32, owner_count)[None, :]).astype(
        jnp.float32
    )
    row_ids = lax.iota(jnp.int32, total_blocks)
    strict_lower = (row_ids[:, None] > row_ids[None, :]).astype(jnp.float32)
    before_all = jnp.dot(strict_lower, owner_hot, precision=lax.Precision.HIGHEST)
    slot_number = jnp.sum(before_all * owner_hot, axis=1)
    mine_mask = (owner_list == my_index).astype(jnp.float32)
    slot_hot = (slot_number[:, None] == lax.iota(jnp.float32, slots_here)[None, :]).astype(
        jnp.float32
    ) * mine_mask[:, None]
    home_hot = ((row_ids // blocks)[:, None] == lax.iota(jnp.int32, owner_count)[None, :]).astype(
        jnp.float32
    )
    return (owner_hot, home_hot, slot_hot)


def owner_work(gathered, left_stats, right_stats, left_root, right_root):
    gram_left = jnp.einsum("sij,skj->sik", gathered, gathered, preferred_element_type=jnp.float32)
    gram_right = jnp.einsum("sji,sjk->sik", gathered, gathered, preferred_element_type=jnp.float32)
    new_left = DECAY_RATE * left_stats[0] + (1.0 - DECAY_RATE) * gram_left
    new_right = DECAY_RATE * right_stats[0] + (1.0 - DECAY_RATE) * gram_right
    half_done = jnp.einsum(
        "sij,sjk->sik", left_root[0], gathered, preferred_element_type=jnp.float32
    ).astype(jnp.bfloat16)
    preconditioned = jnp.einsum(
        "sij,sjk->sik", half_done, right_root[0], preferred_element_type=jnp.float32
    ).astype(jnp.bfloat16)
    return (preconditioned, new_left[None], new_right[None])


def per_device_general(gradients, second_moment, owners, left_stats, right_stats, left_root, right_root):
    owner_count = lax.axis_size("fsdp")
    my_index = lax.axis_index("fsdp")
    blocks = gradients.shape[1]
    block_side = gradients.shape[3]
    slots_here = left_stats.shape[1]
    grad_local = gradients[0]
    owner_list = owners[0, :, 0]
    total_blocks = owner_list.shape[0]
    adam_dir = grad_local.astype(jnp.float32) / (jnp.sqrt(second_moment[0]) + ADAM_EPS)
    block_sq = jnp.sum(adam_dir * adam_dir, axis=(1, 2))
    global_sq = lax.psum(jnp.sum(block_sq), ("fsdp", "layer"))
    entry_count = float(total_blocks * lax.axis_size("layer") * block_side * block_side)
    clip_factor = jnp.minimum(1.0, UPDATE_RMS / jnp.sqrt(global_sq / entry_count))
    owner_hot, home_hot, slot_hot = selection_tables(
        owner_list, owner_count, blocks, slots_here, my_index
    )
    first_row = my_index * blocks
    my_owner_hot = lax.dynamic_slice_in_dim(owner_hot, first_row, blocks, 0).astype(jnp.bfloat16)
    outgoing = jnp.einsum(
        "jo,jxy->oxy", my_owner_hot, grad_local, preferred_element_type=jnp.float32
    ).astype(jnp.bfloat16)
    received = lax.all_to_all(outgoing, "fsdp", split_axis=0, concat_axis=0, tiled=True)
    pick_table = jnp.einsum("bs,bh->sh", slot_hot, home_hot).astype(jnp.bfloat16)
    gathered = jnp.einsum(
        "sh,hxy->sxy", pick_table, received, preferred_element_type=jnp.float32
    ).astype(jnp.bfloat16)
    preconditioned, new_left, new_right = owner_work(
        gathered, left_stats, right_stats, left_root, right_root
    )
    answers = jnp.einsum(
        "sh,sxy->hxy", pick_table, preconditioned, preferred_element_type=jnp.float32
    ).astype(jnp.bfloat16)
    returned = lax.all_to_all(answers, "fsdp", split_axis=0, concat_axis=0, tiled=True)
    home_blocks = jnp.einsum(
        "jo,oxy->jxy", my_owner_hot, returned, preferred_element_type=jnp.float32
    )
    pre_float = home_blocks.astype(jnp.bfloat16).astype(jnp.float32)
    graft_ratio = jnp.sqrt(block_sq / float(block_side * block_side)) / jnp.sqrt(
        jnp.sum(pre_float * pre_float, axis=(1, 2)) / float(block_side * block_side) + NORM_FLOOR
    )
    update = (pre_float * (graft_ratio * clip_factor)[:, None, None]).astype(jnp.bfloat16)
    return (update[None], new_left, new_right)


TAIL = 16


def kernel_params(mebibytes):
    return pltpu.CompilerParams(vmem_limit_bytes=mebibytes * 2**20)


def home_slot(named, target):
    block = jnp.int32(0)
    for j in range(1, len(named)):
        block = jnp.where(named[j] == target, jnp.int32(j), block)
    return block


def route_kernel(order, owners_hbm, me_ref, grad_hbm, *refs):
    outs, (owners_ref, held, owner_sem, grad_sem) = refs[:-4], refs[-4:]
    count = held.shape[0]
    me = me_ref[0]
    fetch_owners = pltpu.make_async_copy(owners_hbm, owners_ref, owner_sem)
    fetch_grads = pltpu.make_async_copy(grad_hbm.at[0], held, grad_sem)
    fetch_owners.start()
    fetch_grads.start()
    fetch_owners.wait()
    named = [owners_ref[me * count + j] for j in range(count)]
    blocks = [home_slot(named, me ^ m) for m in order]
    fetch_grads.wait()
    for block, out in zip(blocks, outs):
        out[...] = held[block]


def route(order, owner_list, me, gradients):
    count, side = gradients.shape[1], gradients.shape[3]
    hbm = pl.BlockSpec(memory_space=pltpu.HBM)
    piece = jax.ShapeDtypeStruct((side, side), gradients.dtype)
    return pl.pallas_call(
        functools.partial(route_kernel, order),
        in_specs=[hbm, pl.BlockSpec(memory_space=pltpu.SMEM), hbm],
        out_specs=[pl.BlockSpec(memory_space=pltpu.VMEM)] * count,
        scratch_shapes=[
            pltpu.SMEM(owner_list.shape, jnp.int32),
            pltpu.VMEM((count, side, side), gradients.dtype),
            pltpu.SemaphoreType.DMA,
            pltpu.SemaphoreType.DMA,
        ],
        out_shape=[piece] * count,
        compiler_params=kernel_params(6),
        cost_estimate=pl.CostEstimate(
            flops=0, bytes_accessed=4 * count * side * side, transcendentals=0
        ),
    )(
        pltpu.with_memory_space_constraint(owner_list, pltpu.HBM),
        me,
        pltpu.with_memory_space_constraint(gradients, pltpu.HBM),
    )


def adam_kernel(grad_hbm, moment_hbm, out_ref, total_ref, grads, moments, sems):
    count, side = grads.shape[0], grads.shape[2]
    lanes = out_ref.shape[1]
    copies = []
    for b in range(count):
        pair = (
            pltpu.make_async_copy(grad_hbm.at[0, b], grads.at[b], sems.at[0, b]),
            pltpu.make_async_copy(moment_hbm.at[0, b], moments.at[b], sems.at[1, b]),
        )
        for copy in pair:
            copy.start()
        copies.append(pair)
    total = jnp.zeros((1, lanes), jnp.float32)
    for b, pair in enumerate(copies):
        for copy in pair:
            copy.wait()
        adam_dir = grads[b].astype(jnp.float32) / (jnp.sqrt(moments[b]) + ADAM_EPS)
        squares = jnp.sum(adam_dir * adam_dir, axis=0, keepdims=True)
        row = squares[:, 0:lanes]
        for k in range(lanes, side, lanes):
            row = row + squares[:, k : k + lanes]
        out_ref[b : b + 1, :] = row
        total = total + row
    total_ref[...] = jnp.broadcast_to(total, total_ref.shape)


def adam_squares(gradients, second_moment):
    count, side = gradients.shape[1], gradients.shape[3]
    hbm = pl.BlockSpec(memory_space=pltpu.HBM)
    return pl.pallas_call(
        adam_kernel,
        in_specs=[hbm, hbm],
        out_specs=[pl.BlockSpec(memory_space=pltpu.VMEM)] * 2,
        out_shape=[
            jax.ShapeDtypeStruct((count, 128), jnp.float32),
            jax.ShapeDtypeStruct((8, 128), jnp.float32),
        ],
        scratch_shapes=[
            pltpu.VMEM((count, side, side), gradients.dtype),
            pltpu.VMEM((count, side, side), second_moment.dtype),
            pltpu.SemaphoreType.DMA((2, count)),
        ],
        compiler_params=kernel_params(8),
        cost_estimate=pl.CostEstimate(
            flops=8 * count * side * side,
            bytes_accessed=6 * count * side * side,
            transcendentals=2 * count * side * side,
        ),
    )(
        pltpu.with_memory_space_constraint(gradients, pltpu.HBM),
        pltpu.with_memory_space_constraint(second_moment, pltpu.HBM),
    )


def tail_kernel(total_ref, out_ref):
    total = jnp.sum(total_ref[0:1, :], keepdims=True)
    high = total.astype(jnp.bfloat16).astype(jnp.float32)
    rest = total - high
    middle = rest.astype(jnp.bfloat16).astype(jnp.float32)
    low = rest - middle
    row = lax.broadcasted_iota(jnp.int32, out_ref.shape, 0)
    value = jnp.where(row == 0, high, jnp.where(row == 1, middle, jnp.where(row == 2, low, 0.0)))
    out_ref[...] = value.astype(jnp.bfloat16)


def sum_tail(total, side):
    return pl.pallas_call(
        tail_kernel,
        in_specs=[pl.BlockSpec(memory_space=pltpu.VMEM)],
        out_specs=pl.BlockSpec(memory_space=pltpu.VMEM),
        out_shape=jax.ShapeDtypeStruct((TAIL, side), jnp.bfloat16),
        compiler_params=kernel_params(2),
        cost_estimate=pl.CostEstimate(flops=4096, bytes_accessed=32768, transcendentals=0),
    )(total)


def precondition_kernel(m, rows, me_ref, grad_ref, left_ref, right_ref, tail_ref, out_ref):
    side = grad_ref.shape[0]
    slot = me_ref[0] ^ m
    half_done = jnp.dot(
        left_ref[0, slot], grad_ref[...], preferred_element_type=jnp.float32
    ).astype(jnp.bfloat16)
    out_ref[0:side, :] = jnp.dot(
        half_done, right_ref[0, slot], preferred_element_type=jnp.float32
    ).astype(jnp.bfloat16)
    if rows:
        out_ref[side:, :] = tail_ref[...]


def precondition(m, rows, me, block, left_root, right_root, tail):
    side = block.shape[0]
    return pl.pallas_call(
        functools.partial(precondition_kernel, m, rows),
        grid_spec=pltpu.PrefetchScalarGridSpec(
            num_scalar_prefetch=1,
            grid=(),
            in_specs=[pl.BlockSpec(memory_space=pltpu.VMEM)] * 4,
            out_specs=pl.BlockSpec(memory_space=pltpu.VMEM),
        ),
        out_shape=jax.ShapeDtypeStruct((side + rows, side), jnp.bfloat16),
        compiler_params=kernel_params(6),
        cost_estimate=pl.CostEstimate(
            flops=4 * side**3, bytes_accessed=8 * side * side, transcendentals=0
        ),
    )(me, block, left_root, right_root, tail)


def gram_kernel(order, me_ref, *refs):
    count = len(refs) - 4
    grads = refs[:count]
    left_ref, right_ref, new_left_ref, new_right_ref = refs[count:]
    step = pl.program_id(0)
    for k, m in enumerate(order):

        @pl.when(step == m)
        def _():
            block = grads[k][...]
            gram_left = lax.dot_general(
                block, block, (((1,), (1,)), ((), ())), preferred_element_type=jnp.float32
            )
            gram_right = lax.dot_general(
                block, block, (((0,), (0,)), ((), ())), preferred_element_type=jnp.float32
            )
            new_left_ref[0, 0] = DECAY_RATE * left_ref[0, 0] + (1.0 - DECAY_RATE) * gram_left
            new_right_ref[0, 0] = DECAY_RATE * right_ref[0, 0] + (1.0 - DECAY_RATE) * gram_right


def gram_update(order, me, blocks, left_stats, right_stats):
    count, side = len(blocks), blocks[0].shape[0]
    stat = pl.BlockSpec((1, 1, side, side), lambda i, me_ref: (0, me_ref[0] ^ i, 0, 0))
    whole = pl.BlockSpec(memory_space=pltpu.VMEM)
    return pl.pallas_call(
        functools.partial(gram_kernel, order),
        grid_spec=pltpu.PrefetchScalarGridSpec(
            num_scalar_prefetch=1,
            grid=(count,),
            in_specs=[whole] * count + [stat, stat],
            out_specs=[stat, stat],
        ),
        out_shape=[
            jax.ShapeDtypeStruct(left_stats.shape, left_stats.dtype),
            jax.ShapeDtypeStruct(right_stats.shape, right_stats.dtype),
        ],
        compiler_params=kernel_params(12),
        cost_estimate=pl.CostEstimate(
            flops=4 * count * side**3, bytes_accessed=18 * count * side * side, transcendentals=0
        ),
    )(me, *blocks, left_stats, right_stats)


def finish_kernel(order, entries, owners_ref, me_ref, *refs):
    count = len(order)
    pieces = refs[:count]
    squares_ref, tail_ref, out_ref, held, sums, sems = refs[count:]
    side, lanes = out_ref.shape[3], squares_ref.shape[1]
    me = me_ref[0]
    named = [owners_ref[me * count + j] for j in range(count)]
    blocks = [home_slot(named, me ^ m) for m in order]
    global_sq = jnp.zeros((1, 1), jnp.float32)
    for rows in [tail_ref[...]] + [piece[side:, :] for piece in pieces if piece.shape[0] > side]:
        terms = rows[:, 0:1].astype(jnp.float32)
        global_sq = global_sq + jnp.sum(terms, axis=0, keepdims=True)
    for k, piece in enumerate(pieces):
        pre_float = piece[0:side, :].astype(jnp.float32)
        row = jnp.sum(pre_float * pre_float, axis=0, keepdims=True)
        parts = [row[:, i : i + lanes] for i in range(0, side, lanes)]
        sums[0, k : k + 1, :] = functools.reduce(jnp.add, parts)
        sums[1, k : k + 1, :] = squares_ref[pl.ds(blocks[k], 1), :]
    area = float(side * side)
    pre_sq = jnp.sum(sums[0], axis=1, keepdims=True)
    block_sq = jnp.sum(sums[1], axis=1, keepdims=True)
    clip_factor = jnp.minimum(1.0, UPDATE_RMS / jnp.sqrt(global_sq / entries))
    graft_ratio = jnp.sqrt(block_sq / area) / jnp.sqrt(pre_sq / area + NORM_FLOOR)
    scale = graft_ratio * clip_factor
    copies = []
    for k, piece in enumerate(pieces):
        pre_float = piece[0:side, :].astype(jnp.float32)
        held[k] = (pre_float * scale[k : k + 1, :]).astype(jnp.bfloat16)
        copy = pltpu.make_async_copy(held.at[k], out_ref.at[0, blocks[k]], sems.at[k])
        copy.start()
        copies.append(copy)
    for copy in copies:
        copy.wait()


def finish(order, owner_list, me, pieces, squares, tail, entries):
    count, side = len(pieces), pieces[0].shape[1]
    return pl.pallas_call(
        functools.partial(finish_kernel, order, entries),
        grid_spec=pltpu.PrefetchScalarGridSpec(
            num_scalar_prefetch=2,
            grid=(),
            in_specs=[pl.BlockSpec(memory_space=pltpu.VMEM)] * (count + 2),
            out_specs=pl.BlockSpec(memory_space=pl.ANY),
            scratch_shapes=[
                pltpu.VMEM((count, side, side), jnp.bfloat16),
                pltpu.VMEM((2, count, squares.shape[1]), jnp.float32),
                pltpu.SemaphoreType.DMA((count,)),
            ],
        ),
        out_shape=jax.ShapeDtypeStruct((1, count, side, side), jnp.bfloat16),
        compiler_params=kernel_params(8),
        cost_estimate=pl.CostEstimate(
            flops=6 * count * side * side, bytes_accessed=4 * count * side * side, transcendentals=0
        ),
    )(owner_list, me, *pieces, squares, tail)


def doublings(size):
    return [2**k for k in range(size.bit_length() - 1)]


def per_device_exchange(
    gradients, second_moment, owners, left_stats, right_stats, left_root, right_root
):
    count = lax.axis_size("fsdp")
    layers = lax.axis_size("layer")
    side = gradients.shape[3]
    me = lax.axis_index("fsdp").astype(jnp.int32).reshape(1)
    owner_list = owners[0, :, 0]
    half = count // 2
    order = [0, half, *range(1, half), *range(half + 1, count)]

    def swap(value, m, axis="fsdp"):
        if m == 0:
            return value
        return lax.ppermute(value, axis, [(i, i ^ m) for i in range(lax.axis_size(axis))])

    outgoing = route(order, owner_list, me, gradients)
    received = [swap(block, m) for m, block in zip(order, outgoing)]
    squares, total = adam_squares(gradients, second_moment)
    for k in doublings(layers):
        total = total + swap(total, k, "layer")
    tail = sum_tail(total, side)
    returned = []
    for m, block in zip(order, received):
        rows = TAIL if m else 0
        done = precondition(m, rows, me, block, left_root, right_root, tail)
        returned.append(swap(done, m))
    new_left, new_right = gram_update(order, me, received, left_stats, right_stats)
    entries = float(owner_list.shape[0] * layers * side * side)
    update = finish(order, owner_list, me, returned, squares, tail, entries)
    return (update, new_left, new_right)


def per_device(gradients, second_moment, owners, left_stats, right_stats, left_root, right_root):
    owner_count, blocks, slots = lax.axis_size("fsdp"), gradients.shape[1], left_stats.shape[1]
    layers = lax.axis_size("layer")
    paired = owner_count == blocks == slots
    paired = paired and owner_count & (owner_count - 1) == 0 and layers & (layers - 1) == 0
    body = per_device_exchange if paired else per_device_general
    return body(
        gradients, second_moment, owners, left_stats, right_stats, left_root, right_root
    )


def solution(mesh):
    return jax.shard_map(
        per_device,
        mesh=mesh,
        in_specs=(
            P("layer", "fsdp", None, None),
            P("layer", "fsdp", None, None),
            P("layer", None, None),
            P("layer", "fsdp", None, None),
            P("layer", "fsdp", None, None),
            P("layer", "fsdp", None, None),
            P("layer", "fsdp", None, None),
        ),
        out_specs=(
            P("layer", "fsdp", None, None),
            P("layer", "fsdp", None, None),
            P("layer", "fsdp", None, None),
        ),
        check_vma=False,
    )
```

```python
import functools

import jax
import jax.numpy as jnp
from jax import lax
from jax.experimental import pallas as pl
from jax.experimental.pallas import tpu as pltpu
from jax.sharding import PartitionSpec as P

ADAM_EPS = 1e-08
DECAY_RATE = 0.95
UPDATE_RMS = 1.0
NORM_FLOOR = 1e-06


def selection_tables(owner_list, owner_count, blocks, slots_here, my_index):
    total_blocks = owner_list.shape[0]
    owner_hot = (owner_list[:, None] == lax.iota(jnp.int32, owner_count)[None, :]).astype(
        jnp.float32
    )
    row_ids = lax.iota(jnp.int32, total_blocks)
    strict_lower = (row_ids[:, None] > row_ids[None, :]).astype(jnp.float32)
    before_all = jnp.dot(strict_lower, owner_hot, precision=lax.Precision.HIGHEST)
    slot_number = jnp.sum(before_all * owner_hot, axis=1)
    mine_mask = (owner_list == my_index).astype(jnp.float32)
    slot_hot = (slot_number[:, None] == lax.iota(jnp.float32, slots_here)[None, :]).astype(
        jnp.float32
    ) * mine_mask[:, None]
    home_hot = ((row_ids // blocks)[:, None] == lax.iota(jnp.int32, owner_count)[None, :]).astype(
        jnp.float32
    )
    return (owner_hot, home_hot, slot_hot)


def owner_work(gathered, left_stats, right_stats, left_root, right_root):
    gram_left = jnp.einsum("sij,skj->sik", gathered, gathered, preferred_element_type=jnp.float32)
    gram_right = jnp.einsum("sji,sjk->sik", gathered, gathered, preferred_element_type=jnp.float32)
    new_left = DECAY_RATE * left_stats[0] + (1.0 - DECAY_RATE) * gram_left
    new_right = DECAY_RATE * right_stats[0] + (1.0 - DECAY_RATE) * gram_right
    half_done = jnp.einsum(
        "sij,sjk->sik", left_root[0], gathered, preferred_element_type=jnp.float32
    ).astype(jnp.bfloat16)
    preconditioned = jnp.einsum(
        "sij,sjk->sik", half_done, right_root[0], preferred_element_type=jnp.float32
    ).astype(jnp.bfloat16)
    return (preconditioned, new_left[None], new_right[None])


def per_device_general(gradients, second_moment, owners, left_stats, right_stats, left_root, right_root):
    owner_count = lax.axis_size("fsdp")
    my_index = lax.axis_index("fsdp")
    blocks = gradients.shape[1]
    block_side = gradients.shape[3]
    slots_here = left_stats.shape[1]
    grad_local = gradients[0]
    owner_list = owners[0, :, 0]
    total_blocks = owner_list.shape[0]
    adam_dir = grad_local.astype(jnp.float32) / (jnp.sqrt(second_moment[0]) + ADAM_EPS)
    block_sq = jnp.sum(adam_dir * adam_dir, axis=(1, 2))
    global_sq = lax.psum(jnp.sum(block_sq), ("fsdp", "layer"))
    entry_count = float(total_blocks * lax.axis_size("layer") * block_side * block_side)
    clip_factor = jnp.minimum(1.0, UPDATE_RMS / jnp.sqrt(global_sq / entry_count))
    owner_hot, home_hot, slot_hot = selection_tables(
        owner_list, owner_count, blocks, slots_here, my_index
    )
    first_row = my_index * blocks
    my_owner_hot = lax.dynamic_slice_in_dim(owner_hot, first_row, blocks, 0).astype(jnp.bfloat16)
    outgoing = jnp.einsum(
        "jo,jxy->oxy", my_owner_hot, grad_local, preferred_element_type=jnp.float32
    ).astype(jnp.bfloat16)
    received = lax.all_to_all(outgoing, "fsdp", split_axis=0, concat_axis=0, tiled=True)
    pick_table = jnp.einsum("bs,bh->sh", slot_hot, home_hot).astype(jnp.bfloat16)
    gathered = jnp.einsum(
        "sh,hxy->sxy", pick_table, received, preferred_element_type=jnp.float32
    ).astype(jnp.bfloat16)
    preconditioned, new_left, new_right = owner_work(
        gathered, left_stats, right_stats, left_root, right_root
    )
    answers = jnp.einsum(
        "sh,sxy->hxy", pick_table, preconditioned, preferred_element_type=jnp.float32
    ).astype(jnp.bfloat16)
    returned = lax.all_to_all(answers, "fsdp", split_axis=0, concat_axis=0, tiled=True)
    home_blocks = jnp.einsum(
        "jo,oxy->jxy", my_owner_hot, returned, preferred_element_type=jnp.float32
    )
    pre_float = home_blocks.astype(jnp.bfloat16).astype(jnp.float32)
    graft_ratio = jnp.sqrt(block_sq / float(block_side * block_side)) / jnp.sqrt(
        jnp.sum(pre_float * pre_float, axis=(1, 2)) / float(block_side * block_side) + NORM_FLOOR
    )
    update = (pre_float * (graft_ratio * clip_factor)[:, None, None]).astype(jnp.bfloat16)
    return (update[None], new_left, new_right)


TAIL = 16


def kernel_params(mebibytes):
    return pltpu.CompilerParams(vmem_limit_bytes=mebibytes * 2**20)


def home_slot(named, target):
    block = jnp.int32(0)
    for j in range(1, len(named)):
        block = jnp.where(named[j] == target, jnp.int32(j), block)
    return block


def route_kernel(order, owners_hbm, me_ref, grad_hbm, *refs):
    outs, (owners_ref, held, owner_sem, grad_sem) = refs[:-4], refs[-4:]
    count = held.shape[0]
    me = me_ref[0]
    fetch_owners = pltpu.make_async_copy(owners_hbm, owners_ref, owner_sem)
    fetch_grads = pltpu.make_async_copy(grad_hbm.at[0], held, grad_sem)
    fetch_owners.start()
    fetch_grads.start()
    fetch_owners.wait()
    named = [owners_ref[me * count + j] for j in range(count)]
    blocks = [home_slot(named, me ^ m) for m in order]
    fetch_grads.wait()
    for block, out in zip(blocks, outs):
        out[...] = held[block]


def route(order, owner_list, me, gradients):
    count, side = gradients.shape[1], gradients.shape[3]
    hbm = pl.BlockSpec(memory_space=pltpu.HBM)
    piece = jax.ShapeDtypeStruct((side, side), gradients.dtype)
    return pl.pallas_call(
        functools.partial(route_kernel, order),
        in_specs=[hbm, pl.BlockSpec(memory_space=pltpu.SMEM), hbm],
        out_specs=[pl.BlockSpec(memory_space=pltpu.VMEM)] * count,
        scratch_shapes=[
            pltpu.SMEM(owner_list.shape, jnp.int32),
            pltpu.VMEM((count, side, side), gradients.dtype),
            pltpu.SemaphoreType.DMA,
            pltpu.SemaphoreType.DMA,
        ],
        out_shape=[piece] * count,
        compiler_params=kernel_params(6),
        cost_estimate=pl.CostEstimate(
            flops=0, bytes_accessed=4 * count * side * side, transcendentals=0
        ),
    )(
        pltpu.with_memory_space_constraint(owner_list, pltpu.HBM),
        me,
        pltpu.with_memory_space_constraint(gradients, pltpu.HBM),
    )


def adam_kernel(grad_hbm, moment_hbm, out_ref, total_ref, grads, moments, sems):
    count, side = grads.shape[0], grads.shape[2]
    lanes = out_ref.shape[1]
    copies = []
    for b in range(count):
        pair = (
            pltpu.make_async_copy(grad_hbm.at[0, b], grads.at[b], sems.at[0, b]),
            pltpu.make_async_copy(moment_hbm.at[0, b], moments.at[b], sems.at[1, b]),
        )
        for copy in pair:
            copy.start()
        copies.append(pair)
    total = jnp.zeros((1, lanes), jnp.float32)
    for b, pair in enumerate(copies):
        for copy in pair:
            copy.wait()
        adam_dir = grads[b].astype(jnp.float32) / (jnp.sqrt(moments[b]) + ADAM_EPS)
        squares = jnp.sum(adam_dir * adam_dir, axis=0, keepdims=True)
        row = squares[:, 0:lanes]
        for k in range(lanes, side, lanes):
            row = row + squares[:, k : k + lanes]
        out_ref[b : b + 1, :] = row
        total = total + row
    total_ref[...] = jnp.broadcast_to(total, total_ref.shape)


def adam_squares(gradients, second_moment):
    count, side = gradients.shape[1], gradients.shape[3]
    hbm = pl.BlockSpec(memory_space=pltpu.HBM)
    return pl.pallas_call(
        adam_kernel,
        in_specs=[hbm, hbm],
        out_specs=[pl.BlockSpec(memory_space=pltpu.VMEM)] * 2,
        out_shape=[
            jax.ShapeDtypeStruct((count, 128), jnp.float32),
            jax.ShapeDtypeStruct((8, 128), jnp.float32),
        ],
        scratch_shapes=[
            pltpu.VMEM((count, side, side), gradients.dtype),
            pltpu.VMEM((count, side, side), second_moment.dtype),
            pltpu.SemaphoreType.DMA((2, count)),
        ],
        compiler_params=kernel_params(8),
        cost_estimate=pl.CostEstimate(
            flops=8 * count * side * side,
            bytes_accessed=6 * count * side * side,
            transcendentals=2 * count * side * side,
        ),
    )(
        pltpu.with_memory_space_constraint(gradients, pltpu.HBM),
        pltpu.with_memory_space_constraint(second_moment, pltpu.HBM),
    )


def as_rows(total, shape):
    high = total.astype(jnp.bfloat16).astype(jnp.float32)
    rest = total - high
    middle = rest.astype(jnp.bfloat16).astype(jnp.float32)
    low = rest - middle
    row = lax.broadcasted_iota(jnp.int32, shape, 0)
    value = jnp.where(row == 0, high, jnp.where(row == 1, middle, jnp.where(row == 2, low, 0.0)))
    return value.astype(jnp.bfloat16)


def from_rows(rows):
    return jnp.sum(rows[:, 0:1].astype(jnp.float32), axis=0, keepdims=True)


def attach_kernel(total_ref, *refs):
    count = len(refs) // 2
    side = refs[0].shape[0]
    rows = as_rows(jnp.sum(total_ref[0:1, :], keepdims=True), (TAIL, side))
    for block, out in zip(refs[:count], refs[count:]):
        out[0:side, :] = block[...]
        out[side:, :] = rows


def attach(total, blocks):
    side, other = blocks[0].shape
    vmem = pl.BlockSpec(memory_space=pltpu.VMEM)
    longer = jax.ShapeDtypeStruct((side + TAIL, other), jnp.bfloat16)
    return pl.pallas_call(
        attach_kernel,
        in_specs=[vmem] * (1 + len(blocks)),
        out_specs=[vmem] * len(blocks),
        out_shape=[longer] * len(blocks),
        compiler_params=kernel_params(4),
        cost_estimate=pl.CostEstimate(
            flops=0, bytes_accessed=4 * len(blocks) * side * side, transcendentals=0
        ),
    )(total, *blocks)


def half_sum_kernel(total_ref, *refs):
    out_ref = refs[-1]
    total = jnp.sum(total_ref[0:1, :], keepdims=True)
    for block in refs[:-1]:
        total = total + from_rows(block[block.shape[1] :, :])
    out_ref[...] = as_rows(total, out_ref.shape)


def half_sum(total, blocks):
    vmem = pl.BlockSpec(memory_space=pltpu.VMEM)
    return pl.pallas_call(
        half_sum_kernel,
        in_specs=[vmem] * (1 + len(blocks)),
        out_specs=vmem,
        out_shape=jax.ShapeDtypeStruct((TAIL, blocks[0].shape[1]), jnp.bfloat16),
        compiler_params=kernel_params(4),
        cost_estimate=pl.CostEstimate(flops=4096, bytes_accessed=32768, transcendentals=0),
    )(total, *blocks)


def precondition_kernel(m, me_ref, grad_ref, left_ref, right_ref, *refs):
    tails, out_ref = refs[:-1], refs[-1]
    side = grad_ref.shape[1]
    slot = me_ref[0] ^ m
    half_done = jnp.dot(
        left_ref[0, slot], grad_ref[0:side, :], preferred_element_type=jnp.float32
    ).astype(jnp.bfloat16)
    out_ref[0:side, :] = jnp.dot(
        half_done, right_ref[0, slot], preferred_element_type=jnp.float32
    ).astype(jnp.bfloat16)
    for tail_ref in tails:
        out_ref[side:, :] = tail_ref[...]


def precondition(m, me, block, left_root, right_root, *tails):
    side = block.shape[1]
    return pl.pallas_call(
        functools.partial(precondition_kernel, m),
        grid_spec=pltpu.PrefetchScalarGridSpec(
            num_scalar_prefetch=1,
            grid=(),
            in_specs=[pl.BlockSpec(memory_space=pltpu.VMEM)] * (3 + len(tails)),
            out_specs=pl.BlockSpec(memory_space=pltpu.VMEM),
        ),
        out_shape=jax.ShapeDtypeStruct((side + TAIL * len(tails), side), jnp.bfloat16),
        compiler_params=kernel_params(6),
        cost_estimate=pl.CostEstimate(
            flops=4 * side**3, bytes_accessed=8 * side * side, transcendentals=0
        ),
    )(me, block, left_root, right_root, *tails)


def gram_kernel(order, me_ref, *refs):
    count = len(refs) - 4
    grads = refs[:count]
    left_ref, right_ref, new_left_ref, new_right_ref = refs[count:]
    step = pl.program_id(0)
    for k, m in enumerate(order):

        @pl.when(step == m)
        def _():
            block = grads[k][0 : grads[k].shape[1], :]
            gram_left = lax.dot_general(
                block, block, (((1,), (1,)), ((), ())), preferred_element_type=jnp.float32
            )
            gram_right = lax.dot_general(
                block, block, (((0,), (0,)), ((), ())), preferred_element_type=jnp.float32
            )
            new_left_ref[0, 0] = DECAY_RATE * left_ref[0, 0] + (1.0 - DECAY_RATE) * gram_left
            new_right_ref[0, 0] = DECAY_RATE * right_ref[0, 0] + (1.0 - DECAY_RATE) * gram_right


def gram_update(order, me, blocks, left_stats, right_stats):
    count, side = len(blocks), blocks[0].shape[1]
    stat = pl.BlockSpec((1, 1, side, side), lambda i, me_ref: (0, me_ref[0] ^ i, 0, 0))
    whole = pl.BlockSpec(memory_space=pltpu.VMEM)
    return pl.pallas_call(
        functools.partial(gram_kernel, order),
        grid_spec=pltpu.PrefetchScalarGridSpec(
            num_scalar_prefetch=1,
            grid=(count,),
            in_specs=[whole] * count + [stat, stat],
            out_specs=[stat, stat],
        ),
        out_shape=[
            jax.ShapeDtypeStruct(left_stats.shape, left_stats.dtype),
            jax.ShapeDtypeStruct(right_stats.shape, right_stats.dtype),
        ],
        compiler_params=kernel_params(12),
        cost_estimate=pl.CostEstimate(
            flops=4 * count * side**3, bytes_accessed=18 * count * side * side, transcendentals=0
        ),
    )(me, *blocks, left_stats, right_stats)


def finish_kernel(order, entries, owners_ref, me_ref, *refs):
    count = len(order)
    pieces = refs[:count]
    squares_ref, tail_ref, out_ref, held, sums, sems = refs[count:]
    side, lanes = out_ref.shape[3], squares_ref.shape[1]
    me = me_ref[0]
    named = [owners_ref[me * count + j] for j in range(count)]
    blocks = [home_slot(named, me ^ m) for m in order]
    global_sq = from_rows(tail_ref[...])
    for piece in pieces:
        if piece.shape[0] > side:
            global_sq = global_sq + from_rows(piece[side:, :])
    for k, piece in enumerate(pieces):
        pre_float = piece[0:side, :].astype(jnp.float32)
        row = jnp.sum(pre_float * pre_float, axis=0, keepdims=True)
        parts = [row[:, i : i + lanes] for i in range(0, side, lanes)]
        sums[0, k : k + 1, :] = functools.reduce(jnp.add, parts)
        sums[1, k : k + 1, :] = squares_ref[pl.ds(blocks[k], 1), :]
    area = float(side * side)
    pre_sq = jnp.sum(sums[0], axis=1, keepdims=True)
    block_sq = jnp.sum(sums[1], axis=1, keepdims=True)
    clip_factor = jnp.minimum(1.0, UPDATE_RMS / jnp.sqrt(global_sq / entries))
    graft_ratio = jnp.sqrt(block_sq / area) / jnp.sqrt(pre_sq / area + NORM_FLOOR)
    scale = graft_ratio * clip_factor
    copies = []
    for k, piece in enumerate(pieces):
        pre_float = piece[0:side, :].astype(jnp.float32)
        held[k] = (pre_float * scale[k : k + 1, :]).astype(jnp.bfloat16)
        copy = pltpu.make_async_copy(held.at[k], out_ref.at[0, blocks[k]], sems.at[k])
        copy.start()
        copies.append(copy)
    for copy in copies:
        copy.wait()


def finish(order, owner_list, me, pieces, squares, tail, entries):
    count, side = len(pieces), pieces[0].shape[1]
    return pl.pallas_call(
        functools.partial(finish_kernel, order, entries),
        grid_spec=pltpu.PrefetchScalarGridSpec(
            num_scalar_prefetch=2,
            grid=(),
            in_specs=[pl.BlockSpec(memory_space=pltpu.VMEM)] * (count + 2),
            out_specs=pl.BlockSpec(memory_space=pl.ANY),
            scratch_shapes=[
                pltpu.VMEM((count, side, side), jnp.bfloat16),
                pltpu.VMEM((2, count, squares.shape[1]), jnp.float32),
                pltpu.SemaphoreType.DMA((count,)),
            ],
        ),
        out_shape=jax.ShapeDtypeStruct((1, count, side, side), jnp.bfloat16),
        compiler_params=kernel_params(8),
        cost_estimate=pl.CostEstimate(
            flops=6 * count * side * side, bytes_accessed=4 * count * side * side, transcendentals=0
        ),
    )(owner_list, me, *pieces, squares, tail)


def doublings(size):
    return [2**k for k in range(size.bit_length() - 1)]


def per_device_exchange(
    gradients, second_moment, owners, left_stats, right_stats, left_root, right_root
):
    count = lax.axis_size("fsdp")
    layers = lax.axis_size("layer")
    side = gradients.shape[3]
    me = lax.axis_index("fsdp").astype(jnp.int32).reshape(1)
    owner_list = owners[0, :, 0]
    half = count // 2
    order = [0, half, *range(1, half), *range(count - 1, half, -1)]
    near = [m for m in order if 0 < m < half]

    def swap(value, m, axis="fsdp"):
        if m == 0:
            return value
        return lax.ppermute(value, axis, [(i, i ^ m) for i in range(lax.axis_size(axis))])

    outgoing = dict(zip(order, route(order, owner_list, me, gradients)))
    squares, total = adam_squares(gradients, second_moment)
    for k in doublings(layers):
        total = total + swap(total, k, "layer")
    outgoing.update(zip(near, attach(total, [outgoing[m] for m in near])))
    received = {m: swap(outgoing[m], m) for m in order}
    tail = half_sum(total, [received[m] for m in near])
    returned = []
    for m in order:
        tails = (tail,) if m == half else ()
        done = precondition(m, me, received[m], left_root, right_root, *tails)
        returned.append(swap(done, m))
    new_left, new_right = gram_update(
        order, me, [received[m] for m in order], left_stats, right_stats
    )
    entries = float(owner_list.shape[0] * layers * side * side)
    update = finish(order, owner_list, me, returned, squares, tail, entries)
    return (update, new_left, new_right)


def per_device(gradients, second_moment, owners, left_stats, right_stats, left_root, right_root):
    owner_count, blocks, slots = lax.axis_size("fsdp"), gradients.shape[1], left_stats.shape[1]
    layers = lax.axis_size("layer")
    paired = owner_count == blocks == slots and owner_count >= 4
    paired = paired and owner_count & (owner_count - 1) == 0 and layers & (layers - 1) == 0
    body = per_device_exchange if paired else per_device_general
    return body(
        gradients, second_moment, owners, left_stats, right_stats, left_root, right_root
    )


def solution(mesh):
    return jax.shard_map(
        per_device,
        mesh=mesh,
        in_specs=(
            P("layer", "fsdp", None, None),
            P("layer", "fsdp", None, None),
            P("layer", None, None),
            P("layer", "fsdp", None, None),
            P("layer", "fsdp", None, None),
            P("layer", "fsdp", None, None),
            P("layer", "fsdp", None, None),
        ),
        out_specs=(
            P("layer", "fsdp", None, None),
            P("layer", "fsdp", None, None),
            P("layer", "fsdp", None, None),
        ),
        check_vma=False,
    )
```

```python
import functools

import jax
import jax.numpy as jnp
from jax import lax
from jax.experimental import pallas as pl
from jax.experimental.pallas import tpu as pltpu
from jax.sharding import PartitionSpec as P

ADAM_EPS = 1e-08
DECAY_RATE = 0.95
UPDATE_RMS = 1.0
NORM_FLOOR = 1e-06


def selection_tables(owner_list, owner_count, blocks, slots_here, my_index):
    total_blocks = owner_list.shape[0]
    owner_hot = (owner_list[:, None] == lax.iota(jnp.int32, owner_count)[None, :]).astype(
        jnp.float32
    )
    row_ids = lax.iota(jnp.int32, total_blocks)
    strict_lower = (row_ids[:, None] > row_ids[None, :]).astype(jnp.float32)
    before_all = jnp.dot(strict_lower, owner_hot, precision=lax.Precision.HIGHEST)
    slot_number = jnp.sum(before_all * owner_hot, axis=1)
    mine_mask = (owner_list == my_index).astype(jnp.float32)
    slot_hot = (slot_number[:, None] == lax.iota(jnp.float32, slots_here)[None, :]).astype(
        jnp.float32
    ) * mine_mask[:, None]
    home_hot = ((row_ids // blocks)[:, None] == lax.iota(jnp.int32, owner_count)[None, :]).astype(
        jnp.float32
    )
    return (owner_hot, home_hot, slot_hot)


def owner_work(gathered, left_stats, right_stats, left_root, right_root):
    gram_left = jnp.einsum("sij,skj->sik", gathered, gathered, preferred_element_type=jnp.float32)
    gram_right = jnp.einsum("sji,sjk->sik", gathered, gathered, preferred_element_type=jnp.float32)
    new_left = DECAY_RATE * left_stats[0] + (1.0 - DECAY_RATE) * gram_left
    new_right = DECAY_RATE * right_stats[0] + (1.0 - DECAY_RATE) * gram_right
    half_done = jnp.einsum(
        "sij,sjk->sik", left_root[0], gathered, preferred_element_type=jnp.float32
    ).astype(jnp.bfloat16)
    preconditioned = jnp.einsum(
        "sij,sjk->sik", half_done, right_root[0], preferred_element_type=jnp.float32
    ).astype(jnp.bfloat16)
    return (preconditioned, new_left[None], new_right[None])


def per_device_general(gradients, second_moment, owners, left_stats, right_stats, left_root, right_root):
    owner_count = lax.axis_size("fsdp")
    my_index = lax.axis_index("fsdp")
    blocks = gradients.shape[1]
    block_side = gradients.shape[3]
    slots_here = left_stats.shape[1]
    grad_local = gradients[0]
    owner_list = owners[0, :, 0]
    total_blocks = owner_list.shape[0]
    adam_dir = grad_local.astype(jnp.float32) / (jnp.sqrt(second_moment[0]) + ADAM_EPS)
    block_sq = jnp.sum(adam_dir * adam_dir, axis=(1, 2))
    global_sq = lax.psum(jnp.sum(block_sq), ("fsdp", "layer"))
    entry_count = float(total_blocks * lax.axis_size("layer") * block_side * block_side)
    clip_factor = jnp.minimum(1.0, UPDATE_RMS / jnp.sqrt(global_sq / entry_count))
    owner_hot, home_hot, slot_hot = selection_tables(
        owner_list, owner_count, blocks, slots_here, my_index
    )
    first_row = my_index * blocks
    my_owner_hot = lax.dynamic_slice_in_dim(owner_hot, first_row, blocks, 0).astype(jnp.bfloat16)
    outgoing = jnp.einsum(
        "jo,jxy->oxy", my_owner_hot, grad_local, preferred_element_type=jnp.float32
    ).astype(jnp.bfloat16)
    received = lax.all_to_all(outgoing, "fsdp", split_axis=0, concat_axis=0, tiled=True)
    pick_table = jnp.einsum("bs,bh->sh", slot_hot, home_hot).astype(jnp.bfloat16)
    gathered = jnp.einsum(
        "sh,hxy->sxy", pick_table, received, preferred_element_type=jnp.float32
    ).astype(jnp.bfloat16)
    preconditioned, new_left, new_right = owner_work(
        gathered, left_stats, right_stats, left_root, right_root
    )
    answers = jnp.einsum(
        "sh,sxy->hxy", pick_table, preconditioned, preferred_element_type=jnp.float32
    ).astype(jnp.bfloat16)
    returned = lax.all_to_all(answers, "fsdp", split_axis=0, concat_axis=0, tiled=True)
    home_blocks = jnp.einsum(
        "jo,oxy->jxy", my_owner_hot, returned, preferred_element_type=jnp.float32
    )
    pre_float = home_blocks.astype(jnp.bfloat16).astype(jnp.float32)
    graft_ratio = jnp.sqrt(block_sq / float(block_side * block_side)) / jnp.sqrt(
        jnp.sum(pre_float * pre_float, axis=(1, 2)) / float(block_side * block_side) + NORM_FLOOR
    )
    update = (pre_float * (graft_ratio * clip_factor)[:, None, None]).astype(jnp.bfloat16)
    return (update[None], new_left, new_right)


TAIL = 16


def kernel_params(mebibytes):
    return pltpu.CompilerParams(vmem_limit_bytes=mebibytes * 2**20)


def home_slot(named, target):
    block = jnp.int32(0)
    for j in range(1, len(named)):
        block = jnp.where(named[j] == target, jnp.int32(j), block)
    return block


def route_kernel(order, owners_hbm, me_ref, grad_hbm, *refs):
    outs, (owners_ref, held, owner_sem, grad_sem) = refs[:-4], refs[-4:]
    count = held.shape[0]
    me = me_ref[0]
    fetch_owners = pltpu.make_async_copy(owners_hbm, owners_ref, owner_sem)
    fetch_grads = pltpu.make_async_copy(grad_hbm.at[0], held, grad_sem)
    fetch_owners.start()
    fetch_grads.start()
    fetch_owners.wait()
    named = [owners_ref[me * count + j] for j in range(count)]
    blocks = [home_slot(named, me ^ m) for m in order]
    fetch_grads.wait()
    for block, out in zip(blocks, outs):
        out[...] = held[block]


def route(order, owner_list, me, gradients):
    count, side = gradients.shape[1], gradients.shape[3]
    hbm = pl.BlockSpec(memory_space=pltpu.HBM)
    piece = jax.ShapeDtypeStruct((side, side), gradients.dtype)
    return pl.pallas_call(
        functools.partial(route_kernel, order),
        in_specs=[hbm, pl.BlockSpec(memory_space=pltpu.SMEM), hbm],
        out_specs=[pl.BlockSpec(memory_space=pltpu.VMEM)] * count,
        scratch_shapes=[
            pltpu.SMEM(owner_list.shape, jnp.int32),
            pltpu.VMEM((count, side, side), gradients.dtype),
            pltpu.SemaphoreType.DMA,
            pltpu.SemaphoreType.DMA,
        ],
        out_shape=[piece] * count,
        compiler_params=kernel_params(6),
        cost_estimate=pl.CostEstimate(
            flops=0, bytes_accessed=4 * count * side * side, transcendentals=0
        ),
    )(
        pltpu.with_memory_space_constraint(owner_list, pltpu.HBM),
        me,
        pltpu.with_memory_space_constraint(gradients, pltpu.HBM),
    )


def adam_kernel(grad_hbm, moment_hbm, out_ref, total_ref, grads, moments, sems):
    count, side = grads.shape[0], grads.shape[2]
    lanes = out_ref.shape[1]
    copies = []
    for b in range(count):
        pair = (
            pltpu.make_async_copy(grad_hbm.at[0, b], grads.at[b], sems.at[0, b]),
            pltpu.make_async_copy(moment_hbm.at[0, b], moments.at[b], sems.at[1, b]),
        )
        for copy in pair:
            copy.start()
        copies.append(pair)
    total = jnp.zeros((1, lanes), jnp.float32)
    for b, pair in enumerate(copies):
        for copy in pair:
            copy.wait()
        adam_dir = grads[b].astype(jnp.float32) / (jnp.sqrt(moments[b]) + ADAM_EPS)
        squares = jnp.sum(adam_dir * adam_dir, axis=0, keepdims=True)
        row = squares[:, 0:lanes]
        for k in range(lanes, side, lanes):
            row = row + squares[:, k : k + lanes]
        out_ref[b : b + 1, :] = row
        total = total + row
    total_ref[...] = jnp.broadcast_to(total, total_ref.shape)


def adam_squares(gradients, second_moment):
    count, side = gradients.shape[1], gradients.shape[3]
    hbm = pl.BlockSpec(memory_space=pltpu.HBM)
    return pl.pallas_call(
        adam_kernel,
        in_specs=[hbm, hbm],
        out_specs=[pl.BlockSpec(memory_space=pltpu.VMEM)] * 2,
        out_shape=[
            jax.ShapeDtypeStruct((count, 128), jnp.float32),
            jax.ShapeDtypeStruct((8, 128), jnp.float32),
        ],
        scratch_shapes=[
            pltpu.VMEM((count, side, side), gradients.dtype),
            pltpu.VMEM((count, side, side), second_moment.dtype),
            pltpu.SemaphoreType.DMA((2, count)),
        ],
        compiler_params=kernel_params(8),
        cost_estimate=pl.CostEstimate(
            flops=8 * count * side * side,
            bytes_accessed=6 * count * side * side,
            transcendentals=2 * count * side * side,
        ),
    )(
        pltpu.with_memory_space_constraint(gradients, pltpu.HBM),
        pltpu.with_memory_space_constraint(second_moment, pltpu.HBM),
    )


def tail_kernel(total_ref, out_ref):
    total = jnp.sum(total_ref[0:1, :], keepdims=True)
    high = total.astype(jnp.bfloat16).astype(jnp.float32)
    rest = total - high
    middle = rest.astype(jnp.bfloat16).astype(jnp.float32)
    low = rest - middle
    row = lax.broadcasted_iota(jnp.int32, out_ref.shape, 0)
    value = jnp.where(row == 0, high, jnp.where(row == 1, middle, jnp.where(row == 2, low, 0.0)))
    out_ref[...] = value.astype(jnp.bfloat16)


def sum_tail(total, side):
    return pl.pallas_call(
        tail_kernel,
        in_specs=[pl.BlockSpec(memory_space=pltpu.VMEM)],
        out_specs=pl.BlockSpec(memory_space=pltpu.VMEM),
        out_shape=jax.ShapeDtypeStruct((TAIL, side), jnp.bfloat16),
        compiler_params=kernel_params(2),
        cost_estimate=pl.CostEstimate(flops=4096, bytes_accessed=32768, transcendentals=0),
    )(total)


def precondition_kernel(m, rows, me_ref, grad_ref, left_ref, right_ref, tail_ref, out_ref):
    side = grad_ref.shape[0]
    slot = me_ref[0] ^ m
    half_done = jnp.dot(
        left_ref[0, slot], grad_ref[...], preferred_element_type=jnp.float32
    ).astype(jnp.bfloat16)
    out_ref[0:side, :] = jnp.dot(
        half_done, right_ref[0, slot], preferred_element_type=jnp.float32
    ).astype(jnp.bfloat16)
    if rows:
        out_ref[side:, :] = tail_ref[...]


def precondition(m, rows, me, block, left_root, right_root, tail):
    side = block.shape[0]
    return pl.pallas_call(
        functools.partial(precondition_kernel, m, rows),
        grid_spec=pltpu.PrefetchScalarGridSpec(
            num_scalar_prefetch=1,
            grid=(),
            in_specs=[pl.BlockSpec(memory_space=pltpu.VMEM)] * 4,
            out_specs=pl.BlockSpec(memory_space=pltpu.VMEM),
        ),
        out_shape=jax.ShapeDtypeStruct((side + rows, side), jnp.bfloat16),
        compiler_params=kernel_params(6),
        cost_estimate=pl.CostEstimate(
            flops=4 * side**3, bytes_accessed=8 * side * side, transcendentals=0
        ),
    )(me, block, left_root, right_root, tail)


def gram_kernel(order, me_ref, *refs):
    count = len(refs) - 4
    grads = refs[:count]
    left_ref, right_ref, new_left_ref, new_right_ref = refs[count:]
    step = pl.program_id(0)
    for k, m in enumerate(order):

        @pl.when(step == m)
        def _():
            block = grads[k][...]
            gram_left = lax.dot_general(
                block, block, (((1,), (1,)), ((), ())), preferred_element_type=jnp.float32
            )
            gram_right = lax.dot_general(
                block, block, (((0,), (0,)), ((), ())), preferred_element_type=jnp.float32
            )
            new_left_ref[0, 0] = DECAY_RATE * left_ref[0, 0] + (1.0 - DECAY_RATE) * gram_left
            new_right_ref[0, 0] = DECAY_RATE * right_ref[0, 0] + (1.0 - DECAY_RATE) * gram_right


def gram_update(order, me, blocks, left_stats, right_stats):
    count, side = len(blocks), blocks[0].shape[0]
    stat = pl.BlockSpec((1, 1, side, side), lambda i, me_ref: (0, me_ref[0] ^ i, 0, 0))
    whole = pl.BlockSpec(memory_space=pltpu.VMEM)
    return pl.pallas_call(
        functools.partial(gram_kernel, order),
        grid_spec=pltpu.PrefetchScalarGridSpec(
            num_scalar_prefetch=1,
            grid=(count,),
            in_specs=[whole] * count + [stat, stat],
            out_specs=[stat, stat],
        ),
        out_shape=[
            jax.ShapeDtypeStruct(left_stats.shape, left_stats.dtype),
            jax.ShapeDtypeStruct(right_stats.shape, right_stats.dtype),
        ],
        compiler_params=kernel_params(12),
        cost_estimate=pl.CostEstimate(
            flops=4 * count * side**3, bytes_accessed=18 * count * side * side, transcendentals=0
        ),
    )(me, *blocks, left_stats, right_stats)


def finish_kernel(order, entries, owners_ref, me_ref, *refs):
    count = len(order)
    pieces = refs[:count]
    squares_ref, tail_ref, out_ref, held, sums, sems = refs[count:]
    side, lanes = out_ref.shape[3], squares_ref.shape[1]
    me = me_ref[0]
    named = [owners_ref[me * count + j] for j in range(count)]
    blocks = [home_slot(named, me ^ m) for m in order]
    global_sq = jnp.zeros((1, 1), jnp.float32)
    for rows in [tail_ref[...]] + [piece[side:, :] for piece in pieces if piece.shape[0] > side]:
        terms = rows[:, 0:1].astype(jnp.float32)
        global_sq = global_sq + jnp.sum(terms, axis=0, keepdims=True)
    for k, piece in enumerate(pieces):
        pre_float = piece[0:side, :].astype(jnp.float32)
        row = jnp.sum(pre_float * pre_float, axis=0, keepdims=True)
        parts = [row[:, i : i + lanes] for i in range(0, side, lanes)]
        sums[0, k : k + 1, :] = functools.reduce(jnp.add, parts)
        sums[1, k : k + 1, :] = squares_ref[pl.ds(blocks[k], 1), :]
    area = float(side * side)
    pre_sq = jnp.sum(sums[0], axis=1, keepdims=True)
    block_sq = jnp.sum(sums[1], axis=1, keepdims=True)
    clip_factor = jnp.minimum(1.0, UPDATE_RMS / jnp.sqrt(global_sq / entries))
    graft_ratio = jnp.sqrt(block_sq / area) / jnp.sqrt(pre_sq / area + NORM_FLOOR)
    scale = graft_ratio * clip_factor
    copies = []
    for k, piece in enumerate(pieces):
        pre_float = piece[0:side, :].astype(jnp.float32)
        held[k] = (pre_float * scale[k : k + 1, :]).astype(jnp.bfloat16)
        copy = pltpu.make_async_copy(held.at[k], out_ref.at[0, blocks[k]], sems.at[k])
        copy.start()
        copies.append(copy)
    for copy in copies:
        copy.wait()


def finish(order, owner_list, me, pieces, squares, tail, entries):
    count, side = len(pieces), pieces[0].shape[1]
    return pl.pallas_call(
        functools.partial(finish_kernel, order, entries),
        grid_spec=pltpu.PrefetchScalarGridSpec(
            num_scalar_prefetch=2,
            grid=(),
            in_specs=[pl.BlockSpec(memory_space=pltpu.VMEM)] * (count + 2),
            out_specs=pl.BlockSpec(memory_space=pl.ANY),
            scratch_shapes=[
                pltpu.VMEM((count, side, side), jnp.bfloat16),
                pltpu.VMEM((2, count, squares.shape[1]), jnp.float32),
                pltpu.SemaphoreType.DMA((count,)),
            ],
        ),
        out_shape=jax.ShapeDtypeStruct((1, count, side, side), jnp.bfloat16),
        compiler_params=kernel_params(8),
        cost_estimate=pl.CostEstimate(
            flops=6 * count * side * side, bytes_accessed=4 * count * side * side, transcendentals=0
        ),
    )(owner_list, me, *pieces, squares, tail)


def doublings(size):
    return [2**k for k in range(size.bit_length() - 1)]


def per_device_exchange(
    gradients, second_moment, owners, left_stats, right_stats, left_root, right_root
):
    count = lax.axis_size("fsdp")
    layers = lax.axis_size("layer")
    side = gradients.shape[3]
    me = lax.axis_index("fsdp").astype(jnp.int32).reshape(1)
    owner_list = owners[0, :, 0]
    half = count // 2
    order = [*range(half - 1), half, half - 1, *range(half + 1, count)]

    def swap(value, m, axis="fsdp"):
        if m == 0:
            return value
        return lax.ppermute(value, axis, [(i, i ^ m) for i in range(lax.axis_size(axis))])

    outgoing = route(order, owner_list, me, gradients)
    received = [swap(block, m) for m, block in zip(order, outgoing)]
    squares, total = adam_squares(gradients, second_moment)
    for k in doublings(layers):
        total = total + swap(total, k, "layer")
    tail = sum_tail(total, side)
    returned = []
    for m, block in zip(order, received):
        rows = TAIL if m else 0
        done = precondition(m, rows, me, block, left_root, right_root, tail)
        returned.append(swap(done, m))
    new_left, new_right = gram_update(order, me, received, left_stats, right_stats)
    entries = float(owner_list.shape[0] * layers * side * side)
    update = finish(order, owner_list, me, returned, squares, tail, entries)
    return (update, new_left, new_right)


def per_device(gradients, second_moment, owners, left_stats, right_stats, left_root, right_root):
    owner_count, blocks, slots = lax.axis_size("fsdp"), gradients.shape[1], left_stats.shape[1]
    layers = lax.axis_size("layer")
    paired = owner_count == blocks == slots
    paired = paired and owner_count & (owner_count - 1) == 0 and layers & (layers - 1) == 0
    body = per_device_exchange if paired else per_device_general
    return body(
        gradients, second_moment, owners, left_stats, right_stats, left_root, right_root
    )


def solution(mesh):
    return jax.shard_map(
        per_device,
        mesh=mesh,
        in_specs=(
            P("layer", "fsdp", None, None),
            P("layer", "fsdp", None, None),
            P("layer", None, None),
            P("layer", "fsdp", None, None),
            P("layer", "fsdp", None, None),
            P("layer", "fsdp", None, None),
            P("layer", "fsdp", None, None),
        ),
        out_specs=(
            P("layer", "fsdp", None, None),
            P("layer", "fsdp", None, None),
            P("layer", "fsdp", None, None),
        ),
        check_vma=False,
    )
```

```python
import functools

import jax
import jax.numpy as jnp
from jax import lax
from jax.experimental import pallas as pl
from jax.experimental.pallas import tpu as pltpu
from jax.sharding import PartitionSpec as P

ADAM_EPS = 1e-08
DECAY_RATE = 0.95
UPDATE_RMS = 1.0
NORM_FLOOR = 1e-06


def selection_tables(owner_list, owner_count, blocks, slots_here, my_index):
    total_blocks = owner_list.shape[0]
    owner_hot = (owner_list[:, None] == lax.iota(jnp.int32, owner_count)[None, :]).astype(
        jnp.float32
    )
    row_ids = lax.iota(jnp.int32, total_blocks)
    strict_lower = (row_ids[:, None] > row_ids[None, :]).astype(jnp.float32)
    before_all = jnp.dot(strict_lower, owner_hot, precision=lax.Precision.HIGHEST)
    slot_number = jnp.sum(before_all * owner_hot, axis=1)
    mine_mask = (owner_list == my_index).astype(jnp.float32)
    slot_hot = (slot_number[:, None] == lax.iota(jnp.float32, slots_here)[None, :]).astype(
        jnp.float32
    ) * mine_mask[:, None]
    home_hot = ((row_ids // blocks)[:, None] == lax.iota(jnp.int32, owner_count)[None, :]).astype(
        jnp.float32
    )
    return (owner_hot, home_hot, slot_hot)


def owner_work(gathered, left_stats, right_stats, left_root, right_root):
    gram_left = jnp.einsum("sij,skj->sik", gathered, gathered, preferred_element_type=jnp.float32)
    gram_right = jnp.einsum("sji,sjk->sik", gathered, gathered, preferred_element_type=jnp.float32)
    new_left = DECAY_RATE * left_stats[0] + (1.0 - DECAY_RATE) * gram_left
    new_right = DECAY_RATE * right_stats[0] + (1.0 - DECAY_RATE) * gram_right
    half_done = jnp.einsum(
        "sij,sjk->sik", left_root[0], gathered, preferred_element_type=jnp.float32
    ).astype(jnp.bfloat16)
    preconditioned = jnp.einsum(
        "sij,sjk->sik", half_done, right_root[0], preferred_element_type=jnp.float32
    ).astype(jnp.bfloat16)
    return (preconditioned, new_left[None], new_right[None])


def per_device_general(gradients, second_moment, owners, left_stats, right_stats, left_root, right_root):
    owner_count = lax.axis_size("fsdp")
    my_index = lax.axis_index("fsdp")
    blocks = gradients.shape[1]
    block_side = gradients.shape[3]
    slots_here = left_stats.shape[1]
    grad_local = gradients[0]
    owner_list = owners[0, :, 0]
    total_blocks = owner_list.shape[0]
    adam_dir = grad_local.astype(jnp.float32) / (jnp.sqrt(second_moment[0]) + ADAM_EPS)
    block_sq = jnp.sum(adam_dir * adam_dir, axis=(1, 2))
    global_sq = lax.psum(jnp.sum(block_sq), ("fsdp", "layer"))
    entry_count = float(total_blocks * lax.axis_size("layer") * block_side * block_side)
    clip_factor = jnp.minimum(1.0, UPDATE_RMS / jnp.sqrt(global_sq / entry_count))
    owner_hot, home_hot, slot_hot = selection_tables(
        owner_list, owner_count, blocks, slots_here, my_index
    )
    first_row = my_index * blocks
    my_owner_hot = lax.dynamic_slice_in_dim(owner_hot, first_row, blocks, 0).astype(jnp.bfloat16)
    outgoing = jnp.einsum(
        "jo,jxy->oxy", my_owner_hot, grad_local, preferred_element_type=jnp.float32
    ).astype(jnp.bfloat16)
    received = lax.all_to_all(outgoing, "fsdp", split_axis=0, concat_axis=0, tiled=True)
    pick_table = jnp.einsum("bs,bh->sh", slot_hot, home_hot).astype(jnp.bfloat16)
    gathered = jnp.einsum(
        "sh,hxy->sxy", pick_table, received, preferred_element_type=jnp.float32
    ).astype(jnp.bfloat16)
    preconditioned, new_left, new_right = owner_work(
        gathered, left_stats, right_stats, left_root, right_root
    )
    answers = jnp.einsum(
        "sh,sxy->hxy", pick_table, preconditioned, preferred_element_type=jnp.float32
    ).astype(jnp.bfloat16)
    returned = lax.all_to_all(answers, "fsdp", split_axis=0, concat_axis=0, tiled=True)
    home_blocks = jnp.einsum(
        "jo,oxy->jxy", my_owner_hot, returned, preferred_element_type=jnp.float32
    )
    pre_float = home_blocks.astype(jnp.bfloat16).astype(jnp.float32)
    graft_ratio = jnp.sqrt(block_sq / float(block_side * block_side)) / jnp.sqrt(
        jnp.sum(pre_float * pre_float, axis=(1, 2)) / float(block_side * block_side) + NORM_FLOOR
    )
    update = (pre_float * (graft_ratio * clip_factor)[:, None, None]).astype(jnp.bfloat16)
    return (update[None], new_left, new_right)


TAIL = 16


def kernel_params(mebibytes):
    return pltpu.CompilerParams(vmem_limit_bytes=mebibytes * 2**20)


def home_slot(named, target):
    block = jnp.int32(0)
    for j in range(1, len(named)):
        block = jnp.where(named[j] == target, jnp.int32(j), block)
    return block


def route_kernel(order, owners_hbm, me_ref, grad_hbm, *refs):
    outs, (owners_ref, held, owner_sem, grad_sem) = refs[:-4], refs[-4:]
    count = held.shape[0]
    me = me_ref[0]
    fetch_owners = pltpu.make_async_copy(owners_hbm, owners_ref, owner_sem)
    fetch_grads = pltpu.make_async_copy(grad_hbm.at[0], held, grad_sem)
    fetch_owners.start()
    fetch_grads.start()
    fetch_owners.wait()
    named = [owners_ref[me * count + j] for j in range(count)]
    blocks = [home_slot(named, me ^ m) for m in order]
    fetch_grads.wait()
    for block, out in zip(blocks, outs):
        out[...] = held[block]


def route(order, owner_list, me, gradients):
    count, side = gradients.shape[1], gradients.shape[3]
    hbm = pl.BlockSpec(memory_space=pltpu.HBM)
    piece = jax.ShapeDtypeStruct((side, side), gradients.dtype)
    return pl.pallas_call(
        functools.partial(route_kernel, order),
        in_specs=[hbm, pl.BlockSpec(memory_space=pltpu.SMEM), hbm],
        out_specs=[pl.BlockSpec(memory_space=pltpu.VMEM)] * count,
        scratch_shapes=[
            pltpu.SMEM(owner_list.shape, jnp.int32),
            pltpu.VMEM((count, side, side), gradients.dtype),
            pltpu.SemaphoreType.DMA,
            pltpu.SemaphoreType.DMA,
        ],
        out_shape=[piece] * count,
        compiler_params=kernel_params(6),
        cost_estimate=pl.CostEstimate(
            flops=0, bytes_accessed=4 * count * side * side, transcendentals=0
        ),
    )(
        pltpu.with_memory_space_constraint(owner_list, pltpu.HBM),
        me,
        pltpu.with_memory_space_constraint(gradients, pltpu.HBM),
    )


def adam_kernel(grad_hbm, moment_hbm, out_ref, total_ref, grads, moments, sems):
    count, side = grads.shape[0], grads.shape[2]
    lanes = out_ref.shape[1]
    copies = []
    for b in range(count):
        pair = (
            pltpu.make_async_copy(grad_hbm.at[0, b], grads.at[b], sems.at[0, b]),
            pltpu.make_async_copy(moment_hbm.at[0, b], moments.at[b], sems.at[1, b]),
        )
        for copy in pair:
            copy.start()
        copies.append(pair)
    total = jnp.zeros((1, lanes), jnp.float32)
    for b, pair in enumerate(copies):
        for copy in pair:
            copy.wait()
        adam_dir = grads[b].astype(jnp.float32) / (jnp.sqrt(moments[b]) + ADAM_EPS)
        squares = jnp.sum(adam_dir * adam_dir, axis=0, keepdims=True)
        row = squares[:, 0:lanes]
        for k in range(lanes, side, lanes):
            row = row + squares[:, k : k + lanes]
        out_ref[b : b + 1, :] = row
        total = total + row
    total_ref[...] = jnp.broadcast_to(total, total_ref.shape)


def adam_squares(gradients, second_moment):
    count, side = gradients.shape[1], gradients.shape[3]
    hbm = pl.BlockSpec(memory_space=pltpu.HBM)
    return pl.pallas_call(
        adam_kernel,
        in_specs=[hbm, hbm],
        out_specs=[pl.BlockSpec(memory_space=pltpu.VMEM)] * 2,
        out_shape=[
            jax.ShapeDtypeStruct((count, 128), jnp.float32),
            jax.ShapeDtypeStruct((8, 128), jnp.float32),
        ],
        scratch_shapes=[
            pltpu.VMEM((count, side, side), gradients.dtype),
            pltpu.VMEM((count, side, side), second_moment.dtype),
            pltpu.SemaphoreType.DMA((2, count)),
        ],
        compiler_params=kernel_params(8),
        cost_estimate=pl.CostEstimate(
            flops=8 * count * side * side,
            bytes_accessed=6 * count * side * side,
            transcendentals=2 * count * side * side,
        ),
    )(
        pltpu.with_memory_space_constraint(gradients, pltpu.HBM),
        pltpu.with_memory_space_constraint(second_moment, pltpu.HBM),
    )


def tail_kernel(total_ref, out_ref):
    total = jnp.sum(total_ref[0:1, :], keepdims=True)
    high = total.astype(jnp.bfloat16).astype(jnp.float32)
    rest = total - high
    middle = rest.astype(jnp.bfloat16).astype(jnp.float32)
    low = rest - middle
    row = lax.broadcasted_iota(jnp.int32, out_ref.shape, 0)
    value = jnp.where(row == 0, high, jnp.where(row == 1, middle, jnp.where(row == 2, low, 0.0)))
    out_ref[...] = value.astype(jnp.bfloat16)


def sum_tail(total, side):
    return pl.pallas_call(
        tail_kernel,
        in_specs=[pl.BlockSpec(memory_space=pltpu.VMEM)],
        out_specs=pl.BlockSpec(memory_space=pltpu.VMEM),
        out_shape=jax.ShapeDtypeStruct((TAIL, side), jnp.bfloat16),
        compiler_params=kernel_params(2),
        cost_estimate=pl.CostEstimate(flops=4096, bytes_accessed=32768, transcendentals=0),
    )(total)


def precondition_kernel(m, rows, me_ref, grad_ref, left_ref, right_ref, tail_ref, out_ref):
    side = grad_ref.shape[0]
    slot = me_ref[0] ^ m
    half_done = jnp.dot(
        left_ref[0, slot], grad_ref[...], preferred_element_type=jnp.float32
    ).astype(jnp.bfloat16)
    out_ref[0:side, :] = jnp.dot(
        half_done, right_ref[0, slot], preferred_element_type=jnp.float32
    ).astype(jnp.bfloat16)
    if rows:
        out_ref[side:, :] = tail_ref[...]


def precondition(m, rows, me, block, left_root, right_root, tail):
    side = block.shape[0]
    return pl.pallas_call(
        functools.partial(precondition_kernel, m, rows),
        grid_spec=pltpu.PrefetchScalarGridSpec(
            num_scalar_prefetch=1,
            grid=(),
            in_specs=[pl.BlockSpec(memory_space=pltpu.VMEM)] * 4,
            out_specs=pl.BlockSpec(memory_space=pltpu.VMEM),
        ),
        out_shape=jax.ShapeDtypeStruct((side + rows, side), jnp.bfloat16),
        compiler_params=kernel_params(6),
        cost_estimate=pl.CostEstimate(
            flops=4 * side**3, bytes_accessed=8 * side * side, transcendentals=0
        ),
    )(me, block, left_root, right_root, tail)


def gram_kernel(order, me_ref, *refs):
    count = len(refs) - 4
    grads = refs[:count]
    left_ref, right_ref, new_left_ref, new_right_ref = refs[count:]
    step = pl.program_id(0)
    for k, m in enumerate(order):

        @pl.when(step == m)
        def _():
            block = grads[k][...]
            gram_left = lax.dot_general(
                block, block, (((1,), (1,)), ((), ())), preferred_element_type=jnp.float32
            )
            gram_right = lax.dot_general(
                block, block, (((0,), (0,)), ((), ())), preferred_element_type=jnp.float32
            )
            new_left_ref[0, 0] = DECAY_RATE * left_ref[0, 0] + (1.0 - DECAY_RATE) * gram_left
            new_right_ref[0, 0] = DECAY_RATE * right_ref[0, 0] + (1.0 - DECAY_RATE) * gram_right


def gram_update(order, me, blocks, left_stats, right_stats):
    count, side = len(blocks), blocks[0].shape[0]
    stat = pl.BlockSpec((1, 1, side, side), lambda i, me_ref: (0, me_ref[0] ^ i, 0, 0))
    whole = pl.BlockSpec(memory_space=pltpu.VMEM)
    return pl.pallas_call(
        functools.partial(gram_kernel, order),
        grid_spec=pltpu.PrefetchScalarGridSpec(
            num_scalar_prefetch=1,
            grid=(count,),
            in_specs=[whole] * count + [stat, stat],
            out_specs=[stat, stat],
        ),
        out_shape=[
            jax.ShapeDtypeStruct(left_stats.shape, left_stats.dtype),
            jax.ShapeDtypeStruct(right_stats.shape, right_stats.dtype),
        ],
        compiler_params=kernel_params(12),
        cost_estimate=pl.CostEstimate(
            flops=4 * count * side**3, bytes_accessed=18 * count * side * side, transcendentals=0
        ),
    )(me, *blocks, left_stats, right_stats)


def finish_kernel(order, entries, owners_ref, me_ref, *refs):
    count = len(order)
    pieces = refs[:count]
    squares_ref, tail_ref, out_ref, held, sums, sems = refs[count:]
    side, lanes = out_ref.shape[3], squares_ref.shape[1]
    me = me_ref[0]
    named = [owners_ref[me * count + j] for j in range(count)]
    blocks = [home_slot(named, me ^ m) for m in order]
    global_sq = jnp.zeros((1, 1), jnp.float32)
    for rows in [tail_ref[...]] + [piece[side:, :] for piece in pieces if piece.shape[0] > side]:
        terms = rows[:, 0:1].astype(jnp.float32)
        global_sq = global_sq + jnp.sum(terms, axis=0, keepdims=True)
    for k, piece in enumerate(pieces):
        pre_float = piece[0:side, :].astype(jnp.float32)
        row = jnp.sum(pre_float * pre_float, axis=0, keepdims=True)
        parts = [row[:, i : i + lanes] for i in range(0, side, lanes)]
        sums[0, k : k + 1, :] = functools.reduce(jnp.add, parts)
        sums[1, k : k + 1, :] = squares_ref[pl.ds(blocks[k], 1), :]
    area = float(side * side)
    pre_sq = jnp.sum(sums[0], axis=1, keepdims=True)
    block_sq = jnp.sum(sums[1], axis=1, keepdims=True)
    clip_factor = jnp.minimum(1.0, UPDATE_RMS / jnp.sqrt(global_sq / entries))
    graft_ratio = jnp.sqrt(block_sq / area) / jnp.sqrt(pre_sq / area + NORM_FLOOR)
    scale = graft_ratio * clip_factor
    copies = []
    for k, piece in enumerate(pieces):
        pre_float = piece[0:side, :].astype(jnp.float32)
        held[k] = (pre_float * scale[k : k + 1, :]).astype(jnp.bfloat16)
        copy = pltpu.make_async_copy(held.at[k], out_ref.at[0, blocks[k]], sems.at[k])
        copy.start()
        copies.append(copy)
    for copy in copies:
        copy.wait()


def finish(order, owner_list, me, pieces, squares, tail, entries):
    count, side = len(pieces), pieces[0].shape[1]
    return pl.pallas_call(
        functools.partial(finish_kernel, order, entries),
        grid_spec=pltpu.PrefetchScalarGridSpec(
            num_scalar_prefetch=2,
            grid=(),
            in_specs=[pl.BlockSpec(memory_space=pltpu.VMEM)] * (count + 2),
            out_specs=pl.BlockSpec(memory_space=pl.ANY),
            scratch_shapes=[
                pltpu.VMEM((count, side, side), jnp.bfloat16),
                pltpu.VMEM((2, count, squares.shape[1]), jnp.float32),
                pltpu.SemaphoreType.DMA((count,)),
            ],
        ),
        out_shape=jax.ShapeDtypeStruct((1, count, side, side), jnp.bfloat16),
        compiler_params=kernel_params(8),
        cost_estimate=pl.CostEstimate(
            flops=6 * count * side * side, bytes_accessed=4 * count * side * side, transcendentals=0
        ),
    )(owner_list, me, *pieces, squares, tail)


def doublings(size):
    return [2**k for k in range(size.bit_length() - 1)]


def per_device_exchange(
    gradients, second_moment, owners, left_stats, right_stats, left_root, right_root
):
    count = lax.axis_size("fsdp")
    layers = lax.axis_size("layer")
    side = gradients.shape[3]
    me = lax.axis_index("fsdp").astype(jnp.int32).reshape(1)
    owner_list = owners[0, :, 0]
    half = count // 2
    order = [*range(half - 1), count - 1, half - 1, *range(count - 2, half - 1, -1)]

    def swap(value, m, axis="fsdp"):
        if m == 0:
            return value
        return lax.ppermute(value, axis, [(i, i ^ m) for i in range(lax.axis_size(axis))])

    outgoing = route(order, owner_list, me, gradients)
    received = [swap(block, m) for m, block in zip(order, outgoing)]
    squares, total = adam_squares(gradients, second_moment)
    for k in doublings(layers):
        total = total + swap(total, k, "layer")
    tail = sum_tail(total, side)
    returned = []
    for m, block in zip(order, received):
        rows = TAIL if m else 0
        done = precondition(m, rows, me, block, left_root, right_root, tail)
        returned.append(swap(done, m))
    new_left, new_right = gram_update(order, me, received, left_stats, right_stats)
    entries = float(owner_list.shape[0] * layers * side * side)
    update = finish(order, owner_list, me, returned, squares, tail, entries)
    return (update, new_left, new_right)


def per_device(gradients, second_moment, owners, left_stats, right_stats, left_root, right_root):
    owner_count, blocks, slots = lax.axis_size("fsdp"), gradients.shape[1], left_stats.shape[1]
    layers = lax.axis_size("layer")
    paired = owner_count == blocks == slots
    paired = paired and owner_count & (owner_count - 1) == 0 and layers & (layers - 1) == 0
    body = per_device_exchange if paired else per_device_general
    return body(
        gradients, second_moment, owners, left_stats, right_stats, left_root, right_root
    )


def solution(mesh):
    return jax.shard_map(
        per_device,
        mesh=mesh,
        in_specs=(
            P("layer", "fsdp", None, None),
            P("layer", "fsdp", None, None),
            P("layer", None, None),
            P("layer", "fsdp", None, None),
            P("layer", "fsdp", None, None),
            P("layer", "fsdp", None, None),
            P("layer", "fsdp", None, None),
        ),
        out_specs=(
            P("layer", "fsdp", None, None),
            P("layer", "fsdp", None, None),
            P("layer", "fsdp", None, None),
        ),
        check_vma=False,
    )
```

```python
import functools

import jax
import jax.numpy as jnp
from jax import lax
from jax.experimental import pallas as pl
from jax.experimental.pallas import tpu as pltpu
from jax.sharding import PartitionSpec as P

ADAM_EPS = 1e-08
DECAY_RATE = 0.95
UPDATE_RMS = 1.0
NORM_FLOOR = 1e-06


def selection_tables(owner_list, owner_count, blocks, slots_here, my_index):
    total_blocks = owner_list.shape[0]
    owner_hot = (owner_list[:, None] == lax.iota(jnp.int32, owner_count)[None, :]).astype(
        jnp.float32
    )
    row_ids = lax.iota(jnp.int32, total_blocks)
    strict_lower = (row_ids[:, None] > row_ids[None, :]).astype(jnp.float32)
    before_all = jnp.dot(strict_lower, owner_hot, precision=lax.Precision.HIGHEST)
    slot_number = jnp.sum(before_all * owner_hot, axis=1)
    mine_mask = (owner_list == my_index).astype(jnp.float32)
    slot_hot = (slot_number[:, None] == lax.iota(jnp.float32, slots_here)[None, :]).astype(
        jnp.float32
    ) * mine_mask[:, None]
    home_hot = ((row_ids // blocks)[:, None] == lax.iota(jnp.int32, owner_count)[None, :]).astype(
        jnp.float32
    )
    return (owner_hot, home_hot, slot_hot)


def owner_work(gathered, left_stats, right_stats, left_root, right_root):
    gram_left = jnp.einsum("sij,skj->sik", gathered, gathered, preferred_element_type=jnp.float32)
    gram_right = jnp.einsum("sji,sjk->sik", gathered, gathered, preferred_element_type=jnp.float32)
    new_left = DECAY_RATE * left_stats[0] + (1.0 - DECAY_RATE) * gram_left
    new_right = DECAY_RATE * right_stats[0] + (1.0 - DECAY_RATE) * gram_right
    half_done = jnp.einsum(
        "sij,sjk->sik", left_root[0], gathered, preferred_element_type=jnp.float32
    ).astype(jnp.bfloat16)
    preconditioned = jnp.einsum(
        "sij,sjk->sik", half_done, right_root[0], preferred_element_type=jnp.float32
    ).astype(jnp.bfloat16)
    return (preconditioned, new_left[None], new_right[None])


def per_device_general(gradients, second_moment, owners, left_stats, right_stats, left_root, right_root):
    owner_count = lax.axis_size("fsdp")
    my_index = lax.axis_index("fsdp")
    blocks = gradients.shape[1]
    block_side = gradients.shape[3]
    slots_here = left_stats.shape[1]
    grad_local = gradients[0]
    owner_list = owners[0, :, 0]
    total_blocks = owner_list.shape[0]
    adam_dir = grad_local.astype(jnp.float32) / (jnp.sqrt(second_moment[0]) + ADAM_EPS)
    block_sq = jnp.sum(adam_dir * adam_dir, axis=(1, 2))
    global_sq = lax.psum(jnp.sum(block_sq), ("fsdp", "layer"))
    entry_count = float(total_blocks * lax.axis_size("layer") * block_side * block_side)
    clip_factor = jnp.minimum(1.0, UPDATE_RMS / jnp.sqrt(global_sq / entry_count))
    owner_hot, home_hot, slot_hot = selection_tables(
        owner_list, owner_count, blocks, slots_here, my_index
    )
    first_row = my_index * blocks
    my_owner_hot = lax.dynamic_slice_in_dim(owner_hot, first_row, blocks, 0).astype(jnp.bfloat16)
    outgoing = jnp.einsum(
        "jo,jxy->oxy", my_owner_hot, grad_local, preferred_element_type=jnp.float32
    ).astype(jnp.bfloat16)
    received = lax.all_to_all(outgoing, "fsdp", split_axis=0, concat_axis=0, tiled=True)
    pick_table = jnp.einsum("bs,bh->sh", slot_hot, home_hot).astype(jnp.bfloat16)
    gathered = jnp.einsum(
        "sh,hxy->sxy", pick_table, received, preferred_element_type=jnp.float32
    ).astype(jnp.bfloat16)
    preconditioned, new_left, new_right = owner_work(
        gathered, left_stats, right_stats, left_root, right_root
    )
    answers = jnp.einsum(
        "sh,sxy->hxy", pick_table, preconditioned, preferred_element_type=jnp.float32
    ).astype(jnp.bfloat16)
    returned = lax.all_to_all(answers, "fsdp", split_axis=0, concat_axis=0, tiled=True)
    home_blocks = jnp.einsum(
        "jo,oxy->jxy", my_owner_hot, returned, preferred_element_type=jnp.float32
    )
    pre_float = home_blocks.astype(jnp.bfloat16).astype(jnp.float32)
    graft_ratio = jnp.sqrt(block_sq / float(block_side * block_side)) / jnp.sqrt(
        jnp.sum(pre_float * pre_float, axis=(1, 2)) / float(block_side * block_side) + NORM_FLOOR
    )
    update = (pre_float * (graft_ratio * clip_factor)[:, None, None]).astype(jnp.bfloat16)
    return (update[None], new_left, new_right)


TAIL = 16


def kernel_params(mebibytes):
    return pltpu.CompilerParams(vmem_limit_bytes=mebibytes * 2**20)


def home_slot(named, target):
    block = jnp.int32(0)
    for j in range(1, len(named)):
        block = jnp.where(named[j] == target, jnp.int32(j), block)
    return block


def route_kernel(order, owners_hbm, me_ref, grad_hbm, *refs):
    outs, (owners_ref, held, owner_sem, grad_sem) = refs[:-4], refs[-4:]
    count = held.shape[0]
    me = me_ref[0]
    fetch_owners = pltpu.make_async_copy(owners_hbm, owners_ref, owner_sem)
    fetch_grads = pltpu.make_async_copy(grad_hbm.at[0], held, grad_sem)
    fetch_owners.start()
    fetch_grads.start()
    fetch_owners.wait()
    named = [owners_ref[me * count + j] for j in range(count)]
    blocks = [home_slot(named, me ^ m) for m in order]
    fetch_grads.wait()
    for block, out in zip(blocks, outs):
        out[...] = held[block]


def route(order, owner_list, me, gradients):
    count, side = gradients.shape[1], gradients.shape[3]
    hbm = pl.BlockSpec(memory_space=pltpu.HBM)
    piece = jax.ShapeDtypeStruct((side, side), gradients.dtype)
    return pl.pallas_call(
        functools.partial(route_kernel, order),
        in_specs=[hbm, pl.BlockSpec(memory_space=pltpu.SMEM), hbm],
        out_specs=[pl.BlockSpec(memory_space=pltpu.VMEM)] * count,
        scratch_shapes=[
            pltpu.SMEM(owner_list.shape, jnp.int32),
            pltpu.VMEM((count, side, side), gradients.dtype),
            pltpu.SemaphoreType.DMA,
            pltpu.SemaphoreType.DMA,
        ],
        out_shape=[piece] * count,
        compiler_params=kernel_params(6),
        cost_estimate=pl.CostEstimate(
            flops=0, bytes_accessed=4 * count * side * side, transcendentals=0
        ),
    )(
        pltpu.with_memory_space_constraint(owner_list, pltpu.HBM),
        me,
        pltpu.with_memory_space_constraint(gradients, pltpu.HBM),
    )


def adam_kernel(grad_hbm, moment_hbm, out_ref, total_ref, grads, moments, sems):
    count, side = grads.shape[0], grads.shape[2]
    lanes = out_ref.shape[1]
    copies = []
    for b in range(count):
        pair = (
            pltpu.make_async_copy(grad_hbm.at[0, b], grads.at[b], sems.at[0, b]),
            pltpu.make_async_copy(moment_hbm.at[0, b], moments.at[b], sems.at[1, b]),
        )
        for copy in pair:
            copy.start()
        copies.append(pair)
    total = jnp.zeros((1, lanes), jnp.float32)
    for b, pair in enumerate(copies):
        for copy in pair:
            copy.wait()
        adam_dir = grads[b].astype(jnp.float32) / (jnp.sqrt(moments[b]) + ADAM_EPS)
        squares = jnp.sum(adam_dir * adam_dir, axis=0, keepdims=True)
        row = squares[:, 0:lanes]
        for k in range(lanes, side, lanes):
            row = row + squares[:, k : k + lanes]
        out_ref[b : b + 1, :] = row
        total = total + row
    total_ref[...] = jnp.broadcast_to(total, total_ref.shape)


def adam_squares(gradients, second_moment):
    count, side = gradients.shape[1], gradients.shape[3]
    hbm = pl.BlockSpec(memory_space=pltpu.HBM)
    return pl.pallas_call(
        adam_kernel,
        in_specs=[hbm, hbm],
        out_specs=[pl.BlockSpec(memory_space=pltpu.VMEM)] * 2,
        out_shape=[
            jax.ShapeDtypeStruct((count, 128), jnp.float32),
            jax.ShapeDtypeStruct((8, 128), jnp.float32),
        ],
        scratch_shapes=[
            pltpu.VMEM((count, side, side), gradients.dtype),
            pltpu.VMEM((count, side, side), second_moment.dtype),
            pltpu.SemaphoreType.DMA((2, count)),
        ],
        compiler_params=kernel_params(8),
        cost_estimate=pl.CostEstimate(
            flops=8 * count * side * side,
            bytes_accessed=6 * count * side * side,
            transcendentals=2 * count * side * side,
        ),
    )(
        pltpu.with_memory_space_constraint(gradients, pltpu.HBM),
        pltpu.with_memory_space_constraint(second_moment, pltpu.HBM),
    )


def tail_kernel(total_ref, out_ref):
    total = jnp.sum(total_ref[0:1, :], keepdims=True)
    high = total.astype(jnp.bfloat16).astype(jnp.float32)
    rest = total - high
    middle = rest.astype(jnp.bfloat16).astype(jnp.float32)
    low = rest - middle
    row = lax.broadcasted_iota(jnp.int32, out_ref.shape, 0)
    value = jnp.where(row == 0, high, jnp.where(row == 1, middle, jnp.where(row == 2, low, 0.0)))
    out_ref[...] = value.astype(jnp.bfloat16)


def sum_tail(total, side):
    return pl.pallas_call(
        tail_kernel,
        in_specs=[pl.BlockSpec(memory_space=pltpu.VMEM)],
        out_specs=pl.BlockSpec(memory_space=pltpu.VMEM),
        out_shape=jax.ShapeDtypeStruct((TAIL, side), jnp.bfloat16),
        compiler_params=kernel_params(2),
        cost_estimate=pl.CostEstimate(flops=4096, bytes_accessed=32768, transcendentals=0),
    )(total)


def precondition_kernel(m, rows, me_ref, grad_ref, left_ref, right_ref, tail_ref, out_ref):
    side = grad_ref.shape[0]
    slot = me_ref[0] ^ m
    half_done = jnp.dot(
        left_ref[0, slot], grad_ref[...], preferred_element_type=jnp.float32
    ).astype(jnp.bfloat16)
    out_ref[0:side, :] = jnp.dot(
        half_done, right_ref[0, slot], preferred_element_type=jnp.float32
    ).astype(jnp.bfloat16)
    if rows:
        out_ref[side:, :] = tail_ref[...]


def precondition(m, rows, me, block, left_root, right_root, tail):
    side = block.shape[0]
    return pl.pallas_call(
        functools.partial(precondition_kernel, m, rows),
        grid_spec=pltpu.PrefetchScalarGridSpec(
            num_scalar_prefetch=1,
            grid=(),
            in_specs=[pl.BlockSpec(memory_space=pltpu.VMEM)] * 4,
            out_specs=pl.BlockSpec(memory_space=pltpu.VMEM),
        ),
        out_shape=jax.ShapeDtypeStruct((side + rows, side), jnp.bfloat16),
        compiler_params=kernel_params(6),
        cost_estimate=pl.CostEstimate(
            flops=4 * side**3, bytes_accessed=8 * side * side, transcendentals=0
        ),
    )(me, block, left_root, right_root, tail)


def gram_kernel(order, me_ref, *refs):
    count = len(refs) - 4
    grads = refs[:count]
    left_ref, right_ref, new_left_ref, new_right_ref = refs[count:]
    step = pl.program_id(0)
    for k, m in enumerate(order):

        @pl.when(step == m)
        def _():
            block = grads[k][...]
            gram_left = lax.dot_general(
                block, block, (((1,), (1,)), ((), ())), preferred_element_type=jnp.float32
            )
            gram_right = lax.dot_general(
                block, block, (((0,), (0,)), ((), ())), preferred_element_type=jnp.float32
            )
            new_left_ref[0, 0] = DECAY_RATE * left_ref[0, 0] + (1.0 - DECAY_RATE) * gram_left
            new_right_ref[0, 0] = DECAY_RATE * right_ref[0, 0] + (1.0 - DECAY_RATE) * gram_right


def gram_update(order, me, blocks, left_stats, right_stats):
    count, side = len(blocks), blocks[0].shape[0]
    stat = pl.BlockSpec((1, 1, side, side), lambda i, me_ref: (0, me_ref[0] ^ i, 0, 0))
    whole = pl.BlockSpec(memory_space=pltpu.VMEM)
    return pl.pallas_call(
        functools.partial(gram_kernel, order),
        grid_spec=pltpu.PrefetchScalarGridSpec(
            num_scalar_prefetch=1,
            grid=(count,),
            in_specs=[whole] * count + [stat, stat],
            out_specs=[stat, stat],
        ),
        out_shape=[
            jax.ShapeDtypeStruct(left_stats.shape, left_stats.dtype),
            jax.ShapeDtypeStruct(right_stats.shape, right_stats.dtype),
        ],
        compiler_params=kernel_params(12),
        cost_estimate=pl.CostEstimate(
            flops=4 * count * side**3, bytes_accessed=18 * count * side * side, transcendentals=0
        ),
    )(me, *blocks, left_stats, right_stats)


def finish_kernel(order, entries, owners_ref, me_ref, *refs):
    count = len(order)
    pieces = refs[:count]
    squares_ref, tail_ref, out_ref, held, sums, sems = refs[count:]
    side, lanes = out_ref.shape[3], squares_ref.shape[1]
    me = me_ref[0]
    named = [owners_ref[me * count + j] for j in range(count)]
    blocks = [home_slot(named, me ^ m) for m in order]
    global_sq = jnp.zeros((1, 1), jnp.float32)
    for rows in [tail_ref[...]] + [piece[side:, :] for piece in pieces if piece.shape[0] > side]:
        terms = rows[:, 0:1].astype(jnp.float32)
        global_sq = global_sq + jnp.sum(terms, axis=0, keepdims=True)
    for k, piece in enumerate(pieces):
        pre_float = piece[0:side, :].astype(jnp.float32)
        row = jnp.sum(pre_float * pre_float, axis=0, keepdims=True)
        parts = [row[:, i : i + lanes] for i in range(0, side, lanes)]
        sums[0, k : k + 1, :] = functools.reduce(jnp.add, parts)
        sums[1, k : k + 1, :] = squares_ref[pl.ds(blocks[k], 1), :]
    area = float(side * side)
    pre_sq = jnp.sum(sums[0], axis=1, keepdims=True)
    block_sq = jnp.sum(sums[1], axis=1, keepdims=True)
    clip_factor = jnp.minimum(1.0, UPDATE_RMS / jnp.sqrt(global_sq / entries))
    graft_ratio = jnp.sqrt(block_sq / area) / jnp.sqrt(pre_sq / area + NORM_FLOOR)
    scale = graft_ratio * clip_factor
    copies = []
    for k, piece in enumerate(pieces):
        pre_float = piece[0:side, :].astype(jnp.float32)
        held[k] = (pre_float * scale[k : k + 1, :]).astype(jnp.bfloat16)
        copy = pltpu.make_async_copy(held.at[k], out_ref.at[0, blocks[k]], sems.at[k])
        copy.start()
        copies.append(copy)
    for copy in copies:
        copy.wait()


def finish(order, owner_list, me, pieces, squares, tail, entries):
    count, side = len(pieces), pieces[0].shape[1]
    return pl.pallas_call(
        functools.partial(finish_kernel, order, entries),
        grid_spec=pltpu.PrefetchScalarGridSpec(
            num_scalar_prefetch=2,
            grid=(),
            in_specs=[pl.BlockSpec(memory_space=pltpu.VMEM)] * (count + 2),
            out_specs=pl.BlockSpec(memory_space=pl.ANY),
            scratch_shapes=[
                pltpu.VMEM((count, side, side), jnp.bfloat16),
                pltpu.VMEM((2, count, squares.shape[1]), jnp.float32),
                pltpu.SemaphoreType.DMA((count,)),
            ],
        ),
        out_shape=jax.ShapeDtypeStruct((1, count, side, side), jnp.bfloat16),
        compiler_params=kernel_params(8),
        cost_estimate=pl.CostEstimate(
            flops=6 * count * side * side, bytes_accessed=4 * count * side * side, transcendentals=0
        ),
    )(owner_list, me, *pieces, squares, tail)


def doublings(size):
    return [2**k for k in range(size.bit_length() - 1)]


def per_device_exchange(
    gradients, second_moment, owners, left_stats, right_stats, left_root, right_root
):
    count = lax.axis_size("fsdp")
    layers = lax.axis_size("layer")
    side = gradients.shape[3]
    me = lax.axis_index("fsdp").astype(jnp.int32).reshape(1)
    owner_list = owners[0, :, 0]
    half = count // 2
    order = [0, 1, 2, half + 1, 3, half, count - 1, count - 2] if count == 8 else list(range(count))

    def swap(value, m, axis="fsdp"):
        if m == 0:
            return value
        return lax.ppermute(value, axis, [(i, i ^ m) for i in range(lax.axis_size(axis))])

    outgoing = route(order, owner_list, me, gradients)
    received = [swap(block, m) for m, block in zip(order, outgoing)]
    squares, total = adam_squares(gradients, second_moment)
    for k in doublings(layers):
        total = total + swap(total, k, "layer")
    tail = sum_tail(total, side)
    returned = []
    for m, block in zip(order, received):
        rows = TAIL if m else 0
        done = precondition(m, rows, me, block, left_root, right_root, tail)
        returned.append(swap(done, m))
    new_left, new_right = gram_update(order, me, received, left_stats, right_stats)
    entries = float(owner_list.shape[0] * layers * side * side)
    update = finish(order, owner_list, me, returned, squares, tail, entries)
    return (update, new_left, new_right)


def per_device(gradients, second_moment, owners, left_stats, right_stats, left_root, right_root):
    owner_count, blocks, slots = lax.axis_size("fsdp"), gradients.shape[1], left_stats.shape[1]
    layers = lax.axis_size("layer")
    paired = owner_count == blocks == slots
    paired = paired and owner_count & (owner_count - 1) == 0 and layers & (layers - 1) == 0
    body = per_device_exchange if paired else per_device_general
    return body(
        gradients, second_moment, owners, left_stats, right_stats, left_root, right_root
    )


def solution(mesh):
    return jax.shard_map(
        per_device,
        mesh=mesh,
        in_specs=(
            P("layer", "fsdp", None, None),
            P("layer", "fsdp", None, None),
            P("layer", None, None),
            P("layer", "fsdp", None, None),
            P("layer", "fsdp", None, None),
            P("layer", "fsdp", None, None),
            P("layer", "fsdp", None, None),
        ),
        out_specs=(
            P("layer", "fsdp", None, None),
            P("layer", "fsdp", None, None),
            P("layer", "fsdp", None, None),
        ),
        check_vma=False,
    )
```

```python
import functools

import jax
import jax.numpy as jnp
from jax import lax
from jax.experimental import pallas as pl
from jax.experimental.pallas import tpu as pltpu
from jax.sharding import PartitionSpec as P

ADAM_EPS = 1e-08
DECAY_RATE = 0.95
UPDATE_RMS = 1.0
NORM_FLOOR = 1e-06


def selection_tables(owner_list, owner_count, blocks, slots_here, my_index):
    total_blocks = owner_list.shape[0]
    owner_hot = (owner_list[:, None] == lax.iota(jnp.int32, owner_count)[None, :]).astype(
        jnp.float32
    )
    row_ids = lax.iota(jnp.int32, total_blocks)
    strict_lower = (row_ids[:, None] > row_ids[None, :]).astype(jnp.float32)
    before_all = jnp.dot(strict_lower, owner_hot, precision=lax.Precision.HIGHEST)
    slot_number = jnp.sum(before_all * owner_hot, axis=1)
    mine_mask = (owner_list == my_index).astype(jnp.float32)
    slot_hot = (slot_number[:, None] == lax.iota(jnp.float32, slots_here)[None, :]).astype(
        jnp.float32
    ) * mine_mask[:, None]
    home_hot = ((row_ids // blocks)[:, None] == lax.iota(jnp.int32, owner_count)[None, :]).astype(
        jnp.float32
    )
    return (owner_hot, home_hot, slot_hot)


def owner_work(gathered, left_stats, right_stats, left_root, right_root):
    gram_left = jnp.einsum("sij,skj->sik", gathered, gathered, preferred_element_type=jnp.float32)
    gram_right = jnp.einsum("sji,sjk->sik", gathered, gathered, preferred_element_type=jnp.float32)
    new_left = DECAY_RATE * left_stats[0] + (1.0 - DECAY_RATE) * gram_left
    new_right = DECAY_RATE * right_stats[0] + (1.0 - DECAY_RATE) * gram_right
    half_done = jnp.einsum(
        "sij,sjk->sik", left_root[0], gathered, preferred_element_type=jnp.float32
    ).astype(jnp.bfloat16)
    preconditioned = jnp.einsum(
        "sij,sjk->sik", half_done, right_root[0], preferred_element_type=jnp.float32
    ).astype(jnp.bfloat16)
    return (preconditioned, new_left[None], new_right[None])


def per_device_general(gradients, second_moment, owners, left_stats, right_stats, left_root, right_root):
    owner_count = lax.axis_size("fsdp")
    my_index = lax.axis_index("fsdp")
    blocks = gradients.shape[1]
    block_side = gradients.shape[3]
    slots_here = left_stats.shape[1]
    grad_local = gradients[0]
    owner_list = owners[0, :, 0]
    total_blocks = owner_list.shape[0]
    adam_dir = grad_local.astype(jnp.float32) / (jnp.sqrt(second_moment[0]) + ADAM_EPS)
    block_sq = jnp.sum(adam_dir * adam_dir, axis=(1, 2))
    global_sq = lax.psum(jnp.sum(block_sq), ("fsdp", "layer"))
    entry_count = float(total_blocks * lax.axis_size("layer") * block_side * block_side)
    clip_factor = jnp.minimum(1.0, UPDATE_RMS / jnp.sqrt(global_sq / entry_count))
    owner_hot, home_hot, slot_hot = selection_tables(
        owner_list, owner_count, blocks, slots_here, my_index
    )
    first_row = my_index * blocks
    my_owner_hot = lax.dynamic_slice_in_dim(owner_hot, first_row, blocks, 0).astype(jnp.bfloat16)
    outgoing = jnp.einsum(
        "jo,jxy->oxy", my_owner_hot, grad_local, preferred_element_type=jnp.float32
    ).astype(jnp.bfloat16)
    received = lax.all_to_all(outgoing, "fsdp", split_axis=0, concat_axis=0, tiled=True)
    pick_table = jnp.einsum("bs,bh->sh", slot_hot, home_hot).astype(jnp.bfloat16)
    gathered = jnp.einsum(
        "sh,hxy->sxy", pick_table, received, preferred_element_type=jnp.float32
    ).astype(jnp.bfloat16)
    preconditioned, new_left, new_right = owner_work(
        gathered, left_stats, right_stats, left_root, right_root
    )
    answers = jnp.einsum(
        "sh,sxy->hxy", pick_table, preconditioned, preferred_element_type=jnp.float32
    ).astype(jnp.bfloat16)
    returned = lax.all_to_all(answers, "fsdp", split_axis=0, concat_axis=0, tiled=True)
    home_blocks = jnp.einsum(
        "jo,oxy->jxy", my_owner_hot, returned, preferred_element_type=jnp.float32
    )
    pre_float = home_blocks.astype(jnp.bfloat16).astype(jnp.float32)
    graft_ratio = jnp.sqrt(block_sq / float(block_side * block_side)) / jnp.sqrt(
        jnp.sum(pre_float * pre_float, axis=(1, 2)) / float(block_side * block_side) + NORM_FLOOR
    )
    update = (pre_float * (graft_ratio * clip_factor)[:, None, None]).astype(jnp.bfloat16)
    return (update[None], new_left, new_right)


TAIL = 16


def kernel_params(mebibytes):
    return pltpu.CompilerParams(vmem_limit_bytes=mebibytes * 2**20)


def home_slot(named, target):
    block = jnp.int32(0)
    for j in range(1, len(named)):
        block = jnp.where(named[j] == target, jnp.int32(j), block)
    return block


def route_kernel(order, owners_hbm, me_ref, grad_hbm, *refs):
    outs, (owners_ref, held, owner_sem, grad_sem) = refs[:-4], refs[-4:]
    count = held.shape[0]
    me = me_ref[0]
    fetch_owners = pltpu.make_async_copy(owners_hbm, owners_ref, owner_sem)
    fetch_grads = pltpu.make_async_copy(grad_hbm.at[0], held, grad_sem)
    fetch_owners.start()
    fetch_grads.start()
    fetch_owners.wait()
    named = [owners_ref[me * count + j] for j in range(count)]
    blocks = [home_slot(named, me ^ m) for m in order]
    fetch_grads.wait()
    for block, out in zip(blocks, outs):
        out[...] = held[block]


def route(order, owner_list, me, gradients):
    count, side = gradients.shape[1], gradients.shape[3]
    hbm = pl.BlockSpec(memory_space=pltpu.HBM)
    piece = jax.ShapeDtypeStruct((side, side), gradients.dtype)
    return pl.pallas_call(
        functools.partial(route_kernel, order),
        in_specs=[hbm, pl.BlockSpec(memory_space=pltpu.SMEM), hbm],
        out_specs=[pl.BlockSpec(memory_space=pltpu.VMEM)] * count,
        scratch_shapes=[
            pltpu.SMEM(owner_list.shape, jnp.int32),
            pltpu.VMEM((count, side, side), gradients.dtype),
            pltpu.SemaphoreType.DMA,
            pltpu.SemaphoreType.DMA,
        ],
        out_shape=[piece] * count,
        compiler_params=kernel_params(6),
        cost_estimate=pl.CostEstimate(
            flops=0, bytes_accessed=4 * count * side * side, transcendentals=0
        ),
    )(
        pltpu.with_memory_space_constraint(owner_list, pltpu.HBM),
        me,
        pltpu.with_memory_space_constraint(gradients, pltpu.HBM),
    )


def adam_kernel(grad_hbm, moment_hbm, out_ref, total_ref, grads, moments, sems):
    count, side = grads.shape[0], grads.shape[2]
    lanes = out_ref.shape[1]
    copies = []
    for b in range(count):
        pair = (
            pltpu.make_async_copy(grad_hbm.at[0, b], grads.at[b], sems.at[0, b]),
            pltpu.make_async_copy(moment_hbm.at[0, b], moments.at[b], sems.at[1, b]),
        )
        for copy in pair:
            copy.start()
        copies.append(pair)
    total = jnp.zeros((1, lanes), jnp.float32)
    for b, pair in enumerate(copies):
        for copy in pair:
            copy.wait()
        adam_dir = grads[b].astype(jnp.float32) / (jnp.sqrt(moments[b]) + ADAM_EPS)
        squares = jnp.sum(adam_dir * adam_dir, axis=0, keepdims=True)
        row = squares[:, 0:lanes]
        for k in range(lanes, side, lanes):
            row = row + squares[:, k : k + lanes]
        out_ref[b : b + 1, :] = row
        total = total + row
    total_ref[...] = jnp.broadcast_to(total, total_ref.shape)


def adam_squares(gradients, second_moment):
    count, side = gradients.shape[1], gradients.shape[3]
    hbm = pl.BlockSpec(memory_space=pltpu.HBM)
    return pl.pallas_call(
        adam_kernel,
        in_specs=[hbm, hbm],
        out_specs=[pl.BlockSpec(memory_space=pltpu.VMEM)] * 2,
        out_shape=[
            jax.ShapeDtypeStruct((count, 128), jnp.float32),
            jax.ShapeDtypeStruct((8, 128), jnp.float32),
        ],
        scratch_shapes=[
            pltpu.VMEM((count, side, side), gradients.dtype),
            pltpu.VMEM((count, side, side), second_moment.dtype),
            pltpu.SemaphoreType.DMA((2, count)),
        ],
        compiler_params=kernel_params(8),
        cost_estimate=pl.CostEstimate(
            flops=8 * count * side * side,
            bytes_accessed=6 * count * side * side,
            transcendentals=2 * count * side * side,
        ),
    )(
        pltpu.with_memory_space_constraint(gradients, pltpu.HBM),
        pltpu.with_memory_space_constraint(second_moment, pltpu.HBM),
    )


def tail_kernel(total_ref, out_ref):
    total = jnp.sum(total_ref[0:1, :], keepdims=True)
    high = total.astype(jnp.bfloat16).astype(jnp.float32)
    rest = total - high
    middle = rest.astype(jnp.bfloat16).astype(jnp.float32)
    low = rest - middle
    row = lax.broadcasted_iota(jnp.int32, out_ref.shape, 0)
    value = jnp.where(row == 0, high, jnp.where(row == 1, middle, jnp.where(row == 2, low, 0.0)))
    out_ref[...] = value.astype(jnp.bfloat16)


def sum_tail(total, side):
    return pl.pallas_call(
        tail_kernel,
        in_specs=[pl.BlockSpec(memory_space=pltpu.VMEM)],
        out_specs=pl.BlockSpec(memory_space=pltpu.VMEM),
        out_shape=jax.ShapeDtypeStruct((TAIL, side), jnp.bfloat16),
        compiler_params=kernel_params(2),
        cost_estimate=pl.CostEstimate(flops=4096, bytes_accessed=32768, transcendentals=0),
    )(total)


def precondition_kernel(m, rows, me_ref, grad_ref, left_ref, right_ref, tail_ref, *refs):
    out_ref = refs[-1]
    side = grad_ref.shape[0]
    slot = me_ref[0] ^ m
    half_done = jnp.dot(
        left_ref[0, slot], grad_ref[...], preferred_element_type=jnp.float32
    ).astype(jnp.bfloat16)
    out_ref[0:side, :] = jnp.dot(
        half_done, right_ref[0, slot], preferred_element_type=jnp.float32
    ).astype(jnp.bfloat16)
    if rows:
        out_ref[side:, :] = tail_ref[...]


def precondition(m, rows, me, block, left_root, right_root, tail, after):
    side = block.shape[0]
    return pl.pallas_call(
        functools.partial(precondition_kernel, m, rows),
        grid_spec=pltpu.PrefetchScalarGridSpec(
            num_scalar_prefetch=1,
            grid=(),
            in_specs=[pl.BlockSpec(memory_space=pltpu.VMEM)] * 4
            + [pl.BlockSpec(memory_space=pl.ANY)] * len(after),
            out_specs=pl.BlockSpec(memory_space=pltpu.VMEM),
        ),
        out_shape=jax.ShapeDtypeStruct((side + rows, side), jnp.bfloat16),
        compiler_params=kernel_params(6),
        cost_estimate=pl.CostEstimate(
            flops=4 * side**3, bytes_accessed=8 * side * side, transcendentals=0
        ),
    )(me, block, left_root, right_root, tail, *after)


def gram_kernel(order, me_ref, *refs):
    count = len(refs) - 4
    grads = refs[:count]
    left_ref, right_ref, new_left_ref, new_right_ref = refs[count:]
    step = pl.program_id(0)
    for k, m in enumerate(order):

        @pl.when(step == m)
        def _():
            block = grads[k][...]
            gram_left = lax.dot_general(
                block, block, (((1,), (1,)), ((), ())), preferred_element_type=jnp.float32
            )
            gram_right = lax.dot_general(
                block, block, (((0,), (0,)), ((), ())), preferred_element_type=jnp.float32
            )
            new_left_ref[0, 0] = DECAY_RATE * left_ref[0, 0] + (1.0 - DECAY_RATE) * gram_left
            new_right_ref[0, 0] = DECAY_RATE * right_ref[0, 0] + (1.0 - DECAY_RATE) * gram_right


def gram_update(order, me, blocks, left_stats, right_stats):
    count, side = len(blocks), blocks[0].shape[0]
    stat = pl.BlockSpec((1, 1, side, side), lambda i, me_ref: (0, me_ref[0] ^ i, 0, 0))
    whole = pl.BlockSpec(memory_space=pltpu.VMEM)
    return pl.pallas_call(
        functools.partial(gram_kernel, order),
        grid_spec=pltpu.PrefetchScalarGridSpec(
            num_scalar_prefetch=1,
            grid=(count,),
            in_specs=[whole] * count + [stat, stat],
            out_specs=[stat, stat],
        ),
        out_shape=[
            jax.ShapeDtypeStruct(left_stats.shape, left_stats.dtype),
            jax.ShapeDtypeStruct(right_stats.shape, right_stats.dtype),
        ],
        compiler_params=kernel_params(12),
        cost_estimate=pl.CostEstimate(
            flops=4 * count * side**3, bytes_accessed=18 * count * side * side, transcendentals=0
        ),
    )(me, *blocks, left_stats, right_stats)


def finish_kernel(order, entries, owners_ref, me_ref, *refs):
    count = len(order)
    pieces = refs[:count]
    squares_ref, tail_ref, out_ref, held, sums, sems = refs[count:]
    side, lanes = out_ref.shape[3], squares_ref.shape[1]
    me = me_ref[0]
    named = [owners_ref[me * count + j] for j in range(count)]
    blocks = [home_slot(named, me ^ m) for m in order]
    global_sq = jnp.zeros((1, 1), jnp.float32)
    for rows in [tail_ref[...]] + [piece[side:, :] for piece in pieces if piece.shape[0] > side]:
        terms = rows[:, 0:1].astype(jnp.float32)
        global_sq = global_sq + jnp.sum(terms, axis=0, keepdims=True)
    for k, piece in enumerate(pieces):
        pre_float = piece[0:side, :].astype(jnp.float32)
        row = jnp.sum(pre_float * pre_float, axis=0, keepdims=True)
        parts = [row[:, i : i + lanes] for i in range(0, side, lanes)]
        sums[0, k : k + 1, :] = functools.reduce(jnp.add, parts)
        sums[1, k : k + 1, :] = squares_ref[pl.ds(blocks[k], 1), :]
    area = float(side * side)
    pre_sq = jnp.sum(sums[0], axis=1, keepdims=True)
    block_sq = jnp.sum(sums[1], axis=1, keepdims=True)
    clip_factor = jnp.minimum(1.0, UPDATE_RMS / jnp.sqrt(global_sq / entries))
    graft_ratio = jnp.sqrt(block_sq / area) / jnp.sqrt(pre_sq / area + NORM_FLOOR)
    scale = graft_ratio * clip_factor
    copies = []
    for k, piece in enumerate(pieces):
        pre_float = piece[0:side, :].astype(jnp.float32)
        held[k] = (pre_float * scale[k : k + 1, :]).astype(jnp.bfloat16)
        copy = pltpu.make_async_copy(held.at[k], out_ref.at[0, blocks[k]], sems.at[k])
        copy.start()
        copies.append(copy)
    for copy in copies:
        copy.wait()


def finish(order, owner_list, me, pieces, squares, tail, entries):
    count, side = len(pieces), pieces[0].shape[1]
    return pl.pallas_call(
        functools.partial(finish_kernel, order, entries),
        grid_spec=pltpu.PrefetchScalarGridSpec(
            num_scalar_prefetch=2,
            grid=(),
            in_specs=[pl.BlockSpec(memory_space=pltpu.VMEM)] * (count + 2),
            out_specs=pl.BlockSpec(memory_space=pl.ANY),
            scratch_shapes=[
                pltpu.VMEM((count, side, side), jnp.bfloat16),
                pltpu.VMEM((2, count, squares.shape[1]), jnp.float32),
                pltpu.SemaphoreType.DMA((count,)),
            ],
        ),
        out_shape=jax.ShapeDtypeStruct((1, count, side, side), jnp.bfloat16),
        compiler_params=kernel_params(8),
        cost_estimate=pl.CostEstimate(
            flops=6 * count * side * side, bytes_accessed=4 * count * side * side, transcendentals=0
        ),
    )(owner_list, me, *pieces, squares, tail)


def doublings(size):
    return [2**k for k in range(size.bit_length() - 1)]


def per_device_exchange(
    gradients, second_moment, owners, left_stats, right_stats, left_root, right_root
):
    count = lax.axis_size("fsdp")
    layers = lax.axis_size("layer")
    side = gradients.shape[3]
    me = lax.axis_index("fsdp").astype(jnp.int32).reshape(1)
    owner_list = owners[0, :, 0]
    half = count // 2
    order = [*range(half - 1), half, half - 1, *range(half + 1, count)]

    def swap(value, m, axis="fsdp"):
        if m == 0:
            return value
        return lax.ppermute(value, axis, [(i, i ^ m) for i in range(lax.axis_size(axis))])

    outgoing = route(order, owner_list, me, gradients)
    received = [swap(block, m) for m, block in zip(order, outgoing)]
    squares, total = adam_squares(gradients, second_moment)
    for k in doublings(layers):
        total = total + swap(total, k, "layer")
    tail = sum_tail(total, side)
    landed = dict(zip(order, received))
    returned = []
    for m, block in zip(order, received):
        rows = TAIL if m else 0
        after = [landed[half + 1]] if m == count - 2 else []
        done = precondition(m, rows, me, block, left_root, right_root, tail, after)
        returned.append(swap(done, m))
    new_left, new_right = gram_update(order, me, received, left_stats, right_stats)
    entries = float(owner_list.shape[0] * layers * side * side)
    update = finish(order, owner_list, me, returned, squares, tail, entries)
    return (update, new_left, new_right)


def per_device(gradients, second_moment, owners, left_stats, right_stats, left_root, right_root):
    owner_count, blocks, slots = lax.axis_size("fsdp"), gradients.shape[1], left_stats.shape[1]
    layers = lax.axis_size("layer")
    paired = owner_count == blocks == slots
    paired = paired and owner_count & (owner_count - 1) == 0 and layers & (layers - 1) == 0
    body = per_device_exchange if paired else per_device_general
    return body(
        gradients, second_moment, owners, left_stats, right_stats, left_root, right_root
    )


def solution(mesh):
    return jax.shard_map(
        per_device,
        mesh=mesh,
        in_specs=(
            P("layer", "fsdp", None, None),
            P("layer", "fsdp", None, None),
            P("layer", None, None),
            P("layer", "fsdp", None, None),
            P("layer", "fsdp", None, None),
            P("layer", "fsdp", None, None),
            P("layer", "fsdp", None, None),
        ),
        out_specs=(
            P("layer", "fsdp", None, None),
            P("layer", "fsdp", None, None),
            P("layer", "fsdp", None, None),
        ),
        check_vma=False,
    )
```

```python
import functools

import jax
import jax.numpy as jnp
from jax import lax
from jax.experimental import pallas as pl
from jax.experimental.pallas import tpu as pltpu
from jax.sharding import PartitionSpec as P

ADAM_EPS = 1e-08
DECAY_RATE = 0.95
UPDATE_RMS = 1.0
NORM_FLOOR = 1e-06


def selection_tables(owner_list, owner_count, blocks, slots_here, my_index):
    total_blocks = owner_list.shape[0]
    owner_hot = (owner_list[:, None] == lax.iota(jnp.int32, owner_count)[None, :]).astype(
        jnp.float32
    )
    row_ids = lax.iota(jnp.int32, total_blocks)
    strict_lower = (row_ids[:, None] > row_ids[None, :]).astype(jnp.float32)
    before_all = jnp.dot(strict_lower, owner_hot, precision=lax.Precision.HIGHEST)
    slot_number = jnp.sum(before_all * owner_hot, axis=1)
    mine_mask = (owner_list == my_index).astype(jnp.float32)
    slot_hot = (slot_number[:, None] == lax.iota(jnp.float32, slots_here)[None, :]).astype(
        jnp.float32
    ) * mine_mask[:, None]
    home_hot = ((row_ids // blocks)[:, None] == lax.iota(jnp.int32, owner_count)[None, :]).astype(
        jnp.float32
    )
    return (owner_hot, home_hot, slot_hot)


def owner_work(gathered, left_stats, right_stats, left_root, right_root):
    gram_left = jnp.einsum("sij,skj->sik", gathered, gathered, preferred_element_type=jnp.float32)
    gram_right = jnp.einsum("sji,sjk->sik", gathered, gathered, preferred_element_type=jnp.float32)
    new_left = DECAY_RATE * left_stats[0] + (1.0 - DECAY_RATE) * gram_left
    new_right = DECAY_RATE * right_stats[0] + (1.0 - DECAY_RATE) * gram_right
    half_done = jnp.einsum(
        "sij,sjk->sik", left_root[0], gathered, preferred_element_type=jnp.float32
    ).astype(jnp.bfloat16)
    preconditioned = jnp.einsum(
        "sij,sjk->sik", half_done, right_root[0], preferred_element_type=jnp.float32
    ).astype(jnp.bfloat16)
    return (preconditioned, new_left[None], new_right[None])


def per_device_general(gradients, second_moment, owners, left_stats, right_stats, left_root, right_root):
    owner_count = lax.axis_size("fsdp")
    my_index = lax.axis_index("fsdp")
    blocks = gradients.shape[1]
    block_side = gradients.shape[3]
    slots_here = left_stats.shape[1]
    grad_local = gradients[0]
    owner_list = owners[0, :, 0]
    total_blocks = owner_list.shape[0]
    adam_dir = grad_local.astype(jnp.float32) / (jnp.sqrt(second_moment[0]) + ADAM_EPS)
    block_sq = jnp.sum(adam_dir * adam_dir, axis=(1, 2))
    global_sq = lax.psum(jnp.sum(block_sq), ("fsdp", "layer"))
    entry_count = float(total_blocks * lax.axis_size("layer") * block_side * block_side)
    clip_factor = jnp.minimum(1.0, UPDATE_RMS / jnp.sqrt(global_sq / entry_count))
    owner_hot, home_hot, slot_hot = selection_tables(
        owner_list, owner_count, blocks, slots_here, my_index
    )
    first_row = my_index * blocks
    my_owner_hot = lax.dynamic_slice_in_dim(owner_hot, first_row, blocks, 0).astype(jnp.bfloat16)
    outgoing = jnp.einsum(
        "jo,jxy->oxy", my_owner_hot, grad_local, preferred_element_type=jnp.float32
    ).astype(jnp.bfloat16)
    received = lax.all_to_all(outgoing, "fsdp", split_axis=0, concat_axis=0, tiled=True)
    pick_table = jnp.einsum("bs,bh->sh", slot_hot, home_hot).astype(jnp.bfloat16)
    gathered = jnp.einsum(
        "sh,hxy->sxy", pick_table, received, preferred_element_type=jnp.float32
    ).astype(jnp.bfloat16)
    preconditioned, new_left, new_right = owner_work(
        gathered, left_stats, right_stats, left_root, right_root
    )
    answers = jnp.einsum(
        "sh,sxy->hxy", pick_table, preconditioned, preferred_element_type=jnp.float32
    ).astype(jnp.bfloat16)
    returned = lax.all_to_all(answers, "fsdp", split_axis=0, concat_axis=0, tiled=True)
    home_blocks = jnp.einsum(
        "jo,oxy->jxy", my_owner_hot, returned, preferred_element_type=jnp.float32
    )
    pre_float = home_blocks.astype(jnp.bfloat16).astype(jnp.float32)
    graft_ratio = jnp.sqrt(block_sq / float(block_side * block_side)) / jnp.sqrt(
        jnp.sum(pre_float * pre_float, axis=(1, 2)) / float(block_side * block_side) + NORM_FLOOR
    )
    update = (pre_float * (graft_ratio * clip_factor)[:, None, None]).astype(jnp.bfloat16)
    return (update[None], new_left, new_right)


TAIL = 16


def kernel_params(mebibytes):
    return pltpu.CompilerParams(vmem_limit_bytes=mebibytes * 2**20)


def partner_tables(count):
    half = count // 2
    even = [0, 1, 2, half, 3, *range(half + 1, count)]
    odd = [{1: half, half: 1}.get(m, m) for m in even]
    return even, odd


def partner(me, step, count):
    even, odd = partner_tables(count)
    return jnp.where(me & 2 == 2, jnp.int32(odd[step]), jnp.int32(even[step]))


def home_slot(named, target):
    block = jnp.int32(0)
    for j in range(1, len(named)):
        block = jnp.where(named[j] == target, jnp.int32(j), block)
    return block


def route_kernel(owners_hbm, me_ref, grad_hbm, *refs):
    outs, (owners_ref, held, owner_sem, grad_sem) = refs[:-4], refs[-4:]
    count = held.shape[0]
    me = me_ref[0]
    fetch_owners = pltpu.make_async_copy(owners_hbm, owners_ref, owner_sem)
    fetch_grads = pltpu.make_async_copy(grad_hbm.at[0], held, grad_sem)
    fetch_owners.start()
    fetch_grads.start()
    fetch_owners.wait()
    named = [owners_ref[me * count + j] for j in range(count)]
    blocks = [home_slot(named, me ^ partner(me, step, count)) for step in range(count)]
    fetch_grads.wait()
    for block, out in zip(blocks, outs):
        out[...] = held[block]


def route(owner_list, me, gradients):
    count, side = gradients.shape[1], gradients.shape[3]
    hbm = pl.BlockSpec(memory_space=pltpu.HBM)
    piece = jax.ShapeDtypeStruct((side, side), gradients.dtype)
    return pl.pallas_call(
        route_kernel,
        in_specs=[hbm, pl.BlockSpec(memory_space=pltpu.SMEM), hbm],
        out_specs=[pl.BlockSpec(memory_space=pltpu.VMEM)] * count,
        scratch_shapes=[
            pltpu.SMEM(owner_list.shape, jnp.int32),
            pltpu.VMEM((count, side, side), gradients.dtype),
            pltpu.SemaphoreType.DMA,
            pltpu.SemaphoreType.DMA,
        ],
        out_shape=[piece] * count,
        compiler_params=kernel_params(6),
        cost_estimate=pl.CostEstimate(
            flops=0, bytes_accessed=4 * count * side * side, transcendentals=0
        ),
    )(
        pltpu.with_memory_space_constraint(owner_list, pltpu.HBM),
        me,
        pltpu.with_memory_space_constraint(gradients, pltpu.HBM),
    )


def adam_kernel(grad_hbm, moment_hbm, out_ref, total_ref, grads, moments, sems):
    count, side = grads.shape[0], grads.shape[2]
    lanes = out_ref.shape[1]
    copies = []
    for b in range(count):
        pair = (
            pltpu.make_async_copy(grad_hbm.at[0, b], grads.at[b], sems.at[0, b]),
            pltpu.make_async_copy(moment_hbm.at[0, b], moments.at[b], sems.at[1, b]),
        )
        for copy in pair:
            copy.start()
        copies.append(pair)
    total = jnp.zeros((1, lanes), jnp.float32)
    for b, pair in enumerate(copies):
        for copy in pair:
            copy.wait()
        adam_dir = grads[b].astype(jnp.float32) / (jnp.sqrt(moments[b]) + ADAM_EPS)
        squares = jnp.sum(adam_dir * adam_dir, axis=0, keepdims=True)
        row = squares[:, 0:lanes]
        for k in range(lanes, side, lanes):
            row = row + squares[:, k : k + lanes]
        out_ref[b : b + 1, :] = row
        total = total + row
    total_ref[...] = jnp.broadcast_to(total, total_ref.shape)


def adam_squares(gradients, second_moment):
    count, side = gradients.shape[1], gradients.shape[3]
    hbm = pl.BlockSpec(memory_space=pltpu.HBM)
    return pl.pallas_call(
        adam_kernel,
        in_specs=[hbm, hbm],
        out_specs=[pl.BlockSpec(memory_space=pltpu.VMEM)] * 2,
        out_shape=[
            jax.ShapeDtypeStruct((count, 128), jnp.float32),
            jax.ShapeDtypeStruct((8, 128), jnp.float32),
        ],
        scratch_shapes=[
            pltpu.VMEM((count, side, side), gradients.dtype),
            pltpu.VMEM((count, side, side), second_moment.dtype),
            pltpu.SemaphoreType.DMA((2, count)),
        ],
        compiler_params=kernel_params(8),
        cost_estimate=pl.CostEstimate(
            flops=8 * count * side * side,
            bytes_accessed=6 * count * side * side,
            transcendentals=2 * count * side * side,
        ),
    )(
        pltpu.with_memory_space_constraint(gradients, pltpu.HBM),
        pltpu.with_memory_space_constraint(second_moment, pltpu.HBM),
    )


def tail_kernel(total_ref, out_ref):
    total = jnp.sum(total_ref[0:1, :], keepdims=True)
    high = total.astype(jnp.bfloat16).astype(jnp.float32)
    rest = total - high
    middle = rest.astype(jnp.bfloat16).astype(jnp.float32)
    low = rest - middle
    row = lax.broadcasted_iota(jnp.int32, out_ref.shape, 0)
    value = jnp.where(row == 0, high, jnp.where(row == 1, middle, jnp.where(row == 2, low, 0.0)))
    out_ref[...] = value.astype(jnp.bfloat16)


def sum_tail(total, side):
    return pl.pallas_call(
        tail_kernel,
        in_specs=[pl.BlockSpec(memory_space=pltpu.VMEM)],
        out_specs=pl.BlockSpec(memory_space=pltpu.VMEM),
        out_shape=jax.ShapeDtypeStruct((TAIL, side), jnp.bfloat16),
        compiler_params=kernel_params(2),
        cost_estimate=pl.CostEstimate(flops=4096, bytes_accessed=32768, transcendentals=0),
    )(total)


def precondition_kernel(step, me_ref, grad_ref, left_ref, right_ref, tail_ref, out_ref):
    side = grad_ref.shape[0]
    me = me_ref[0]
    slot = me ^ partner(me, step, left_ref.shape[1])
    half_done = jnp.dot(
        left_ref[0, slot], grad_ref[...], preferred_element_type=jnp.float32
    ).astype(jnp.bfloat16)
    out_ref[0:side, :] = jnp.dot(
        half_done, right_ref[0, slot], preferred_element_type=jnp.float32
    ).astype(jnp.bfloat16)
    if step:
        out_ref[side:, :] = tail_ref[...]


def precondition(step, me, block, left_root, right_root, tail):
    side = block.shape[0]
    return pl.pallas_call(
        functools.partial(precondition_kernel, step),
        grid_spec=pltpu.PrefetchScalarGridSpec(
            num_scalar_prefetch=1,
            grid=(),
            in_specs=[pl.BlockSpec(memory_space=pltpu.VMEM)] * 4,
            out_specs=pl.BlockSpec(memory_space=pltpu.VMEM),
        ),
        out_shape=jax.ShapeDtypeStruct((side + (TAIL if step else 0), side), jnp.bfloat16),
        compiler_params=kernel_params(6),
        cost_estimate=pl.CostEstimate(
            flops=4 * side**3, bytes_accessed=8 * side * side, transcendentals=0
        ),
    )(me, block, left_root, right_root, tail)


def gram_kernel(me_ref, *refs):
    count = len(refs) - 4
    grads = refs[:count]
    left_ref, right_ref, new_left_ref, new_right_ref = refs[count:]
    step = pl.program_id(0)
    for k in range(count):

        @pl.when(step == k)
        def _():
            block = grads[k][...]
            gram_left = lax.dot_general(
                block, block, (((1,), (1,)), ((), ())), preferred_element_type=jnp.float32
            )
            gram_right = lax.dot_general(
                block, block, (((0,), (0,)), ((), ())), preferred_element_type=jnp.float32
            )
            new_left_ref[0, 0] = DECAY_RATE * left_ref[0, 0] + (1.0 - DECAY_RATE) * gram_left
            new_right_ref[0, 0] = DECAY_RATE * right_ref[0, 0] + (1.0 - DECAY_RATE) * gram_right


def gram_update(me, blocks, left_stats, right_stats):
    count, side = len(blocks), blocks[0].shape[0]

    def slot(i, me_ref):
        me = me_ref[0]
        m = jnp.int32(0)
        for step in range(1, count):
            m = jnp.where(i == step, partner(me, step, count), m)
        return (0, me ^ m, 0, 0)

    stat = pl.BlockSpec((1, 1, side, side), slot)
    whole = pl.BlockSpec(memory_space=pltpu.VMEM)
    return pl.pallas_call(
        gram_kernel,
        grid_spec=pltpu.PrefetchScalarGridSpec(
            num_scalar_prefetch=1,
            grid=(count,),
            in_specs=[whole] * count + [stat, stat],
            out_specs=[stat, stat],
        ),
        out_shape=[
            jax.ShapeDtypeStruct(left_stats.shape, left_stats.dtype),
            jax.ShapeDtypeStruct(right_stats.shape, right_stats.dtype),
        ],
        compiler_params=kernel_params(12),
        cost_estimate=pl.CostEstimate(
            flops=4 * count * side**3, bytes_accessed=18 * count * side * side, transcendentals=0
        ),
    )(me, *blocks, left_stats, right_stats)


def finish_kernel(entries, owners_ref, me_ref, *refs):
    count = len(refs) - 6
    pieces = refs[:count]
    squares_ref, tail_ref, out_ref, held, sums, sems = refs[count:]
    side, lanes = out_ref.shape[3], squares_ref.shape[1]
    me = me_ref[0]
    named = [owners_ref[me * count + j] for j in range(count)]
    blocks = [home_slot(named, me ^ partner(me, step, count)) for step in range(count)]
    global_sq = jnp.zeros((1, 1), jnp.float32)
    for rows in [tail_ref[...]] + [piece[side:, :] for piece in pieces if piece.shape[0] > side]:
        terms = rows[:, 0:1].astype(jnp.float32)
        global_sq = global_sq + jnp.sum(terms, axis=0, keepdims=True)
    for k, piece in enumerate(pieces):
        pre_float = piece[0:side, :].astype(jnp.float32)
        row = jnp.sum(pre_float * pre_float, axis=0, keepdims=True)
        parts = [row[:, i : i + lanes] for i in range(0, side, lanes)]
        sums[0, k : k + 1, :] = functools.reduce(jnp.add, parts)
        sums[1, k : k + 1, :] = squares_ref[pl.ds(blocks[k], 1), :]
    area = float(side * side)
    pre_sq = jnp.sum(sums[0], axis=1, keepdims=True)
    block_sq = jnp.sum(sums[1], axis=1, keepdims=True)
    clip_factor = jnp.minimum(1.0, UPDATE_RMS / jnp.sqrt(global_sq / entries))
    graft_ratio = jnp.sqrt(block_sq / area) / jnp.sqrt(pre_sq / area + NORM_FLOOR)
    scale = graft_ratio * clip_factor
    copies = []
    for k, piece in enumerate(pieces):
        pre_float = piece[0:side, :].astype(jnp.float32)
        held[k] = (pre_float * scale[k : k + 1, :]).astype(jnp.bfloat16)
        copy = pltpu.make_async_copy(held.at[k], out_ref.at[0, blocks[k]], sems.at[k])
        copy.start()
        copies.append(copy)
    for copy in copies:
        copy.wait()


def finish(owner_list, me, pieces, squares, tail, entries):
    count, side = len(pieces), pieces[0].shape[1]
    return pl.pallas_call(
        functools.partial(finish_kernel, entries),
        grid_spec=pltpu.PrefetchScalarGridSpec(
            num_scalar_prefetch=2,
            grid=(),
            in_specs=[pl.BlockSpec(memory_space=pltpu.VMEM)] * (count + 2),
            out_specs=pl.BlockSpec(memory_space=pl.ANY),
            scratch_shapes=[
                pltpu.VMEM((count, side, side), jnp.bfloat16),
                pltpu.VMEM((2, count, squares.shape[1]), jnp.float32),
                pltpu.SemaphoreType.DMA((count,)),
            ],
        ),
        out_shape=jax.ShapeDtypeStruct((1, count, side, side), jnp.bfloat16),
        compiler_params=kernel_params(8),
        cost_estimate=pl.CostEstimate(
            flops=6 * count * side * side, bytes_accessed=4 * count * side * side, transcendentals=0
        ),
    )(owner_list, me, *pieces, squares, tail)


def doublings(size):
    return [2**k for k in range(size.bit_length() - 1)]


def per_device_exchange(
    gradients, second_moment, owners, left_stats, right_stats, left_root, right_root
):
    count, layers = lax.axis_size("fsdp"), lax.axis_size("layer")
    side = gradients.shape[3]
    me = lax.axis_index("fsdp").astype(jnp.int32).reshape(1)
    owner_list = owners[0, :, 0]
    tables = partner_tables(count)

    def swap(value, step):
        if step == 0:
            return value
        return lax.ppermute(value, "fsdp", [(i, i ^ tables[i // 2 % 2][step]) for i in range(count)])

    outgoing = route(owner_list, me, gradients)
    received = [swap(block, step) for step, block in enumerate(outgoing)]
    squares, total = adam_squares(gradients, second_moment)
    for k in doublings(layers):
        total = total + lax.ppermute(total, "layer", [(i, i ^ k) for i in range(layers)])
    tail = sum_tail(total, side)
    returned = []
    for step, block in enumerate(received):
        done = precondition(step, me, block, left_root, right_root, tail)
        returned.append(swap(done, step))
    new_left, new_right = gram_update(me, received, left_stats, right_stats)
    entries = float(owner_list.shape[0] * layers * side * side)
    update = finish(owner_list, me, returned, squares, tail, entries)
    return (update, new_left, new_right)


def per_device(gradients, second_moment, owners, left_stats, right_stats, left_root, right_root):
    owner_count, blocks, slots = lax.axis_size("fsdp"), gradients.shape[1], left_stats.shape[1]
    layers = lax.axis_size("layer")
    paired = owner_count == blocks == slots and owner_count >= 8
    paired = paired and owner_count & (owner_count - 1) == 0 and layers & (layers - 1) == 0
    body = per_device_exchange if paired else per_device_general
    return body(
        gradients, second_moment, owners, left_stats, right_stats, left_root, right_root
    )


def solution(mesh):
    return jax.shard_map(
        per_device,
        mesh=mesh,
        in_specs=(
            P("layer", "fsdp", None, None),
            P("layer", "fsdp", None, None),
            P("layer", None, None),
            P("layer", "fsdp", None, None),
            P("layer", "fsdp", None, None),
            P("layer", "fsdp", None, None),
            P("layer", "fsdp", None, None),
        ),
        out_specs=(
            P("layer", "fsdp", None, None),
            P("layer", "fsdp", None, None),
            P("layer", "fsdp", None, None),
        ),
        check_vma=False,
    )
```

```python
import functools

import jax
import jax.numpy as jnp
from jax import lax
from jax.experimental import pallas as pl
from jax.experimental.pallas import tpu as pltpu
from jax.sharding import PartitionSpec as P

ADAM_EPS = 1e-08
DECAY_RATE = 0.95
UPDATE_RMS = 1.0
NORM_FLOOR = 1e-06


def selection_tables(owner_list, owner_count, blocks, slots_here, my_index):
    total_blocks = owner_list.shape[0]
    owner_hot = (owner_list[:, None] == lax.iota(jnp.int32, owner_count)[None, :]).astype(
        jnp.float32
    )
    row_ids = lax.iota(jnp.int32, total_blocks)
    strict_lower = (row_ids[:, None] > row_ids[None, :]).astype(jnp.float32)
    before_all = jnp.dot(strict_lower, owner_hot, precision=lax.Precision.HIGHEST)
    slot_number = jnp.sum(before_all * owner_hot, axis=1)
    mine_mask = (owner_list == my_index).astype(jnp.float32)
    slot_hot = (slot_number[:, None] == lax.iota(jnp.float32, slots_here)[None, :]).astype(
        jnp.float32
    ) * mine_mask[:, None]
    home_hot = ((row_ids // blocks)[:, None] == lax.iota(jnp.int32, owner_count)[None, :]).astype(
        jnp.float32
    )
    return (owner_hot, home_hot, slot_hot)


def owner_work(gathered, left_stats, right_stats, left_root, right_root):
    gram_left = jnp.einsum("sij,skj->sik", gathered, gathered, preferred_element_type=jnp.float32)
    gram_right = jnp.einsum("sji,sjk->sik", gathered, gathered, preferred_element_type=jnp.float32)
    new_left = DECAY_RATE * left_stats[0] + (1.0 - DECAY_RATE) * gram_left
    new_right = DECAY_RATE * right_stats[0] + (1.0 - DECAY_RATE) * gram_right
    half_done = jnp.einsum(
        "sij,sjk->sik", left_root[0], gathered, preferred_element_type=jnp.float32
    ).astype(jnp.bfloat16)
    preconditioned = jnp.einsum(
        "sij,sjk->sik", half_done, right_root[0], preferred_element_type=jnp.float32
    ).astype(jnp.bfloat16)
    return (preconditioned, new_left[None], new_right[None])


def per_device_general(gradients, second_moment, owners, left_stats, right_stats, left_root, right_root):
    owner_count = lax.axis_size("fsdp")
    my_index = lax.axis_index("fsdp")
    blocks = gradients.shape[1]
    block_side = gradients.shape[3]
    slots_here = left_stats.shape[1]
    grad_local = gradients[0]
    owner_list = owners[0, :, 0]
    total_blocks = owner_list.shape[0]
    adam_dir = grad_local.astype(jnp.float32) / (jnp.sqrt(second_moment[0]) + ADAM_EPS)
    block_sq = jnp.sum(adam_dir * adam_dir, axis=(1, 2))
    global_sq = lax.psum(jnp.sum(block_sq), ("fsdp", "layer"))
    entry_count = float(total_blocks * lax.axis_size("layer") * block_side * block_side)
    clip_factor = jnp.minimum(1.0, UPDATE_RMS / jnp.sqrt(global_sq / entry_count))
    owner_hot, home_hot, slot_hot = selection_tables(
        owner_list, owner_count, blocks, slots_here, my_index
    )
    first_row = my_index * blocks
    my_owner_hot = lax.dynamic_slice_in_dim(owner_hot, first_row, blocks, 0).astype(jnp.bfloat16)
    outgoing = jnp.einsum(
        "jo,jxy->oxy", my_owner_hot, grad_local, preferred_element_type=jnp.float32
    ).astype(jnp.bfloat16)
    received = lax.all_to_all(outgoing, "fsdp", split_axis=0, concat_axis=0, tiled=True)
    pick_table = jnp.einsum("bs,bh->sh", slot_hot, home_hot).astype(jnp.bfloat16)
    gathered = jnp.einsum(
        "sh,hxy->sxy", pick_table, received, preferred_element_type=jnp.float32
    ).astype(jnp.bfloat16)
    preconditioned, new_left, new_right = owner_work(
        gathered, left_stats, right_stats, left_root, right_root
    )
    answers = jnp.einsum(
        "sh,sxy->hxy", pick_table, preconditioned, preferred_element_type=jnp.float32
    ).astype(jnp.bfloat16)
    returned = lax.all_to_all(answers, "fsdp", split_axis=0, concat_axis=0, tiled=True)
    home_blocks = jnp.einsum(
        "jo,oxy->jxy", my_owner_hot, returned, preferred_element_type=jnp.float32
    )
    pre_float = home_blocks.astype(jnp.bfloat16).astype(jnp.float32)
    graft_ratio = jnp.sqrt(block_sq / float(block_side * block_side)) / jnp.sqrt(
        jnp.sum(pre_float * pre_float, axis=(1, 2)) / float(block_side * block_side) + NORM_FLOOR
    )
    update = (pre_float * (graft_ratio * clip_factor)[:, None, None]).astype(jnp.bfloat16)
    return (update[None], new_left, new_right)


TAIL = 16


def kernel_params(mebibytes):
    return pltpu.CompilerParams(vmem_limit_bytes=mebibytes * 2**20)


def partner_tables(count):
    half = count // 2
    even = [*range(half - 1), half, half - 1, *range(half + 1, count)]
    odd = [{1: half, half: 1}.get(m, m) for m in even]
    return even, odd


def fsdp_index(who, layers):
    return lax.shift_right_logical(who, jnp.int32(layers.bit_length() - 1))


def partner(who, step, count):
    even, odd = partner_tables(count)
    return jnp.where(who & 1 == 1, jnp.int32(odd[step]), jnp.int32(even[step]))


def home_slot(named, target):
    block = jnp.int32(0)
    for j in range(1, len(named)):
        block = jnp.where(named[j] == target, jnp.int32(j), block)
    return block


def route_kernel(layers, owners_hbm, who_ref, grad_hbm, *refs):
    outs, (owners_ref, held, owner_sem, grad_sem) = refs[:-4], refs[-4:]
    count = held.shape[0]
    who = who_ref[0]
    me = fsdp_index(who, layers)
    fetch_owners = pltpu.make_async_copy(owners_hbm, owners_ref, owner_sem)
    fetch_grads = pltpu.make_async_copy(grad_hbm.at[0], held, grad_sem)
    fetch_owners.start()
    fetch_grads.start()
    fetch_owners.wait()
    named = [owners_ref[me * count + j] for j in range(count)]
    blocks = [home_slot(named, me ^ partner(who, step, count)) for step in range(count)]
    fetch_grads.wait()
    for block, out in zip(blocks, outs):
        out[...] = held[block]


def route(layers, owner_list, who, gradients):
    count, side = gradients.shape[1], gradients.shape[3]
    hbm = pl.BlockSpec(memory_space=pltpu.HBM)
    piece = jax.ShapeDtypeStruct((side, side), gradients.dtype)
    return pl.pallas_call(
        functools.partial(route_kernel, layers),
        in_specs=[hbm, pl.BlockSpec(memory_space=pltpu.SMEM), hbm],
        out_specs=[pl.BlockSpec(memory_space=pltpu.VMEM)] * count,
        scratch_shapes=[
            pltpu.SMEM(owner_list.shape, jnp.int32),
            pltpu.VMEM((count, side, side), gradients.dtype),
            pltpu.SemaphoreType.DMA,
            pltpu.SemaphoreType.DMA,
        ],
        out_shape=[piece] * count,
        compiler_params=kernel_params(6),
        cost_estimate=pl.CostEstimate(
            flops=0, bytes_accessed=4 * count * side * side, transcendentals=0
        ),
    )(
        pltpu.with_memory_space_constraint(owner_list, pltpu.HBM),
        who,
        pltpu.with_memory_space_constraint(gradients, pltpu.HBM),
    )


def adam_kernel(grad_hbm, moment_hbm, out_ref, total_ref, grads, moments, sems):
    count, side = grads.shape[0], grads.shape[2]
    lanes = out_ref.shape[1]
    copies = []
    for b in range(count):
        pair = (
            pltpu.make_async_copy(grad_hbm.at[0, b], grads.at[b], sems.at[0, b]),
            pltpu.make_async_copy(moment_hbm.at[0, b], moments.at[b], sems.at[1, b]),
        )
        for copy in pair:
            copy.start()
        copies.append(pair)
    total = jnp.zeros((1, lanes), jnp.float32)
    for b, pair in enumerate(copies):
        for copy in pair:
            copy.wait()
        adam_dir = grads[b].astype(jnp.float32) / (jnp.sqrt(moments[b]) + ADAM_EPS)
        squares = jnp.sum(adam_dir * adam_dir, axis=0, keepdims=True)
        row = squares[:, 0:lanes]
        for k in range(lanes, side, lanes):
            row = row + squares[:, k : k + lanes]
        out_ref[b : b + 1, :] = row
        total = total + row
    total_ref[...] = jnp.broadcast_to(total, total_ref.shape)


def adam_squares(gradients, second_moment):
    count, side = gradients.shape[1], gradients.shape[3]
    hbm = pl.BlockSpec(memory_space=pltpu.HBM)
    return pl.pallas_call(
        adam_kernel,
        in_specs=[hbm, hbm],
        out_specs=[pl.BlockSpec(memory_space=pltpu.VMEM)] * 2,
        out_shape=[
            jax.ShapeDtypeStruct((count, 128), jnp.float32),
            jax.ShapeDtypeStruct((8, 128), jnp.float32),
        ],
        scratch_shapes=[
            pltpu.VMEM((count, side, side), gradients.dtype),
            pltpu.VMEM((count, side, side), second_moment.dtype),
            pltpu.SemaphoreType.DMA((2, count)),
        ],
        compiler_params=kernel_params(8),
        cost_estimate=pl.CostEstimate(
            flops=8 * count * side * side,
            bytes_accessed=6 * count * side * side,
            transcendentals=2 * count * side * side,
        ),
    )(
        pltpu.with_memory_space_constraint(gradients, pltpu.HBM),
        pltpu.with_memory_space_constraint(second_moment, pltpu.HBM),
    )


def tail_kernel(total_ref, out_ref):
    total = jnp.sum(total_ref[0:1, :], keepdims=True)
    high = total.astype(jnp.bfloat16).astype(jnp.float32)
    rest = total - high
    middle = rest.astype(jnp.bfloat16).astype(jnp.float32)
    low = rest - middle
    row = lax.broadcasted_iota(jnp.int32, out_ref.shape, 0)
    value = jnp.where(row == 0, high, jnp.where(row == 1, middle, jnp.where(row == 2, low, 0.0)))
    out_ref[...] = value.astype(jnp.bfloat16)


def sum_tail(total, side):
    return pl.pallas_call(
        tail_kernel,
        in_specs=[pl.BlockSpec(memory_space=pltpu.VMEM)],
        out_specs=pl.BlockSpec(memory_space=pltpu.VMEM),
        out_shape=jax.ShapeDtypeStruct((TAIL, side), jnp.bfloat16),
        compiler_params=kernel_params(2),
        cost_estimate=pl.CostEstimate(flops=4096, bytes_accessed=32768, transcendentals=0),
    )(total)


def precondition_kernel(step, layers, who_ref, grad_ref, left_ref, right_ref, tail_ref, out_ref):
    side = grad_ref.shape[0]
    who = who_ref[0]
    slot = fsdp_index(who, layers) ^ partner(who, step, left_ref.shape[1])
    half_done = jnp.dot(
        left_ref[0, slot], grad_ref[...], preferred_element_type=jnp.float32
    ).astype(jnp.bfloat16)
    out_ref[0:side, :] = jnp.dot(
        half_done, right_ref[0, slot], preferred_element_type=jnp.float32
    ).astype(jnp.bfloat16)
    if step:
        out_ref[side:, :] = tail_ref[...]


def precondition(step, layers, who, block, left_root, right_root, tail):
    side = block.shape[0]
    return pl.pallas_call(
        functools.partial(precondition_kernel, step, layers),
        grid_spec=pltpu.PrefetchScalarGridSpec(
            num_scalar_prefetch=1,
            grid=(),
            in_specs=[pl.BlockSpec(memory_space=pltpu.VMEM)] * 4,
            out_specs=pl.BlockSpec(memory_space=pltpu.VMEM),
        ),
        out_shape=jax.ShapeDtypeStruct((side + (TAIL if step else 0), side), jnp.bfloat16),
        compiler_params=kernel_params(6),
        cost_estimate=pl.CostEstimate(
            flops=4 * side**3, bytes_accessed=8 * side * side, transcendentals=0
        ),
    )(who, block, left_root, right_root, tail)


def gram_kernel(who_ref, *refs):
    count = len(refs) - 4
    grads = refs[:count]
    left_ref, right_ref, new_left_ref, new_right_ref = refs[count:]
    step = pl.program_id(0)
    for k in range(count):

        @pl.when(step == k)
        def _():
            block = grads[k][...]
            gram_left = lax.dot_general(
                block, block, (((1,), (1,)), ((), ())), preferred_element_type=jnp.float32
            )
            gram_right = lax.dot_general(
                block, block, (((0,), (0,)), ((), ())), preferred_element_type=jnp.float32
            )
            new_left_ref[0, 0] = DECAY_RATE * left_ref[0, 0] + (1.0 - DECAY_RATE) * gram_left
            new_right_ref[0, 0] = DECAY_RATE * right_ref[0, 0] + (1.0 - DECAY_RATE) * gram_right


def gram_update(layers, who, blocks, left_stats, right_stats):
    count, side = len(blocks), blocks[0].shape[0]

    def slot(i, who_ref):
        who = who_ref[0]
        m = jnp.int32(0)
        for step in range(1, count):
            m = jnp.where(i == step, partner(who, step, count), m)
        return (0, fsdp_index(who, layers) ^ m, 0, 0)

    stat = pl.BlockSpec((1, 1, side, side), slot)
    whole = pl.BlockSpec(memory_space=pltpu.VMEM)
    return pl.pallas_call(
        gram_kernel,
        grid_spec=pltpu.PrefetchScalarGridSpec(
            num_scalar_prefetch=1,
            grid=(count,),
            in_specs=[whole] * count + [stat, stat],
            out_specs=[stat, stat],
        ),
        out_shape=[
            jax.ShapeDtypeStruct(left_stats.shape, left_stats.dtype),
            jax.ShapeDtypeStruct(right_stats.shape, right_stats.dtype),
        ],
        compiler_params=kernel_params(12),
        cost_estimate=pl.CostEstimate(
            flops=4 * count * side**3, bytes_accessed=18 * count * side * side, transcendentals=0
        ),
    )(who, *blocks, left_stats, right_stats)


def finish_kernel(layers, entries, owners_ref, who_ref, *refs):
    count = len(refs) - 6
    pieces = refs[:count]
    squares_ref, tail_ref, out_ref, held, sums, sems = refs[count:]
    side, lanes = out_ref.shape[3], squares_ref.shape[1]
    who = who_ref[0]
    me = fsdp_index(who, layers)
    named = [owners_ref[me * count + j] for j in range(count)]
    blocks = [home_slot(named, me ^ partner(who, step, count)) for step in range(count)]
    global_sq = jnp.zeros((1, 1), jnp.float32)
    for rows in [tail_ref[...]] + [piece[side:, :] for piece in pieces if piece.shape[0] > side]:
        terms = rows[:, 0:1].astype(jnp.float32)
        global_sq = global_sq + jnp.sum(terms, axis=0, keepdims=True)
    for k, piece in enumerate(pieces):
        pre_float = piece[0:side, :].astype(jnp.float32)
        row = jnp.sum(pre_float * pre_float, axis=0, keepdims=True)
        parts = [row[:, i : i + lanes] for i in range(0, side, lanes)]
        sums[0, k : k + 1, :] = functools.reduce(jnp.add, parts)
        sums[1, k : k + 1, :] = squares_ref[pl.ds(blocks[k], 1), :]
    area = float(side * side)
    pre_sq = jnp.sum(sums[0], axis=1, keepdims=True)
    block_sq = jnp.sum(sums[1], axis=1, keepdims=True)
    clip_factor = jnp.minimum(1.0, UPDATE_RMS / jnp.sqrt(global_sq / entries))
    graft_ratio = jnp.sqrt(block_sq / area) / jnp.sqrt(pre_sq / area + NORM_FLOOR)
    scale = graft_ratio * clip_factor
    copies = []
    for k, piece in enumerate(pieces):
        pre_float = piece[0:side, :].astype(jnp.float32)
        held[k] = (pre_float * scale[k : k + 1, :]).astype(jnp.bfloat16)
        copy = pltpu.make_async_copy(held.at[k], out_ref.at[0, blocks[k]], sems.at[k])
        copy.start()
        copies.append(copy)
    for copy in copies:
        copy.wait()


def finish(layers, owner_list, who, pieces, squares, tail, entries):
    count, side = len(pieces), pieces[0].shape[1]
    return pl.pallas_call(
        functools.partial(finish_kernel, layers, entries),
        grid_spec=pltpu.PrefetchScalarGridSpec(
            num_scalar_prefetch=2,
            grid=(),
            in_specs=[pl.BlockSpec(memory_space=pltpu.VMEM)] * (count + 2),
            out_specs=pl.BlockSpec(memory_space=pl.ANY),
            scratch_shapes=[
                pltpu.VMEM((count, side, side), jnp.bfloat16),
                pltpu.VMEM((2, count, squares.shape[1]), jnp.float32),
                pltpu.SemaphoreType.DMA((count,)),
            ],
        ),
        out_shape=jax.ShapeDtypeStruct((1, count, side, side), jnp.bfloat16),
        compiler_params=kernel_params(8),
        cost_estimate=pl.CostEstimate(
            flops=6 * count * side * side, bytes_accessed=4 * count * side * side, transcendentals=0
        ),
    )(owner_list, who, *pieces, squares, tail)


def doublings(size):
    return [2**k for k in range(size.bit_length() - 1)]


def per_device_exchange(
    gradients, second_moment, owners, left_stats, right_stats, left_root, right_root
):
    count, layers = lax.axis_size("fsdp"), lax.axis_size("layer")
    side = gradients.shape[3]
    who = lax.axis_index(("fsdp", "layer")).astype(jnp.int32).reshape(1)
    owner_list = owners[0, :, 0]
    tables = partner_tables(count)

    def swap(value, step):
        if step == 0:
            return value
        pairs = [
            (i * layers + k, (i ^ tables[k % 2][step]) * layers + k)
            for i in range(count)
            for k in range(layers)
        ]
        return lax.ppermute(value, ("fsdp", "layer"), pairs)

    outgoing = route(layers, owner_list, who, gradients)
    received = [swap(block, step) for step, block in enumerate(outgoing)]
    squares, total = adam_squares(gradients, second_moment)
    for k in doublings(layers):
        total = total + lax.ppermute(total, "layer", [(i, i ^ k) for i in range(layers)])
    tail = sum_tail(total, side)
    returned = []
    for step, block in enumerate(received):
        done = precondition(step, layers, who, block, left_root, right_root, tail)
        returned.append(swap(done, step))
    new_left, new_right = gram_update(layers, who, received, left_stats, right_stats)
    entries = float(owner_list.shape[0] * layers * side * side)
    update = finish(layers, owner_list, who, returned, squares, tail, entries)
    return (update, new_left, new_right)


def per_device(gradients, second_moment, owners, left_stats, right_stats, left_root, right_root):
    owner_count, blocks, slots = lax.axis_size("fsdp"), gradients.shape[1], left_stats.shape[1]
    layers = lax.axis_size("layer")
    paired = owner_count == blocks == slots and owner_count >= 8
    paired = paired and owner_count & (owner_count - 1) == 0 and layers & (layers - 1) == 0
    body = per_device_exchange if paired else per_device_general
    return body(
        gradients, second_moment, owners, left_stats, right_stats, left_root, right_root
    )


def solution(mesh):
    return jax.shard_map(
        per_device,
        mesh=mesh,
        in_specs=(
            P("layer", "fsdp", None, None),
            P("layer", "fsdp", None, None),
            P("layer", None, None),
            P("layer", "fsdp", None, None),
            P("layer", "fsdp", None, None),
            P("layer", "fsdp", None, None),
            P("layer", "fsdp", None, None),
        ),
        out_specs=(
            P("layer", "fsdp", None, None),
            P("layer", "fsdp", None, None),
            P("layer", "fsdp", None, None),
        ),
        check_vma=False,
    )
```

```python
import functools

import jax
import jax.numpy as jnp
from jax import lax
from jax.experimental import pallas as pl
from jax.experimental.pallas import tpu as pltpu
from jax.sharding import PartitionSpec as P

ADAM_EPS = 1e-08
DECAY_RATE = 0.95
UPDATE_RMS = 1.0
NORM_FLOOR = 1e-06


def selection_tables(owner_list, owner_count, blocks, slots_here, my_index):
    total_blocks = owner_list.shape[0]
    owner_hot = (owner_list[:, None] == lax.iota(jnp.int32, owner_count)[None, :]).astype(
        jnp.float32
    )
    row_ids = lax.iota(jnp.int32, total_blocks)
    strict_lower = (row_ids[:, None] > row_ids[None, :]).astype(jnp.float32)
    before_all = jnp.dot(strict_lower, owner_hot, precision=lax.Precision.HIGHEST)
    slot_number = jnp.sum(before_all * owner_hot, axis=1)
    mine_mask = (owner_list == my_index).astype(jnp.float32)
    slot_hot = (slot_number[:, None] == lax.iota(jnp.float32, slots_here)[None, :]).astype(
        jnp.float32
    ) * mine_mask[:, None]
    home_hot = ((row_ids // blocks)[:, None] == lax.iota(jnp.int32, owner_count)[None, :]).astype(
        jnp.float32
    )
    return (owner_hot, home_hot, slot_hot)


def owner_work(gathered, left_stats, right_stats, left_root, right_root):
    gram_left = jnp.einsum("sij,skj->sik", gathered, gathered, preferred_element_type=jnp.float32)
    gram_right = jnp.einsum("sji,sjk->sik", gathered, gathered, preferred_element_type=jnp.float32)
    new_left = DECAY_RATE * left_stats[0] + (1.0 - DECAY_RATE) * gram_left
    new_right = DECAY_RATE * right_stats[0] + (1.0 - DECAY_RATE) * gram_right
    half_done = jnp.einsum(
        "sij,sjk->sik", left_root[0], gathered, preferred_element_type=jnp.float32
    ).astype(jnp.bfloat16)
    preconditioned = jnp.einsum(
        "sij,sjk->sik", half_done, right_root[0], preferred_element_type=jnp.float32
    ).astype(jnp.bfloat16)
    return (preconditioned, new_left[None], new_right[None])


def per_device_general(gradients, second_moment, owners, left_stats, right_stats, left_root, right_root):
    owner_count = lax.axis_size("fsdp")
    my_index = lax.axis_index("fsdp")
    blocks = gradients.shape[1]
    block_side = gradients.shape[3]
    slots_here = left_stats.shape[1]
    grad_local = gradients[0]
    owner_list = owners[0, :, 0]
    total_blocks = owner_list.shape[0]
    adam_dir = grad_local.astype(jnp.float32) / (jnp.sqrt(second_moment[0]) + ADAM_EPS)
    block_sq = jnp.sum(adam_dir * adam_dir, axis=(1, 2))
    global_sq = lax.psum(jnp.sum(block_sq), ("fsdp", "layer"))
    entry_count = float(total_blocks * lax.axis_size("layer") * block_side * block_side)
    clip_factor = jnp.minimum(1.0, UPDATE_RMS / jnp.sqrt(global_sq / entry_count))
    owner_hot, home_hot, slot_hot = selection_tables(
        owner_list, owner_count, blocks, slots_here, my_index
    )
    first_row = my_index * blocks
    my_owner_hot = lax.dynamic_slice_in_dim(owner_hot, first_row, blocks, 0).astype(jnp.bfloat16)
    outgoing = jnp.einsum(
        "jo,jxy->oxy", my_owner_hot, grad_local, preferred_element_type=jnp.float32
    ).astype(jnp.bfloat16)
    received = lax.all_to_all(outgoing, "fsdp", split_axis=0, concat_axis=0, tiled=True)
    pick_table = jnp.einsum("bs,bh->sh", slot_hot, home_hot).astype(jnp.bfloat16)
    gathered = jnp.einsum(
        "sh,hxy->sxy", pick_table, received, preferred_element_type=jnp.float32
    ).astype(jnp.bfloat16)
    preconditioned, new_left, new_right = owner_work(
        gathered, left_stats, right_stats, left_root, right_root
    )
    answers = jnp.einsum(
        "sh,sxy->hxy", pick_table, preconditioned, preferred_element_type=jnp.float32
    ).astype(jnp.bfloat16)
    returned = lax.all_to_all(answers, "fsdp", split_axis=0, concat_axis=0, tiled=True)
    home_blocks = jnp.einsum(
        "jo,oxy->jxy", my_owner_hot, returned, preferred_element_type=jnp.float32
    )
    pre_float = home_blocks.astype(jnp.bfloat16).astype(jnp.float32)
    graft_ratio = jnp.sqrt(block_sq / float(block_side * block_side)) / jnp.sqrt(
        jnp.sum(pre_float * pre_float, axis=(1, 2)) / float(block_side * block_side) + NORM_FLOOR
    )
    update = (pre_float * (graft_ratio * clip_factor)[:, None, None]).astype(jnp.bfloat16)
    return (update[None], new_left, new_right)


TAIL = 16


def kernel_params(mebibytes):
    return pltpu.CompilerParams(vmem_limit_bytes=mebibytes * 2**20)


def home_slot(named, target):
    block = jnp.int32(0)
    for j in range(1, len(named)):
        block = jnp.where(named[j] == target, jnp.int32(j), block)
    return block


def route_kernel(order, owners_hbm, me_ref, grad_hbm, *refs):
    outs, (owners_ref, held, owner_sem, grad_sem) = refs[:-4], refs[-4:]
    count = held.shape[0]
    me = me_ref[0]
    fetch_owners = pltpu.make_async_copy(owners_hbm, owners_ref, owner_sem)
    fetch_grads = pltpu.make_async_copy(grad_hbm.at[0], held, grad_sem)
    fetch_owners.start()
    fetch_grads.start()
    fetch_owners.wait()
    named = [owners_ref[me * count + j] for j in range(count)]
    blocks = [home_slot(named, me ^ m) for m in order]
    fetch_grads.wait()
    for block, out in zip(blocks, outs):
        out[...] = held[block]


def route(order, owner_list, me, gradients):
    count, side = gradients.shape[1], gradients.shape[3]
    hbm = pl.BlockSpec(memory_space=pltpu.HBM)
    piece = jax.ShapeDtypeStruct((side, side), gradients.dtype)
    return pl.pallas_call(
        functools.partial(route_kernel, order),
        in_specs=[hbm, pl.BlockSpec(memory_space=pltpu.SMEM), hbm],
        out_specs=[pl.BlockSpec(memory_space=pltpu.VMEM)] * count,
        scratch_shapes=[
            pltpu.SMEM(owner_list.shape, jnp.int32),
            pltpu.VMEM((count, side, side), gradients.dtype),
            pltpu.SemaphoreType.DMA,
            pltpu.SemaphoreType.DMA,
        ],
        out_shape=[piece] * count,
        compiler_params=kernel_params(6),
        cost_estimate=pl.CostEstimate(
            flops=0, bytes_accessed=4 * count * side * side, transcendentals=0
        ),
    )(
        pltpu.with_memory_space_constraint(owner_list, pltpu.HBM),
        me,
        pltpu.with_memory_space_constraint(gradients, pltpu.HBM),
    )


def adam_kernel(grad_hbm, moment_hbm, out_ref, total_ref, grads, moments, sems):
    count, side = grads.shape[0], grads.shape[2]
    lanes = out_ref.shape[1]
    copies = []
    for b in range(count):
        pair = (
            pltpu.make_async_copy(grad_hbm.at[0, b], grads.at[b], sems.at[0, b]),
            pltpu.make_async_copy(moment_hbm.at[0, b], moments.at[b], sems.at[1, b]),
        )
        for copy in pair:
            copy.start()
        copies.append(pair)
    total = jnp.zeros((1, lanes), jnp.float32)
    for b, pair in enumerate(copies):
        for copy in pair:
            copy.wait()
        adam_dir = grads[b].astype(jnp.float32) / (jnp.sqrt(moments[b]) + ADAM_EPS)
        squares = jnp.sum(adam_dir * adam_dir, axis=0, keepdims=True)
        row = squares[:, 0:lanes]
        for k in range(lanes, side, lanes):
            row = row + squares[:, k : k + lanes]
        out_ref[b : b + 1, :] = row
        total = total + row
    total_ref[...] = jnp.broadcast_to(total, total_ref.shape)


def adam_squares(gradients, second_moment):
    count, side = gradients.shape[1], gradients.shape[3]
    hbm = pl.BlockSpec(memory_space=pltpu.HBM)
    return pl.pallas_call(
        adam_kernel,
        in_specs=[hbm, hbm],
        out_specs=[pl.BlockSpec(memory_space=pltpu.VMEM)] * 2,
        out_shape=[
            jax.ShapeDtypeStruct((count, 128), jnp.float32),
            jax.ShapeDtypeStruct((8, 128), jnp.float32),
        ],
        scratch_shapes=[
            pltpu.VMEM((count, side, side), gradients.dtype),
            pltpu.VMEM((count, side, side), second_moment.dtype),
            pltpu.SemaphoreType.DMA((2, count)),
        ],
        compiler_params=kernel_params(8),
        cost_estimate=pl.CostEstimate(
            flops=8 * count * side * side,
            bytes_accessed=6 * count * side * side,
            transcendentals=2 * count * side * side,
        ),
    )(
        pltpu.with_memory_space_constraint(gradients, pltpu.HBM),
        pltpu.with_memory_space_constraint(second_moment, pltpu.HBM),
    )


def split_terms(value):
    high = value.astype(jnp.bfloat16).astype(jnp.float32)
    rest = value - high
    middle = rest.astype(jnp.bfloat16).astype(jnp.float32)
    return high, middle, rest - middle


def with_rows(rest, first, terms):
    row = lax.broadcasted_iota(jnp.int32, rest.shape, 0)
    for k, term in enumerate(terms):
        rest = jnp.where(row == first + k, term, rest)
    return rest


def tail_kernel(total_ref, out_ref):
    total = jnp.sum(total_ref[0:1, :], keepdims=True)
    rows = with_rows(jnp.zeros(out_ref.shape, jnp.float32), 0, split_terms(total))
    out_ref[...] = rows.astype(jnp.bfloat16)


def sum_tail(total, side):
    return pl.pallas_call(
        tail_kernel,
        in_specs=[pl.BlockSpec(memory_space=pltpu.VMEM)],
        out_specs=pl.BlockSpec(memory_space=pltpu.VMEM),
        out_shape=jax.ShapeDtypeStruct((TAIL, side), jnp.bfloat16),
        compiler_params=kernel_params(2),
        cost_estimate=pl.CostEstimate(flops=4096, bytes_accessed=32768, transcendentals=0),
    )(total)


def precondition_kernel(m, me_ref, grad_ref, left_ref, right_ref, tail_ref, out_ref):
    side = grad_ref.shape[0]
    slot = me_ref[0] ^ m
    half_done = jnp.dot(
        left_ref[0, slot], grad_ref[...], preferred_element_type=jnp.float32
    ).astype(jnp.bfloat16)
    preconditioned = jnp.dot(
        half_done, right_ref[0, slot], preferred_element_type=jnp.float32
    ).astype(jnp.bfloat16)
    out_ref[0:side, :] = preconditioned
    pre_float = preconditioned.astype(jnp.float32)
    squares = jnp.sum(pre_float * pre_float, axis=0, keepdims=True)
    rows = with_rows(tail_ref[...].astype(jnp.float32), 3, split_terms(squares))
    out_ref[side:, :] = rows.astype(jnp.bfloat16)


def precondition(m, me, block, left_root, right_root, tail):
    side = block.shape[0]
    return pl.pallas_call(
        functools.partial(precondition_kernel, m),
        grid_spec=pltpu.PrefetchScalarGridSpec(
            num_scalar_prefetch=1,
            grid=(),
            in_specs=[pl.BlockSpec(memory_space=pltpu.VMEM)] * 4,
            out_specs=pl.BlockSpec(memory_space=pltpu.VMEM),
        ),
        out_shape=jax.ShapeDtypeStruct((side + TAIL, side), jnp.bfloat16),
        compiler_params=kernel_params(6),
        cost_estimate=pl.CostEstimate(
            flops=4 * side**3, bytes_accessed=8 * side * side, transcendentals=0
        ),
    )(me, block, left_root, right_root, tail)


def gram_kernel(order, me_ref, *refs):
    count = len(refs) - 4
    grads = refs[:count]
    left_ref, right_ref, new_left_ref, new_right_ref = refs[count:]
    step = pl.program_id(0)
    for k, m in enumerate(order):

        @pl.when(step == m)
        def _():
            block = grads[k][...]
            gram_left = lax.dot_general(
                block, block, (((1,), (1,)), ((), ())), preferred_element_type=jnp.float32
            )
            gram_right = lax.dot_general(
                block, block, (((0,), (0,)), ((), ())), preferred_element_type=jnp.float32
            )
            new_left_ref[0, 0] = DECAY_RATE * left_ref[0, 0] + (1.0 - DECAY_RATE) * gram_left
            new_right_ref[0, 0] = DECAY_RATE * right_ref[0, 0] + (1.0 - DECAY_RATE) * gram_right


def gram_update(order, me, blocks, left_stats, right_stats):
    count, side = len(blocks), blocks[0].shape[0]
    stat = pl.BlockSpec((1, 1, side, side), lambda i, me_ref: (0, me_ref[0] ^ i, 0, 0))
    whole = pl.BlockSpec(memory_space=pltpu.VMEM)
    return pl.pallas_call(
        functools.partial(gram_kernel, order),
        grid_spec=pltpu.PrefetchScalarGridSpec(
            num_scalar_prefetch=1,
            grid=(count,),
            in_specs=[whole] * count + [stat, stat],
            out_specs=[stat, stat],
        ),
        out_shape=[
            jax.ShapeDtypeStruct(left_stats.shape, left_stats.dtype),
            jax.ShapeDtypeStruct(right_stats.shape, right_stats.dtype),
        ],
        compiler_params=kernel_params(12),
        cost_estimate=pl.CostEstimate(
            flops=4 * count * side**3, bytes_accessed=18 * count * side * side, transcendentals=0
        ),
    )(me, *blocks, left_stats, right_stats)


def finish_kernel(order, entries, owners_ref, me_ref, *refs):
    count = len(order)
    pieces = refs[:count]
    squares_ref, out_ref, held, sums, sems = refs[count:]
    side, lanes = out_ref.shape[3], squares_ref.shape[1]
    me = me_ref[0]
    named = [owners_ref[me * count + j] for j in range(count)]
    blocks = [home_slot(named, me ^ m) for m in order]
    global_sq = jnp.zeros((1, 1), jnp.float32)
    for k, piece in enumerate(pieces):
        rows = piece[side:, :].astype(jnp.float32)
        global_sq = global_sq + jnp.sum(rows[0:3, 0:1], axis=0, keepdims=True)
        row = jnp.sum(rows[3:6, :], axis=0, keepdims=True)
        parts = [row[:, i : i + lanes] for i in range(0, side, lanes)]
        sums[0, k : k + 1, :] = functools.reduce(jnp.add, parts)
        sums[1, k : k + 1, :] = squares_ref[pl.ds(blocks[k], 1), :]
    area = float(side * side)
    pre_sq = jnp.sum(sums[0], axis=1, keepdims=True)
    block_sq = jnp.sum(sums[1], axis=1, keepdims=True)
    clip_factor = jnp.minimum(1.0, UPDATE_RMS / jnp.sqrt(global_sq / entries))
    graft_ratio = jnp.sqrt(block_sq / area) / jnp.sqrt(pre_sq / area + NORM_FLOOR)
    scale = graft_ratio * clip_factor
    copies = []
    for k, piece in enumerate(pieces):
        pre_float = piece[0:side, :].astype(jnp.float32)
        held[k] = (pre_float * scale[k : k + 1, :]).astype(jnp.bfloat16)
        copy = pltpu.make_async_copy(held.at[k], out_ref.at[0, blocks[k]], sems.at[k])
        copy.start()
        copies.append(copy)
    for copy in copies:
        copy.wait()


def finish(order, owner_list, me, pieces, squares, entries):
    count, side = len(pieces), pieces[0].shape[1]
    return pl.pallas_call(
        functools.partial(finish_kernel, order, entries),
        grid_spec=pltpu.PrefetchScalarGridSpec(
            num_scalar_prefetch=2,
            grid=(),
            in_specs=[pl.BlockSpec(memory_space=pltpu.VMEM)] * (count + 1),
            out_specs=pl.BlockSpec(memory_space=pl.ANY),
            scratch_shapes=[
                pltpu.VMEM((count, side, side), jnp.bfloat16),
                pltpu.VMEM((2, count, squares.shape[1]), jnp.float32),
                pltpu.SemaphoreType.DMA((count,)),
            ],
        ),
        out_shape=jax.ShapeDtypeStruct((1, count, side, side), jnp.bfloat16),
        compiler_params=kernel_params(8),
        cost_estimate=pl.CostEstimate(
            flops=6 * count * side * side, bytes_accessed=4 * count * side * side, transcendentals=0
        ),
    )(owner_list, me, *pieces, squares)


def doublings(size):
    return [2**k for k in range(size.bit_length() - 1)]


def per_device_exchange(
    gradients, second_moment, owners, left_stats, right_stats, left_root, right_root
):
    count = lax.axis_size("fsdp")
    layers = lax.axis_size("layer")
    side = gradients.shape[3]
    me = lax.axis_index("fsdp").astype(jnp.int32).reshape(1)
    owner_list = owners[0, :, 0]
    half = count // 2
    order = [*range(half - 1), half, half - 1, *range(half + 1, count)]

    def swap(value, m, axis="fsdp"):
        if m == 0:
            return value
        return lax.ppermute(value, axis, [(i, i ^ m) for i in range(lax.axis_size(axis))])

    outgoing = route(order, owner_list, me, gradients)
    received = [swap(block, m) for m, block in zip(order, outgoing)]
    squares, total = adam_squares(gradients, second_moment)
    for k in doublings(layers):
        total = total + swap(total, k, "layer")
    tail = sum_tail(total, side)
    returned = []
    for m, block in zip(order, received):
        done = precondition(m, me, block, left_root, right_root, tail)
        returned.append(swap(done, m))
    new_left, new_right = gram_update(order, me, received, left_stats, right_stats)
    entries = float(owner_list.shape[0] * layers * side * side)
    update = finish(order, owner_list, me, returned, squares, entries)
    return (update, new_left, new_right)


def per_device(gradients, second_moment, owners, left_stats, right_stats, left_root, right_root):
    owner_count, blocks, slots = lax.axis_size("fsdp"), gradients.shape[1], left_stats.shape[1]
    layers = lax.axis_size("layer")
    paired = owner_count == blocks == slots
    paired = paired and owner_count & (owner_count - 1) == 0 and layers & (layers - 1) == 0
    body = per_device_exchange if paired else per_device_general
    return body(
        gradients, second_moment, owners, left_stats, right_stats, left_root, right_root
    )


def solution(mesh):
    return jax.shard_map(
        per_device,
        mesh=mesh,
        in_specs=(
            P("layer", "fsdp", None, None),
            P("layer", "fsdp", None, None),
            P("layer", None, None),
            P("layer", "fsdp", None, None),
            P("layer", "fsdp", None, None),
            P("layer", "fsdp", None, None),
            P("layer", "fsdp", None, None),
        ),
        out_specs=(
            P("layer", "fsdp", None, None),
            P("layer", "fsdp", None, None),
            P("layer", "fsdp", None, None),
        ),
        check_vma=False,
    )
```

```python
import functools

import jax
import jax.numpy as jnp
from jax import lax
from jax.experimental import pallas as pl
from jax.experimental.pallas import tpu as pltpu
from jax.sharding import PartitionSpec as P

ADAM_EPS = 1e-08
DECAY_RATE = 0.95
UPDATE_RMS = 1.0
NORM_FLOOR = 1e-06


def selection_tables(owner_list, owner_count, blocks, slots_here, my_index):
    total_blocks = owner_list.shape[0]
    owner_hot = (owner_list[:, None] == lax.iota(jnp.int32, owner_count)[None, :]).astype(
        jnp.float32
    )
    row_ids = lax.iota(jnp.int32, total_blocks)
    strict_lower = (row_ids[:, None] > row_ids[None, :]).astype(jnp.float32)
    before_all = jnp.dot(strict_lower, owner_hot, precision=lax.Precision.HIGHEST)
    slot_number = jnp.sum(before_all * owner_hot, axis=1)
    mine_mask = (owner_list == my_index).astype(jnp.float32)
    slot_hot = (slot_number[:, None] == lax.iota(jnp.float32, slots_here)[None, :]).astype(
        jnp.float32
    ) * mine_mask[:, None]
    home_hot = ((row_ids // blocks)[:, None] == lax.iota(jnp.int32, owner_count)[None, :]).astype(
        jnp.float32
    )
    return (owner_hot, home_hot, slot_hot)


def owner_work(gathered, left_stats, right_stats, left_root, right_root):
    gram_left = jnp.einsum("sij,skj->sik", gathered, gathered, preferred_element_type=jnp.float32)
    gram_right = jnp.einsum("sji,sjk->sik", gathered, gathered, preferred_element_type=jnp.float32)
    new_left = DECAY_RATE * left_stats[0] + (1.0 - DECAY_RATE) * gram_left
    new_right = DECAY_RATE * right_stats[0] + (1.0 - DECAY_RATE) * gram_right
    half_done = jnp.einsum(
        "sij,sjk->sik", left_root[0], gathered, preferred_element_type=jnp.float32
    ).astype(jnp.bfloat16)
    preconditioned = jnp.einsum(
        "sij,sjk->sik", half_done, right_root[0], preferred_element_type=jnp.float32
    ).astype(jnp.bfloat16)
    return (preconditioned, new_left[None], new_right[None])


def per_device_general(gradients, second_moment, owners, left_stats, right_stats, left_root, right_root):
    owner_count = lax.axis_size("fsdp")
    my_index = lax.axis_index("fsdp")
    blocks = gradients.shape[1]
    block_side = gradients.shape[3]
    slots_here = left_stats.shape[1]
    grad_local = gradients[0]
    owner_list = owners[0, :, 0]
    total_blocks = owner_list.shape[0]
    adam_dir = grad_local.astype(jnp.float32) / (jnp.sqrt(second_moment[0]) + ADAM_EPS)
    block_sq = jnp.sum(adam_dir * adam_dir, axis=(1, 2))
    global_sq = lax.psum(jnp.sum(block_sq), ("fsdp", "layer"))
    entry_count = float(total_blocks * lax.axis_size("layer") * block_side * block_side)
    clip_factor = jnp.minimum(1.0, UPDATE_RMS / jnp.sqrt(global_sq / entry_count))
    owner_hot, home_hot, slot_hot = selection_tables(
        owner_list, owner_count, blocks, slots_here, my_index
    )
    first_row = my_index * blocks
    my_owner_hot = lax.dynamic_slice_in_dim(owner_hot, first_row, blocks, 0).astype(jnp.bfloat16)
    outgoing = jnp.einsum(
        "jo,jxy->oxy", my_owner_hot, grad_local, preferred_element_type=jnp.float32
    ).astype(jnp.bfloat16)
    received = lax.all_to_all(outgoing, "fsdp", split_axis=0, concat_axis=0, tiled=True)
    pick_table = jnp.einsum("bs,bh->sh", slot_hot, home_hot).astype(jnp.bfloat16)
    gathered = jnp.einsum(
        "sh,hxy->sxy", pick_table, received, preferred_element_type=jnp.float32
    ).astype(jnp.bfloat16)
    preconditioned, new_left, new_right = owner_work(
        gathered, left_stats, right_stats, left_root, right_root
    )
    answers = jnp.einsum(
        "sh,sxy->hxy", pick_table, preconditioned, preferred_element_type=jnp.float32
    ).astype(jnp.bfloat16)
    returned = lax.all_to_all(answers, "fsdp", split_axis=0, concat_axis=0, tiled=True)
    home_blocks = jnp.einsum(
        "jo,oxy->jxy", my_owner_hot, returned, preferred_element_type=jnp.float32
    )
    pre_float = home_blocks.astype(jnp.bfloat16).astype(jnp.float32)
    graft_ratio = jnp.sqrt(block_sq / float(block_side * block_side)) / jnp.sqrt(
        jnp.sum(pre_float * pre_float, axis=(1, 2)) / float(block_side * block_side) + NORM_FLOOR
    )
    update = (pre_float * (graft_ratio * clip_factor)[:, None, None]).astype(jnp.bfloat16)
    return (update[None], new_left, new_right)


TAIL = 16


def kernel_params(mebibytes):
    return pltpu.CompilerParams(vmem_limit_bytes=mebibytes * 2**20)


def home_slot(named, target):
    block = jnp.int32(0)
    for j in range(1, len(named)):
        block = jnp.where(named[j] == target, jnp.int32(j), block)
    return block


def route_kernel(order, owners_hbm, me_ref, grad_hbm, *refs):
    outs, (owners_ref, held, owner_sem, grad_sem) = refs[:-4], refs[-4:]
    count = held.shape[0]
    me = me_ref[0]
    fetch_owners = pltpu.make_async_copy(owners_hbm, owners_ref, owner_sem)
    fetch_grads = pltpu.make_async_copy(grad_hbm.at[0], held, grad_sem)
    fetch_owners.start()
    fetch_grads.start()
    fetch_owners.wait()
    named = [owners_ref[me * count + j] for j in range(count)]
    blocks = [home_slot(named, me ^ m) for m in order]
    fetch_grads.wait()
    for block, out in zip(blocks, outs):
        out[...] = held[block]


def route(order, owner_list, me, gradients):
    count, side = gradients.shape[1], gradients.shape[3]
    hbm = pl.BlockSpec(memory_space=pltpu.HBM)
    piece = jax.ShapeDtypeStruct((side, side), gradients.dtype)
    return pl.pallas_call(
        functools.partial(route_kernel, order),
        in_specs=[hbm, pl.BlockSpec(memory_space=pltpu.SMEM), hbm],
        out_specs=[pl.BlockSpec(memory_space=pltpu.VMEM)] * count,
        scratch_shapes=[
            pltpu.SMEM(owner_list.shape, jnp.int32),
            pltpu.VMEM((count, side, side), gradients.dtype),
            pltpu.SemaphoreType.DMA,
            pltpu.SemaphoreType.DMA,
        ],
        out_shape=[piece] * count,
        compiler_params=kernel_params(6),
        cost_estimate=pl.CostEstimate(
            flops=0, bytes_accessed=4 * count * side * side, transcendentals=0
        ),
    )(
        pltpu.with_memory_space_constraint(owner_list, pltpu.HBM),
        me,
        pltpu.with_memory_space_constraint(gradients, pltpu.HBM),
    )


def adam_kernel(grad_hbm, moment_hbm, out_ref, total_ref, grads, moments, sems):
    count, side = grads.shape[0], grads.shape[2]
    lanes = out_ref.shape[1]
    copies = []
    for b in range(count):
        pair = (
            pltpu.make_async_copy(grad_hbm.at[0, b], grads.at[b], sems.at[0, b]),
            pltpu.make_async_copy(moment_hbm.at[0, b], moments.at[b], sems.at[1, b]),
        )
        for copy in pair:
            copy.start()
        copies.append(pair)
    total = jnp.zeros((1, lanes), jnp.float32)
    for b, pair in enumerate(copies):
        for copy in pair:
            copy.wait()
        adam_dir = grads[b].astype(jnp.float32) / (jnp.sqrt(moments[b]) + ADAM_EPS)
        squares = jnp.sum(adam_dir * adam_dir, axis=0, keepdims=True)
        row = squares[:, 0:lanes]
        for k in range(lanes, side, lanes):
            row = row + squares[:, k : k + lanes]
        out_ref[b : b + 1, :] = row
        total = total + row
    total_ref[...] = jnp.broadcast_to(total, total_ref.shape)


def adam_squares(gradients, second_moment):
    count, side = gradients.shape[1], gradients.shape[3]
    hbm = pl.BlockSpec(memory_space=pltpu.HBM)
    return pl.pallas_call(
        adam_kernel,
        in_specs=[hbm, hbm],
        out_specs=[pl.BlockSpec(memory_space=pltpu.VMEM)] * 2,
        out_shape=[
            jax.ShapeDtypeStruct((count, 128), jnp.float32),
            jax.ShapeDtypeStruct((8, 128), jnp.float32),
        ],
        scratch_shapes=[
            pltpu.VMEM((count, side, side), gradients.dtype),
            pltpu.VMEM((count, side, side), second_moment.dtype),
            pltpu.SemaphoreType.DMA((2, count)),
        ],
        compiler_params=kernel_params(8),
        cost_estimate=pl.CostEstimate(
            flops=8 * count * side * side,
            bytes_accessed=6 * count * side * side,
            transcendentals=2 * count * side * side,
        ),
    )(
        pltpu.with_memory_space_constraint(gradients, pltpu.HBM),
        pltpu.with_memory_space_constraint(second_moment, pltpu.HBM),
    )


def split_terms(value):
    high = value.astype(jnp.bfloat16).astype(jnp.float32)
    rest = value - high
    middle = rest.astype(jnp.bfloat16).astype(jnp.float32)
    return high, middle, rest - middle


def with_rows(rest, first, terms):
    row = lax.broadcasted_iota(jnp.int32, rest.shape, 0)
    for k, term in enumerate(terms):
        rest = jnp.where(row == first + k, term, rest)
    return rest


def tail_kernel(total_ref, out_ref):
    total = jnp.sum(total_ref[0:1, :], keepdims=True)
    rows = with_rows(jnp.zeros(out_ref.shape, jnp.float32), 0, split_terms(total))
    out_ref[...] = rows.astype(jnp.bfloat16)


def sum_tail(total, side):
    return pl.pallas_call(
        tail_kernel,
        in_specs=[pl.BlockSpec(memory_space=pltpu.VMEM)],
        out_specs=pl.BlockSpec(memory_space=pltpu.VMEM),
        out_shape=jax.ShapeDtypeStruct((TAIL, side), jnp.bfloat16),
        compiler_params=kernel_params(2),
        cost_estimate=pl.CostEstimate(flops=4096, bytes_accessed=32768, transcendentals=0),
    )(total)


def precondition_kernel(m, me_ref, grad_ref, left_ref, right_ref, tail_ref, out_ref):
    side = grad_ref.shape[0]
    slot = me_ref[0] ^ m
    half_done = jnp.dot(
        left_ref[0, slot], grad_ref[...], preferred_element_type=jnp.float32
    ).astype(jnp.bfloat16)
    preconditioned = jnp.dot(
        half_done, right_ref[0, slot], preferred_element_type=jnp.float32
    ).astype(jnp.bfloat16)
    out_ref[0:side, :] = preconditioned
    pre_float = preconditioned.astype(jnp.float32)
    squares = jnp.sum(pre_float * pre_float, axis=0, keepdims=True)
    rows = with_rows(tail_ref[...].astype(jnp.float32), 3, split_terms(squares))
    out_ref[side:, :] = rows.astype(jnp.bfloat16)


def precondition(m, me, block, left_root, right_root, tail):
    side = block.shape[0]
    return pl.pallas_call(
        functools.partial(precondition_kernel, m),
        grid_spec=pltpu.PrefetchScalarGridSpec(
            num_scalar_prefetch=1,
            grid=(),
            in_specs=[pl.BlockSpec(memory_space=pltpu.VMEM)] * 4,
            out_specs=pl.BlockSpec(memory_space=pltpu.VMEM),
        ),
        out_shape=jax.ShapeDtypeStruct((side + TAIL, side), jnp.bfloat16),
        compiler_params=kernel_params(6),
        cost_estimate=pl.CostEstimate(
            flops=4 * side**3, bytes_accessed=8 * side * side, transcendentals=0
        ),
    )(me, block, left_root, right_root, tail)


def gram_kernel(order, me_ref, *refs):
    count = len(refs) - 4
    grads = refs[:count]
    left_ref, right_ref, new_left_ref, new_right_ref = refs[count:]
    step = pl.program_id(0)
    for k, m in enumerate(order):

        @pl.when(step == m)
        def _():
            block = grads[k][...]
            gram_left = lax.dot_general(
                block, block, (((1,), (1,)), ((), ())), preferred_element_type=jnp.float32
            )
            gram_right = lax.dot_general(
                block, block, (((0,), (0,)), ((), ())), preferred_element_type=jnp.float32
            )
            new_left_ref[0, 0] = DECAY_RATE * left_ref[0, 0] + (1.0 - DECAY_RATE) * gram_left
            new_right_ref[0, 0] = DECAY_RATE * right_ref[0, 0] + (1.0 - DECAY_RATE) * gram_right


def gram_update(order, me, blocks, left_stats, right_stats):
    count, side = len(blocks), blocks[0].shape[0]
    stat = pl.BlockSpec((1, 1, side, side), lambda i, me_ref: (0, me_ref[0] ^ i, 0, 0))
    whole = pl.BlockSpec(memory_space=pltpu.VMEM)
    return pl.pallas_call(
        functools.partial(gram_kernel, order),
        grid_spec=pltpu.PrefetchScalarGridSpec(
            num_scalar_prefetch=1,
            grid=(count,),
            in_specs=[whole] * count + [stat, stat],
            out_specs=[stat, stat],
        ),
        out_shape=[
            jax.ShapeDtypeStruct(left_stats.shape, left_stats.dtype),
            jax.ShapeDtypeStruct(right_stats.shape, right_stats.dtype),
        ],
        compiler_params=kernel_params(12),
        cost_estimate=pl.CostEstimate(
            flops=4 * count * side**3, bytes_accessed=18 * count * side * side, transcendentals=0
        ),
    )(me, *blocks, left_stats, right_stats)


def finish_kernel(order, entries, owners_ref, me_ref, *refs):
    count = len(order)
    pieces = refs[:count]
    squares_ref, out_ref, held, sums, sems = refs[count:]
    side, lanes = out_ref.shape[3], squares_ref.shape[1]
    me = me_ref[0]
    named = [owners_ref[me * count + j] for j in range(count)]
    blocks = [home_slot(named, me ^ m) for m in order]
    global_sq = jnp.zeros((1, 1), jnp.float32)
    for k, piece in enumerate(pieces):
        rows = piece[side:, :].astype(jnp.float32)
        global_sq = global_sq + jnp.sum(rows[0:3, 0:1], axis=0, keepdims=True)
        row = jnp.sum(rows[3:6, :], axis=0, keepdims=True)
        parts = [row[:, i : i + lanes] for i in range(0, side, lanes)]
        sums[0, k : k + 1, :] = functools.reduce(jnp.add, parts)
        sums[1, k : k + 1, :] = squares_ref[pl.ds(blocks[k], 1), :]
    area = float(side * side)
    pre_sq = jnp.sum(sums[0], axis=1, keepdims=True)
    block_sq = jnp.sum(sums[1], axis=1, keepdims=True)
    clip_factor = jnp.minimum(1.0, UPDATE_RMS / jnp.sqrt(global_sq / entries))
    graft_ratio = jnp.sqrt(block_sq / area) / jnp.sqrt(pre_sq / area + NORM_FLOOR)
    scale = graft_ratio * clip_factor
    copies = []
    for k, piece in enumerate(pieces):
        pre_float = piece[0:side, :].astype(jnp.float32)
        held[k] = (pre_float * scale[k : k + 1, :]).astype(jnp.bfloat16)
        copy = pltpu.make_async_copy(held.at[k], out_ref.at[0, blocks[k]], sems.at[k])
        copy.start()
        copies.append(copy)
    for copy in copies:
        copy.wait()


def finish(order, owner_list, me, pieces, squares, entries):
    count, side = len(pieces), pieces[0].shape[1]
    return pl.pallas_call(
        functools.partial(finish_kernel, order, entries),
        grid_spec=pltpu.PrefetchScalarGridSpec(
            num_scalar_prefetch=2,
            grid=(),
            in_specs=[pl.BlockSpec(memory_space=pltpu.VMEM)] * (count + 1),
            out_specs=pl.BlockSpec(memory_space=pl.ANY),
            scratch_shapes=[
                pltpu.VMEM((count, side, side), jnp.bfloat16),
                pltpu.VMEM((2, count, squares.shape[1]), jnp.float32),
                pltpu.SemaphoreType.DMA((count,)),
            ],
        ),
        out_shape=jax.ShapeDtypeStruct((1, count, side, side), jnp.bfloat16),
        compiler_params=kernel_params(8),
        cost_estimate=pl.CostEstimate(
            flops=6 * count * side * side, bytes_accessed=4 * count * side * side, transcendentals=0
        ),
    )(owner_list, me, *pieces, squares)


def doublings(size):
    return [2**k for k in range(size.bit_length() - 1)]


def per_device_exchange(
    gradients, second_moment, owners, left_stats, right_stats, left_root, right_root
):
    count = lax.axis_size("fsdp")
    layers = lax.axis_size("layer")
    side = gradients.shape[3]
    me = lax.axis_index("fsdp").astype(jnp.int32).reshape(1)
    owner_list = owners[0, :, 0]
    half = count // 2
    order = [0, *range(half - 2, 0, -1), half, half - 1, *range(half + 1, count)]

    def swap(value, m, axis="fsdp"):
        if m == 0:
            return value
        return lax.ppermute(value, axis, [(i, i ^ m) for i in range(lax.axis_size(axis))])

    outgoing = route(order, owner_list, me, gradients)
    received = [swap(block, m) for m, block in zip(order, outgoing)]
    squares, total = adam_squares(gradients, second_moment)
    for k in doublings(layers):
        total = total + swap(total, k, "layer")
    tail = sum_tail(total, side)
    returned = []
    for m, block in zip(order, received):
        done = precondition(m, me, block, left_root, right_root, tail)
        returned.append(swap(done, m))
    new_left, new_right = gram_update(order, me, received, left_stats, right_stats)
    entries = float(owner_list.shape[0] * layers * side * side)
    update = finish(order, owner_list, me, returned, squares, entries)
    return (update, new_left, new_right)


def per_device(gradients, second_moment, owners, left_stats, right_stats, left_root, right_root):
    owner_count, blocks, slots = lax.axis_size("fsdp"), gradients.shape[1], left_stats.shape[1]
    layers = lax.axis_size("layer")
    paired = owner_count == blocks == slots
    paired = paired and owner_count & (owner_count - 1) == 0 and layers & (layers - 1) == 0
    body = per_device_exchange if paired else per_device_general
    return body(
        gradients, second_moment, owners, left_stats, right_stats, left_root, right_root
    )


def solution(mesh):
    return jax.shard_map(
        per_device,
        mesh=mesh,
        in_specs=(
            P("layer", "fsdp", None, None),
            P("layer", "fsdp", None, None),
            P("layer", None, None),
            P("layer", "fsdp", None, None),
            P("layer", "fsdp", None, None),
            P("layer", "fsdp", None, None),
            P("layer", "fsdp", None, None),
        ),
        out_specs=(
            P("layer", "fsdp", None, None),
            P("layer", "fsdp", None, None),
            P("layer", "fsdp", None, None),
        ),
        check_vma=False,
    )
```

```python
import functools

import jax
import jax.numpy as jnp
from jax import lax
from jax.experimental import pallas as pl
from jax.experimental.pallas import tpu as pltpu
from jax.sharding import PartitionSpec as P

ADAM_EPS = 1e-08
DECAY_RATE = 0.95
UPDATE_RMS = 1.0
NORM_FLOOR = 1e-06


def selection_tables(owner_list, owner_count, blocks, slots_here, my_index):
    total_blocks = owner_list.shape[0]
    owner_hot = (owner_list[:, None] == lax.iota(jnp.int32, owner_count)[None, :]).astype(
        jnp.float32
    )
    row_ids = lax.iota(jnp.int32, total_blocks)
    strict_lower = (row_ids[:, None] > row_ids[None, :]).astype(jnp.float32)
    before_all = jnp.dot(strict_lower, owner_hot, precision=lax.Precision.HIGHEST)
    slot_number = jnp.sum(before_all * owner_hot, axis=1)
    mine_mask = (owner_list == my_index).astype(jnp.float32)
    slot_hot = (slot_number[:, None] == lax.iota(jnp.float32, slots_here)[None, :]).astype(
        jnp.float32
    ) * mine_mask[:, None]
    home_hot = ((row_ids // blocks)[:, None] == lax.iota(jnp.int32, owner_count)[None, :]).astype(
        jnp.float32
    )
    return (owner_hot, home_hot, slot_hot)


def owner_work(gathered, left_stats, right_stats, left_root, right_root):
    gram_left = jnp.einsum("sij,skj->sik", gathered, gathered, preferred_element_type=jnp.float32)
    gram_right = jnp.einsum("sji,sjk->sik", gathered, gathered, preferred_element_type=jnp.float32)
    new_left = DECAY_RATE * left_stats[0] + (1.0 - DECAY_RATE) * gram_left
    new_right = DECAY_RATE * right_stats[0] + (1.0 - DECAY_RATE) * gram_right
    half_done = jnp.einsum(
        "sij,sjk->sik", left_root[0], gathered, preferred_element_type=jnp.float32
    ).astype(jnp.bfloat16)
    preconditioned = jnp.einsum(
        "sij,sjk->sik", half_done, right_root[0], preferred_element_type=jnp.float32
    ).astype(jnp.bfloat16)
    return (preconditioned, new_left[None], new_right[None])


def per_device_general(gradients, second_moment, owners, left_stats, right_stats, left_root, right_root):
    owner_count = lax.axis_size("fsdp")
    my_index = lax.axis_index("fsdp")
    blocks = gradients.shape[1]
    block_side = gradients.shape[3]
    slots_here = left_stats.shape[1]
    grad_local = gradients[0]
    owner_list = owners[0, :, 0]
    total_blocks = owner_list.shape[0]
    adam_dir = grad_local.astype(jnp.float32) / (jnp.sqrt(second_moment[0]) + ADAM_EPS)
    block_sq = jnp.sum(adam_dir * adam_dir, axis=(1, 2))
    global_sq = lax.psum(jnp.sum(block_sq), ("fsdp", "layer"))
    entry_count = float(total_blocks * lax.axis_size("layer") * block_side * block_side)
    clip_factor = jnp.minimum(1.0, UPDATE_RMS / jnp.sqrt(global_sq / entry_count))
    owner_hot, home_hot, slot_hot = selection_tables(
        owner_list, owner_count, blocks, slots_here, my_index
    )
    first_row = my_index * blocks
    my_owner_hot = lax.dynamic_slice_in_dim(owner_hot, first_row, blocks, 0).astype(jnp.bfloat16)
    outgoing = jnp.einsum(
        "jo,jxy->oxy", my_owner_hot, grad_local, preferred_element_type=jnp.float32
    ).astype(jnp.bfloat16)
    received = lax.all_to_all(outgoing, "fsdp", split_axis=0, concat_axis=0, tiled=True)
    pick_table = jnp.einsum("bs,bh->sh", slot_hot, home_hot).astype(jnp.bfloat16)
    gathered = jnp.einsum(
        "sh,hxy->sxy", pick_table, received, preferred_element_type=jnp.float32
    ).astype(jnp.bfloat16)
    preconditioned, new_left, new_right = owner_work(
        gathered, left_stats, right_stats, left_root, right_root
    )
    answers = jnp.einsum(
        "sh,sxy->hxy", pick_table, preconditioned, preferred_element_type=jnp.float32
    ).astype(jnp.bfloat16)
    returned = lax.all_to_all(answers, "fsdp", split_axis=0, concat_axis=0, tiled=True)
    home_blocks = jnp.einsum(
        "jo,oxy->jxy", my_owner_hot, returned, preferred_element_type=jnp.float32
    )
    pre_float = home_blocks.astype(jnp.bfloat16).astype(jnp.float32)
    graft_ratio = jnp.sqrt(block_sq / float(block_side * block_side)) / jnp.sqrt(
        jnp.sum(pre_float * pre_float, axis=(1, 2)) / float(block_side * block_side) + NORM_FLOOR
    )
    update = (pre_float * (graft_ratio * clip_factor)[:, None, None]).astype(jnp.bfloat16)
    return (update[None], new_left, new_right)


TAIL = 16


def kernel_params(mebibytes):
    return pltpu.CompilerParams(vmem_limit_bytes=mebibytes * 2**20)


def partner_tables(count):
    half = count // 2
    even = [*range(half - 1), half, half - 1, *range(half + 1, count)]
    odd = [{1: half, half: 1}.get(m, m) for m in even]
    return even, odd


def fsdp_index(who, layers):
    return lax.shift_right_logical(who, jnp.int32(layers.bit_length() - 1))


def partner(who, layers, step, count):
    even, odd = partner_tables(count)
    turn = who ^ lax.shift_right_logical(fsdp_index(who, layers), jnp.int32(1))
    return jnp.where(turn & 1 == 1, jnp.int32(odd[step]), jnp.int32(even[step]))


def home_slot(named, target):
    block = jnp.int32(0)
    for j in range(1, len(named)):
        block = jnp.where(named[j] == target, jnp.int32(j), block)
    return block


def route_kernel(layers, owners_hbm, who_ref, grad_hbm, *refs):
    outs, (owners_ref, held, owner_sem, grad_sem) = refs[:-4], refs[-4:]
    count = held.shape[0]
    who = who_ref[0]
    me = fsdp_index(who, layers)
    fetch_owners = pltpu.make_async_copy(owners_hbm, owners_ref, owner_sem)
    fetch_grads = pltpu.make_async_copy(grad_hbm.at[0], held, grad_sem)
    fetch_owners.start()
    fetch_grads.start()
    fetch_owners.wait()
    named = [owners_ref[me * count + j] for j in range(count)]
    blocks = [home_slot(named, me ^ partner(who, layers, step, count)) for step in range(count)]
    fetch_grads.wait()
    for block, out in zip(blocks, outs):
        out[...] = held[block]


def route(layers, owner_list, who, gradients):
    count, side = gradients.shape[1], gradients.shape[3]
    hbm = pl.BlockSpec(memory_space=pltpu.HBM)
    piece = jax.ShapeDtypeStruct((side, side), gradients.dtype)
    return pl.pallas_call(
        functools.partial(route_kernel, layers),
        in_specs=[hbm, pl.BlockSpec(memory_space=pltpu.SMEM), hbm],
        out_specs=[pl.BlockSpec(memory_space=pltpu.VMEM)] * count,
        scratch_shapes=[
            pltpu.SMEM(owner_list.shape, jnp.int32),
            pltpu.VMEM((count, side, side), gradients.dtype),
            pltpu.SemaphoreType.DMA,
            pltpu.SemaphoreType.DMA,
        ],
        out_shape=[piece] * count,
        compiler_params=kernel_params(6),
        cost_estimate=pl.CostEstimate(
            flops=0, bytes_accessed=4 * count * side * side, transcendentals=0
        ),
    )(
        pltpu.with_memory_space_constraint(owner_list, pltpu.HBM),
        who,
        pltpu.with_memory_space_constraint(gradients, pltpu.HBM),
    )


def adam_kernel(grad_hbm, moment_hbm, out_ref, total_ref, grads, moments, sems):
    count, side = grads.shape[0], grads.shape[2]
    lanes = out_ref.shape[1]
    copies = []
    for b in range(count):
        pair = (
            pltpu.make_async_copy(grad_hbm.at[0, b], grads.at[b], sems.at[0, b]),
            pltpu.make_async_copy(moment_hbm.at[0, b], moments.at[b], sems.at[1, b]),
        )
        for copy in pair:
            copy.start()
        copies.append(pair)
    total = jnp.zeros((1, lanes), jnp.float32)
    for b, pair in enumerate(copies):
        for copy in pair:
            copy.wait()
        adam_dir = grads[b].astype(jnp.float32) / (jnp.sqrt(moments[b]) + ADAM_EPS)
        squares = jnp.sum(adam_dir * adam_dir, axis=0, keepdims=True)
        row = squares[:, 0:lanes]
        for k in range(lanes, side, lanes):
            row = row + squares[:, k : k + lanes]
        out_ref[b : b + 1, :] = row
        total = total + row
    total_ref[...] = jnp.broadcast_to(total, total_ref.shape)


def adam_squares(gradients, second_moment):
    count, side = gradients.shape[1], gradients.shape[3]
    hbm = pl.BlockSpec(memory_space=pltpu.HBM)
    return pl.pallas_call(
        adam_kernel,
        in_specs=[hbm, hbm],
        out_specs=[pl.BlockSpec(memory_space=pltpu.VMEM)] * 2,
        out_shape=[
            jax.ShapeDtypeStruct((count, 128), jnp.float32),
            jax.ShapeDtypeStruct((8, 128), jnp.float32),
        ],
        scratch_shapes=[
            pltpu.VMEM((count, side, side), gradients.dtype),
            pltpu.VMEM((count, side, side), second_moment.dtype),
            pltpu.SemaphoreType.DMA((2, count)),
        ],
        compiler_params=kernel_params(8),
        cost_estimate=pl.CostEstimate(
            flops=8 * count * side * side,
            bytes_accessed=6 * count * side * side,
            transcendentals=2 * count * side * side,
        ),
    )(
        pltpu.with_memory_space_constraint(gradients, pltpu.HBM),
        pltpu.with_memory_space_constraint(second_moment, pltpu.HBM),
    )


def tail_kernel(total_ref, out_ref):
    total = jnp.sum(total_ref[0:1, :], keepdims=True)
    high = total.astype(jnp.bfloat16).astype(jnp.float32)
    rest = total - high
    middle = rest.astype(jnp.bfloat16).astype(jnp.float32)
    low = rest - middle
    row = lax.broadcasted_iota(jnp.int32, out_ref.shape, 0)
    value = jnp.where(row == 0, high, jnp.where(row == 1, middle, jnp.where(row == 2, low, 0.0)))
    out_ref[...] = value.astype(jnp.bfloat16)


def sum_tail(total, side):
    return pl.pallas_call(
        tail_kernel,
        in_specs=[pl.BlockSpec(memory_space=pltpu.VMEM)],
        out_specs=pl.BlockSpec(memory_space=pltpu.VMEM),
        out_shape=jax.ShapeDtypeStruct((TAIL, side), jnp.bfloat16),
        compiler_params=kernel_params(2),
        cost_estimate=pl.CostEstimate(flops=4096, bytes_accessed=32768, transcendentals=0),
    )(total)


def precondition_kernel(step, layers, who_ref, grad_ref, left_ref, right_ref, tail_ref, out_ref):
    side = grad_ref.shape[0]
    who = who_ref[0]
    slot = fsdp_index(who, layers) ^ partner(who, layers, step, left_ref.shape[1])
    half_done = jnp.dot(
        left_ref[0, slot], grad_ref[...], preferred_element_type=jnp.float32
    ).astype(jnp.bfloat16)
    out_ref[0:side, :] = jnp.dot(
        half_done, right_ref[0, slot], preferred_element_type=jnp.float32
    ).astype(jnp.bfloat16)
    if step:
        out_ref[side:, :] = tail_ref[...]


def precondition(step, layers, who, block, left_root, right_root, tail):
    side = block.shape[0]
    return pl.pallas_call(
        functools.partial(precondition_kernel, step, layers),
        grid_spec=pltpu.PrefetchScalarGridSpec(
            num_scalar_prefetch=1,
            grid=(),
            in_specs=[pl.BlockSpec(memory_space=pltpu.VMEM)] * 4,
            out_specs=pl.BlockSpec(memory_space=pltpu.VMEM),
        ),
        out_shape=jax.ShapeDtypeStruct((side + (TAIL if step else 0), side), jnp.bfloat16),
        compiler_params=kernel_params(6),
        cost_estimate=pl.CostEstimate(
            flops=4 * side**3, bytes_accessed=8 * side * side, transcendentals=0
        ),
    )(who, block, left_root, right_root, tail)


def gram_kernel(who_ref, *refs):
    count = len(refs) - 4
    grads = refs[:count]
    left_ref, right_ref, new_left_ref, new_right_ref = refs[count:]
    step = pl.program_id(0)
    for k in range(count):

        @pl.when(step == k)
        def _():
            block = grads[k][...]
            gram_left = lax.dot_general(
                block, block, (((1,), (1,)), ((), ())), preferred_element_type=jnp.float32
            )
            gram_right = lax.dot_general(
                block, block, (((0,), (0,)), ((), ())), preferred_element_type=jnp.float32
            )
            new_left_ref[0, 0] = DECAY_RATE * left_ref[0, 0] + (1.0 - DECAY_RATE) * gram_left
            new_right_ref[0, 0] = DECAY_RATE * right_ref[0, 0] + (1.0 - DECAY_RATE) * gram_right


def gram_update(layers, who, blocks, left_stats, right_stats):
    count, side = len(blocks), blocks[0].shape[0]

    def slot(i, who_ref):
        who = who_ref[0]
        m = jnp.int32(0)
        for step in range(1, count):
            m = jnp.where(i == step, partner(who, layers, step, count), m)
        return (0, fsdp_index(who, layers) ^ m, 0, 0)

    stat = pl.BlockSpec((1, 1, side, side), slot)
    whole = pl.BlockSpec(memory_space=pltpu.VMEM)
    return pl.pallas_call(
        gram_kernel,
        grid_spec=pltpu.PrefetchScalarGridSpec(
            num_scalar_prefetch=1,
            grid=(count,),
            in_specs=[whole] * count + [stat, stat],
            out_specs=[stat, stat],
        ),
        out_shape=[
            jax.ShapeDtypeStruct(left_stats.shape, left_stats.dtype),
            jax.ShapeDtypeStruct(right_stats.shape, right_stats.dtype),
        ],
        compiler_params=kernel_params(12),
        cost_estimate=pl.CostEstimate(
            flops=4 * count * side**3, bytes_accessed=18 * count * side * side, transcendentals=0
        ),
    )(who, *blocks, left_stats, right_stats)


def finish_kernel(layers, entries, owners_ref, who_ref, *refs):
    count = len(refs) - 6
    pieces = refs[:count]
    squares_ref, tail_ref, out_ref, held, sums, sems = refs[count:]
    side, lanes = out_ref.shape[3], squares_ref.shape[1]
    who = who_ref[0]
    me = fsdp_index(who, layers)
    named = [owners_ref[me * count + j] for j in range(count)]
    blocks = [home_slot(named, me ^ partner(who, layers, step, count)) for step in range(count)]
    global_sq = jnp.zeros((1, 1), jnp.float32)
    for rows in [tail_ref[...]] + [piece[side:, :] for piece in pieces if piece.shape[0] > side]:
        terms = rows[:, 0:1].astype(jnp.float32)
        global_sq = global_sq + jnp.sum(terms, axis=0, keepdims=True)
    for k, piece in enumerate(pieces):
        pre_float = piece[0:side, :].astype(jnp.float32)
        row = jnp.sum(pre_float * pre_float, axis=0, keepdims=True)
        parts = [row[:, i : i + lanes] for i in range(0, side, lanes)]
        sums[0, k : k + 1, :] = functools.reduce(jnp.add, parts)
        sums[1, k : k + 1, :] = squares_ref[pl.ds(blocks[k], 1), :]
    area = float(side * side)
    pre_sq = jnp.sum(sums[0], axis=1, keepdims=True)
    block_sq = jnp.sum(sums[1], axis=1, keepdims=True)
    clip_factor = jnp.minimum(1.0, UPDATE_RMS / jnp.sqrt(global_sq / entries))
    graft_ratio = jnp.sqrt(block_sq / area) / jnp.sqrt(pre_sq / area + NORM_FLOOR)
    scale = graft_ratio * clip_factor
    copies = []
    for k, piece in enumerate(pieces):
        pre_float = piece[0:side, :].astype(jnp.float32)
        held[k] = (pre_float * scale[k : k + 1, :]).astype(jnp.bfloat16)
        copy = pltpu.make_async_copy(held.at[k], out_ref.at[0, blocks[k]], sems.at[k])
        copy.start()
        copies.append(copy)
    for copy in copies:
        copy.wait()


def finish(layers, owner_list, who, pieces, squares, tail, entries):
    count, side = len(pieces), pieces[0].shape[1]
    return pl.pallas_call(
        functools.partial(finish_kernel, layers, entries),
        grid_spec=pltpu.PrefetchScalarGridSpec(
            num_scalar_prefetch=2,
            grid=(),
            in_specs=[pl.BlockSpec(memory_space=pltpu.VMEM)] * (count + 2),
            out_specs=pl.BlockSpec(memory_space=pl.ANY),
            scratch_shapes=[
                pltpu.VMEM((count, side, side), jnp.bfloat16),
                pltpu.VMEM((2, count, squares.shape[1]), jnp.float32),
                pltpu.SemaphoreType.DMA((count,)),
            ],
        ),
        out_shape=jax.ShapeDtypeStruct((1, count, side, side), jnp.bfloat16),
        compiler_params=kernel_params(8),
        cost_estimate=pl.CostEstimate(
            flops=6 * count * side * side, bytes_accessed=4 * count * side * side, transcendentals=0
        ),
    )(owner_list, who, *pieces, squares, tail)


def doublings(size):
    return [2**k for k in range(size.bit_length() - 1)]


def per_device_exchange(
    gradients, second_moment, owners, left_stats, right_stats, left_root, right_root
):
    count, layers = lax.axis_size("fsdp"), lax.axis_size("layer")
    side = gradients.shape[3]
    who = lax.axis_index(("fsdp", "layer")).astype(jnp.int32).reshape(1)
    owner_list = owners[0, :, 0]
    tables = partner_tables(count)

    def swap(value, step):
        if step == 0:
            return value
        pairs = [
            (i * layers + k, (i ^ tables[(k ^ (i >> 1)) & 1][step]) * layers + k)
            for i in range(count)
            for k in range(layers)
        ]
        return lax.ppermute(value, ("fsdp", "layer"), pairs)

    outgoing = route(layers, owner_list, who, gradients)
    received = [swap(block, step) for step, block in enumerate(outgoing)]
    squares, total = adam_squares(gradients, second_moment)
    for k in doublings(layers):
        total = total + lax.ppermute(total, "layer", [(i, i ^ k) for i in range(layers)])
    tail = sum_tail(total, side)
    returned = []
    for step, block in enumerate(received):
        done = precondition(step, layers, who, block, left_root, right_root, tail)
        returned.append(swap(done, step))
    new_left, new_right = gram_update(layers, who, received, left_stats, right_stats)
    entries = float(owner_list.shape[0] * layers * side * side)
    update = finish(layers, owner_list, who, returned, squares, tail, entries)
    return (update, new_left, new_right)


def per_device(gradients, second_moment, owners, left_stats, right_stats, left_root, right_root):
    owner_count, blocks, slots = lax.axis_size("fsdp"), gradients.shape[1], left_stats.shape[1]
    layers = lax.axis_size("layer")
    paired = owner_count == blocks == slots and owner_count >= 8
    paired = paired and owner_count & (owner_count - 1) == 0 and layers & (layers - 1) == 0
    body = per_device_exchange if paired else per_device_general
    return body(
        gradients, second_moment, owners, left_stats, right_stats, left_root, right_root
    )


def solution(mesh):
    return jax.shard_map(
        per_device,
        mesh=mesh,
        in_specs=(
            P("layer", "fsdp", None, None),
            P("layer", "fsdp", None, None),
            P("layer", None, None),
            P("layer", "fsdp", None, None),
            P("layer", "fsdp", None, None),
            P("layer", "fsdp", None, None),
            P("layer", "fsdp", None, None),
        ),
        out_specs=(
            P("layer", "fsdp", None, None),
            P("layer", "fsdp", None, None),
            P("layer", "fsdp", None, None),
        ),
        check_vma=False,
    )
```

```python
import functools

import jax
import jax.numpy as jnp
from jax import lax
from jax.experimental import pallas as pl
from jax.experimental.pallas import tpu as pltpu
from jax.sharding import PartitionSpec as P

ADAM_EPS = 1e-08
DECAY_RATE = 0.95
UPDATE_RMS = 1.0
NORM_FLOOR = 1e-06


def selection_tables(owner_list, owner_count, blocks, slots_here, my_index):
    total_blocks = owner_list.shape[0]
    owner_hot = (owner_list[:, None] == lax.iota(jnp.int32, owner_count)[None, :]).astype(
        jnp.float32
    )
    row_ids = lax.iota(jnp.int32, total_blocks)
    strict_lower = (row_ids[:, None] > row_ids[None, :]).astype(jnp.float32)
    before_all = jnp.dot(strict_lower, owner_hot, precision=lax.Precision.HIGHEST)
    slot_number = jnp.sum(before_all * owner_hot, axis=1)
    mine_mask = (owner_list == my_index).astype(jnp.float32)
    slot_hot = (slot_number[:, None] == lax.iota(jnp.float32, slots_here)[None, :]).astype(
        jnp.float32
    ) * mine_mask[:, None]
    home_hot = ((row_ids // blocks)[:, None] == lax.iota(jnp.int32, owner_count)[None, :]).astype(
        jnp.float32
    )
    return (owner_hot, home_hot, slot_hot)


def owner_work(gathered, left_stats, right_stats, left_root, right_root):
    gram_left = jnp.einsum("sij,skj->sik", gathered, gathered, preferred_element_type=jnp.float32)
    gram_right = jnp.einsum("sji,sjk->sik", gathered, gathered, preferred_element_type=jnp.float32)
    new_left = DECAY_RATE * left_stats[0] + (1.0 - DECAY_RATE) * gram_left
    new_right = DECAY_RATE * right_stats[0] + (1.0 - DECAY_RATE) * gram_right
    half_done = jnp.einsum(
        "sij,sjk->sik", left_root[0], gathered, preferred_element_type=jnp.float32
    ).astype(jnp.bfloat16)
    preconditioned = jnp.einsum(
        "sij,sjk->sik", half_done, right_root[0], preferred_element_type=jnp.float32
    ).astype(jnp.bfloat16)
    return (preconditioned, new_left[None], new_right[None])


def per_device_general(gradients, second_moment, owners, left_stats, right_stats, left_root, right_root):
    owner_count = lax.axis_size("fsdp")
    my_index = lax.axis_index("fsdp")
    blocks = gradients.shape[1]
    block_side = gradients.shape[3]
    slots_here = left_stats.shape[1]
    grad_local = gradients[0]
    owner_list = owners[0, :, 0]
    total_blocks = owner_list.shape[0]
    adam_dir = grad_local.astype(jnp.float32) / (jnp.sqrt(second_moment[0]) + ADAM_EPS)
    block_sq = jnp.sum(adam_dir * adam_dir, axis=(1, 2))
    global_sq = lax.psum(jnp.sum(block_sq), ("fsdp", "layer"))
    entry_count = float(total_blocks * lax.axis_size("layer") * block_side * block_side)
    clip_factor = jnp.minimum(1.0, UPDATE_RMS / jnp.sqrt(global_sq / entry_count))
    owner_hot, home_hot, slot_hot = selection_tables(
        owner_list, owner_count, blocks, slots_here, my_index
    )
    first_row = my_index * blocks
    my_owner_hot = lax.dynamic_slice_in_dim(owner_hot, first_row, blocks, 0).astype(jnp.bfloat16)
    outgoing = jnp.einsum(
        "jo,jxy->oxy", my_owner_hot, grad_local, preferred_element_type=jnp.float32
    ).astype(jnp.bfloat16)
    received = lax.all_to_all(outgoing, "fsdp", split_axis=0, concat_axis=0, tiled=True)
    pick_table = jnp.einsum("bs,bh->sh", slot_hot, home_hot).astype(jnp.bfloat16)
    gathered = jnp.einsum(
        "sh,hxy->sxy", pick_table, received, preferred_element_type=jnp.float32
    ).astype(jnp.bfloat16)
    preconditioned, new_left, new_right = owner_work(
        gathered, left_stats, right_stats, left_root, right_root
    )
    answers = jnp.einsum(
        "sh,sxy->hxy", pick_table, preconditioned, preferred_element_type=jnp.float32
    ).astype(jnp.bfloat16)
    returned = lax.all_to_all(answers, "fsdp", split_axis=0, concat_axis=0, tiled=True)
    home_blocks = jnp.einsum(
        "jo,oxy->jxy", my_owner_hot, returned, preferred_element_type=jnp.float32
    )
    pre_float = home_blocks.astype(jnp.bfloat16).astype(jnp.float32)
    graft_ratio = jnp.sqrt(block_sq / float(block_side * block_side)) / jnp.sqrt(
        jnp.sum(pre_float * pre_float, axis=(1, 2)) / float(block_side * block_side) + NORM_FLOOR
    )
    update = (pre_float * (graft_ratio * clip_factor)[:, None, None]).astype(jnp.bfloat16)
    return (update[None], new_left, new_right)


TAIL = 16


def kernel_params(mebibytes):
    return pltpu.CompilerParams(vmem_limit_bytes=mebibytes * 2**20)


def home_slot(named, target):
    block = jnp.int32(0)
    for j in range(1, len(named)):
        block = jnp.where(named[j] == target, jnp.int32(j), block)
    return block


def route_kernel(order, owners_hbm, me_ref, grad_hbm, *refs):
    outs, (owners_ref, held, owner_sem, grad_sem) = refs[:-4], refs[-4:]
    count = held.shape[0]
    me = me_ref[0]
    fetch_owners = pltpu.make_async_copy(owners_hbm, owners_ref, owner_sem)
    fetch_grads = pltpu.make_async_copy(grad_hbm.at[0], held, grad_sem)
    fetch_owners.start()
    fetch_grads.start()
    fetch_owners.wait()
    named = [owners_ref[me * count + j] for j in range(count)]
    blocks = [home_slot(named, me ^ m) for m in order]
    fetch_grads.wait()
    for block, out in zip(blocks, outs):
        out[...] = held[block]


def route(order, owner_list, me, gradients):
    count, side = gradients.shape[1], gradients.shape[3]
    hbm = pl.BlockSpec(memory_space=pltpu.HBM)
    piece = jax.ShapeDtypeStruct((side, side), gradients.dtype)
    return pl.pallas_call(
        functools.partial(route_kernel, order),
        in_specs=[hbm, pl.BlockSpec(memory_space=pltpu.SMEM), hbm],
        out_specs=[pl.BlockSpec(memory_space=pltpu.VMEM)] * count,
        scratch_shapes=[
            pltpu.SMEM(owner_list.shape, jnp.int32),
            pltpu.VMEM((count, side, side), gradients.dtype),
            pltpu.SemaphoreType.DMA,
            pltpu.SemaphoreType.DMA,
        ],
        out_shape=[piece] * count,
        compiler_params=kernel_params(6),
        cost_estimate=pl.CostEstimate(
            flops=0, bytes_accessed=4 * count * side * side, transcendentals=0
        ),
    )(
        pltpu.with_memory_space_constraint(owner_list, pltpu.HBM),
        me,
        pltpu.with_memory_space_constraint(gradients, pltpu.HBM),
    )


def adam_kernel(grad_hbm, moment_hbm, out_ref, total_ref, grads, moments, sems):
    count, side = grads.shape[0], grads.shape[2]
    lanes = out_ref.shape[1]
    copies = []
    for b in range(count):
        pair = (
            pltpu.make_async_copy(grad_hbm.at[0, b], grads.at[b], sems.at[0, b]),
            pltpu.make_async_copy(moment_hbm.at[0, b], moments.at[b], sems.at[1, b]),
        )
        for copy in pair:
            copy.start()
        copies.append(pair)
    total = jnp.zeros((1, lanes), jnp.float32)
    for b, pair in enumerate(copies):
        for copy in pair:
            copy.wait()
        adam_dir = grads[b].astype(jnp.float32) / (jnp.sqrt(moments[b]) + ADAM_EPS)
        squares = jnp.sum(adam_dir * adam_dir, axis=0, keepdims=True)
        row = squares[:, 0:lanes]
        for k in range(lanes, side, lanes):
            row = row + squares[:, k : k + lanes]
        out_ref[b : b + 1, :] = row
        total = total + row
    total_ref[...] = jnp.broadcast_to(total, total_ref.shape)


def adam_squares(gradients, second_moment):
    count, side = gradients.shape[1], gradients.shape[3]
    hbm = pl.BlockSpec(memory_space=pltpu.HBM)
    return pl.pallas_call(
        adam_kernel,
        in_specs=[hbm, hbm],
        out_specs=[pl.BlockSpec(memory_space=pltpu.VMEM)] * 2,
        out_shape=[
            jax.ShapeDtypeStruct((count, 128), jnp.float32),
            jax.ShapeDtypeStruct((8, 128), jnp.float32),
        ],
        scratch_shapes=[
            pltpu.VMEM((count, side, side), gradients.dtype),
            pltpu.VMEM((count, side, side), second_moment.dtype),
            pltpu.SemaphoreType.DMA((2, count)),
        ],
        compiler_params=kernel_params(8),
        cost_estimate=pl.CostEstimate(
            flops=8 * count * side * side,
            bytes_accessed=6 * count * side * side,
            transcendentals=2 * count * side * side,
        ),
    )(
        pltpu.with_memory_space_constraint(gradients, pltpu.HBM),
        pltpu.with_memory_space_constraint(second_moment, pltpu.HBM),
    )


def split_terms(value):
    high = value.astype(jnp.bfloat16).astype(jnp.float32)
    rest = value - high
    middle = rest.astype(jnp.bfloat16).astype(jnp.float32)
    return high, middle, rest - middle


def with_rows(rest, first, terms):
    row = lax.broadcasted_iota(jnp.int32, rest.shape, 0)
    for k, term in enumerate(terms):
        rest = jnp.where(row == first + k, term, rest)
    return rest


def tail_kernel(total_ref, out_ref):
    total = jnp.sum(total_ref[0:1, :], keepdims=True)
    rows = with_rows(jnp.zeros(out_ref.shape, jnp.float32), 0, split_terms(total))
    out_ref[...] = rows.astype(jnp.bfloat16)


def sum_tail(total, side):
    return pl.pallas_call(
        tail_kernel,
        in_specs=[pl.BlockSpec(memory_space=pltpu.VMEM)],
        out_specs=pl.BlockSpec(memory_space=pltpu.VMEM),
        out_shape=jax.ShapeDtypeStruct((TAIL, side), jnp.bfloat16),
        compiler_params=kernel_params(2),
        cost_estimate=pl.CostEstimate(flops=4096, bytes_accessed=32768, transcendentals=0),
    )(total)


def precondition_kernel(m, me_ref, grad_ref, left_ref, right_ref, tail_ref, out_ref):
    side = grad_ref.shape[0]
    slot = me_ref[0] ^ m
    half_done = jnp.dot(
        left_ref[0, slot], grad_ref[...], preferred_element_type=jnp.float32
    ).astype(jnp.bfloat16)
    preconditioned = jnp.dot(
        half_done, right_ref[0, slot], preferred_element_type=jnp.float32
    ).astype(jnp.bfloat16)
    out_ref[0:side, :] = preconditioned
    pre_float = preconditioned.astype(jnp.float32)
    squares = jnp.sum(pre_float * pre_float, axis=0, keepdims=True)
    rows = with_rows(tail_ref[...].astype(jnp.float32), 3, split_terms(squares))
    out_ref[side:, :] = rows.astype(jnp.bfloat16)


def precondition(m, me, block, left_root, right_root, tail):
    side = block.shape[0]
    return pl.pallas_call(
        functools.partial(precondition_kernel, m),
        grid_spec=pltpu.PrefetchScalarGridSpec(
            num_scalar_prefetch=1,
            grid=(),
            in_specs=[pl.BlockSpec(memory_space=pltpu.VMEM)] * 4,
            out_specs=pl.BlockSpec(memory_space=pltpu.VMEM),
        ),
        out_shape=jax.ShapeDtypeStruct((side + TAIL, side), jnp.bfloat16),
        compiler_params=kernel_params(6),
        cost_estimate=pl.CostEstimate(
            flops=4 * side**3, bytes_accessed=8 * side * side, transcendentals=0
        ),
    )(me, block, left_root, right_root, tail)


def gram_kernel(order, me_ref, *refs):
    count = len(refs) - 4
    grads = refs[:count]
    left_ref, right_ref, new_left_ref, new_right_ref = refs[count:]
    step = pl.program_id(0)
    for k, m in enumerate(order):

        @pl.when(step == m)
        def _():
            block = grads[k][...]
            gram_left = lax.dot_general(
                block, block, (((1,), (1,)), ((), ())), preferred_element_type=jnp.float32
            )
            gram_right = lax.dot_general(
                block, block, (((0,), (0,)), ((), ())), preferred_element_type=jnp.float32
            )
            new_left_ref[0, 0] = DECAY_RATE * left_ref[0, 0] + (1.0 - DECAY_RATE) * gram_left
            new_right_ref[0, 0] = DECAY_RATE * right_ref[0, 0] + (1.0 - DECAY_RATE) * gram_right


def gram_update(order, me, blocks, left_stats, right_stats):
    count, side = len(blocks), blocks[0].shape[0]
    stat = pl.BlockSpec((1, 1, side, side), lambda i, me_ref: (0, me_ref[0] ^ i, 0, 0))
    whole = pl.BlockSpec(memory_space=pltpu.VMEM)
    return pl.pallas_call(
        functools.partial(gram_kernel, order),
        grid_spec=pltpu.PrefetchScalarGridSpec(
            num_scalar_prefetch=1,
            grid=(count,),
            in_specs=[whole] * count + [stat, stat],
            out_specs=[stat, stat],
        ),
        out_shape=[
            jax.ShapeDtypeStruct(left_stats.shape, left_stats.dtype),
            jax.ShapeDtypeStruct(right_stats.shape, right_stats.dtype),
        ],
        compiler_params=kernel_params(12),
        cost_estimate=pl.CostEstimate(
            flops=4 * count * side**3, bytes_accessed=18 * count * side * side, transcendentals=0
        ),
    )(me, *blocks, left_stats, right_stats)


def finish_kernel(order, entries, owners_ref, me_ref, *refs):
    count = len(order)
    pieces = refs[:count]
    squares_ref, out_ref, held, sums, sems = refs[count:]
    side, lanes = out_ref.shape[3], squares_ref.shape[1]
    me = me_ref[0]
    named = [owners_ref[me * count + j] for j in range(count)]
    blocks = [home_slot(named, me ^ m) for m in order]
    global_sq = jnp.zeros((1, 1), jnp.float32)
    for k, piece in enumerate(pieces):
        rows = piece[side:, :].astype(jnp.float32)
        global_sq = global_sq + jnp.sum(rows[0:3, 0:1], axis=0, keepdims=True)
        row = jnp.sum(rows[3:6, :], axis=0, keepdims=True)
        parts = [row[:, i : i + lanes] for i in range(0, side, lanes)]
        sums[0, k : k + 1, :] = functools.reduce(jnp.add, parts)
        sums[1, k : k + 1, :] = squares_ref[pl.ds(blocks[k], 1), :]
    area = float(side * side)
    pre_sq = jnp.sum(sums[0], axis=1, keepdims=True)
    block_sq = jnp.sum(sums[1], axis=1, keepdims=True)
    clip_factor = jnp.minimum(1.0, UPDATE_RMS / jnp.sqrt(global_sq / entries))
    graft_ratio = jnp.sqrt(block_sq / area) / jnp.sqrt(pre_sq / area + NORM_FLOOR)
    scale = graft_ratio * clip_factor
    copies = []
    for k, piece in enumerate(pieces):
        pre_float = piece[0:side, :].astype(jnp.float32)
        held[k] = (pre_float * scale[k : k + 1, :]).astype(jnp.bfloat16)
        copy = pltpu.make_async_copy(held.at[k], out_ref.at[0, blocks[k]], sems.at[k])
        copy.start()
        copies.append(copy)
    for copy in copies:
        copy.wait()


def finish(order, owner_list, me, pieces, squares, entries):
    count, side = len(pieces), pieces[0].shape[1]
    return pl.pallas_call(
        functools.partial(finish_kernel, order, entries),
        grid_spec=pltpu.PrefetchScalarGridSpec(
            num_scalar_prefetch=2,
            grid=(),
            in_specs=[pl.BlockSpec(memory_space=pltpu.VMEM)] * (count + 1),
            out_specs=pl.BlockSpec(memory_space=pl.ANY),
            scratch_shapes=[
                pltpu.VMEM((count, side, side), jnp.bfloat16),
                pltpu.VMEM((2, count, squares.shape[1]), jnp.float32),
                pltpu.SemaphoreType.DMA((count,)),
            ],
        ),
        out_shape=jax.ShapeDtypeStruct((1, count, side, side), jnp.bfloat16),
        compiler_params=kernel_params(8),
        cost_estimate=pl.CostEstimate(
            flops=6 * count * side * side, bytes_accessed=4 * count * side * side, transcendentals=0
        ),
    )(owner_list, me, *pieces, squares)


def doublings(size):
    return [2**k for k in range(size.bit_length() - 1)]


def per_device_exchange(
    gradients, second_moment, owners, left_stats, right_stats, left_root, right_root
):
    count = lax.axis_size("fsdp")
    layers = lax.axis_size("layer")
    side = gradients.shape[3]
    me = lax.axis_index("fsdp").astype(jnp.int32).reshape(1)
    owner_list = owners[0, :, 0]
    half = count // 2
    order = [*range(half - 1), half + 1, half - 1, half, *range(half + 2, count - 2)]
    order += [count - 1, count - 2]

    def swap(value, m, axis="fsdp"):
        if m == 0:
            return value
        return lax.ppermute(value, axis, [(i, i ^ m) for i in range(lax.axis_size(axis))])

    outgoing = route(order, owner_list, me, gradients)
    received = [swap(block, m) for m, block in zip(order, outgoing)]
    squares, total = adam_squares(gradients, second_moment)
    for k in doublings(layers):
        total = total + swap(total, k, "layer")
    tail = sum_tail(total, side)
    returned = []
    for m, block in zip(order, received):
        done = precondition(m, me, block, left_root, right_root, tail)
        returned.append(swap(done, m))
    new_left, new_right = gram_update(order, me, received, left_stats, right_stats)
    entries = float(owner_list.shape[0] * layers * side * side)
    update = finish(order, owner_list, me, returned, squares, entries)
    return (update, new_left, new_right)


def per_device(gradients, second_moment, owners, left_stats, right_stats, left_root, right_root):
    owner_count, blocks, slots = lax.axis_size("fsdp"), gradients.shape[1], left_stats.shape[1]
    layers = lax.axis_size("layer")
    paired = owner_count == blocks == slots
    paired = paired and owner_count & (owner_count - 1) == 0 and layers & (layers - 1) == 0
    body = per_device_exchange if paired else per_device_general
    return body(
        gradients, second_moment, owners, left_stats, right_stats, left_root, right_root
    )


def solution(mesh):
    return jax.shard_map(
        per_device,
        mesh=mesh,
        in_specs=(
            P("layer", "fsdp", None, None),
            P("layer", "fsdp", None, None),
            P("layer", None, None),
            P("layer", "fsdp", None, None),
            P("layer", "fsdp", None, None),
            P("layer", "fsdp", None, None),
            P("layer", "fsdp", None, None),
        ),
        out_specs=(
            P("layer", "fsdp", None, None),
            P("layer", "fsdp", None, None),
            P("layer", "fsdp", None, None),
        ),
        check_vma=False,
    )
```
